32 devices in a mesh: tile: 8 (over z, y), spec: 4 (over x, core).
Axes of the slice: x: 2, y: 2, z: 4, core: 2. Of those that a mesh axis runs over, the one named last changes fastest.
Arguments:
- grad_columns: bfloat16 [8192, 512], P('tile', 'spec'), may hold values from -6 to 6
- grad_flux: float32 [16, 8192], P('spec', 'tile'), may hold values from -6 to 6
- remap_part: int32 [8192, 4], P('tile'), may hold values from 0 to 7, all different within a row; in each aligned block of 1024 rows (0 to 1023, 1024 to 2047, ...) at most 1024 rows name the same one
- remap_slot: int32 [8192, 4], P('tile'), may hold values from 0 to 1023
- remap_weight: float32 [8192, 4], P('tile'), may hold values from 0.2 to 1
- col_count: int32 [8], P('tile'), may hold values from 341 to 1024, as said below
- neighbors: int32 [8192, 4], P('tile'), may hold values from 0 to 1279, as said below
- kappa: float32 [16], P('spec'), may hold values from 0.03 to 0.2
- thickness: float32 [16, 32], P('spec'), may hold values from 0.2 to 2
- vertical: bfloat16 [16, 32, 32], P('spec'), may hold values from -1 to 1
- reaction: bfloat16 [16, 16], P(None, 'spec'), may hold values from -1.5 to 1.5
Outputs:
- grad_state: bfloat16 [8192, 512], P('tile', 'spec')
- grad_bottom: float32 [16, 8192], P('spec', 'tile')
The draws below stay inside these ranges and needn't reach their ends.
Inputs may be any that keep to these rules, and one draw needn't show every extreme that they name: `remap_part`: each coarse cell names 4 different partitions; the entries of the cells of one tile (1024 cells) name one partition at most 1024 times. `col_count`: live counts of partitions differ up to threefold; one partition holds 1024 live columns and one holds 341. `neighbors`: row p * 1024 + i lists the codes of 4 neighbours of slot i of partition p; every named slot is live; the first partition names no previous and the last no next partition.
All inputs are finite; a program needn't handle non-finite values.
Results may differ from the reference program's by a relative error of at most 0.008.
Values may be sent and summed in bfloat16 or wider, within the bound.
No kernel may reach another device: no remote copies, remote signals or barrier semaphores. Data moves between devices by JAX's collectives and lax.ppermute only.
A program may use at most 128 MiB of HBM per device.

```python
import math
import jax
import jax.numpy as jnp
import numpy as np
from jax import lax

S = 16
L = 32
CMAX = 1024
CC = 1024
RB = 4
NB = 4
SUB = 4
HW = 128
PARTS_SIZE = 8
NF = 8192
NC = 8192
CAP = 1024
N_TILE = 8


def count_helper(key):
    sub_key = jax.random.fold_in(key, 11)
    key_base, key_first, key_second = jax.random.split(sub_key, 3)
    counts = jax.random.randint(key_base, (PARTS_SIZE,), CMAX // 3, CMAX + 1)
    first_index = jax.random.randint(key_first, (), 0, PARTS_SIZE)
    second_index = (first_index + 1 + jax.random.randint(key_second, (), 0, PARTS_SIZE - 1)) % PARTS_SIZE
    counts = counts.at[first_index].set(CMAX).at[second_index].set(CMAX // 3)
    return counts.astype(jnp.int32)


def draw_col_count(key, part):
    return count_helper(key)


def draw_neighbors(key, part):
    counts = count_helper(key)
    offset_key = jax.random.fold_in(key, 23)
    offsets = jax.random.randint(offset_key, (PARTS_SIZE, CMAX, NB), -8, 9)
    slot_ids = jnp.arange(CMAX, dtype=jnp.int32)
    part_ids = jnp.arange(PARTS_SIZE, dtype=jnp.int32)
    own_codes = jnp.clip(slot_ids[None, :, None] + offsets, 0, counts[:, None, None] - 1)
    cross_prev = (slot_ids[None, :] < HW) & (part_ids[:, None] > 0)
    cross_next = (slot_ids[None, :] >= HW) & (slot_ids[None, :] < 2 * HW) & (part_ids[:, None] < PARTS_SIZE - 1)
    first_code = jnp.where(cross_prev | cross_next, CMAX + slot_ids[None, :], own_codes[:, :, 0])
    codes = own_codes.at[:, :, 0].set(first_code)
    return codes.reshape(PARTS_SIZE * CMAX, NB).astype(jnp.int32)


def set_ends(result, stream_key, least, top_value):
    spot = [jax.random.randint(jax.random.fold_in(stream_key, axis), (), 0, length) for axis, length in enumerate(result.shape)]
    widest = result.shape.index(max(result.shape))
    next_to = spot[:widest] + [(spot[widest] + 1) % result.shape[widest]] + spot[widest + 1:]
    return result.at[tuple(spot)].set(least).at[tuple(next_to)].set(top_value)


def block_levels(stream_key, dims, cuts, least, largest):
    def one(dim, parts):
        draws = jax.random.uniform(jax.random.fold_in(jax.random.fold_in(stream_key, 6), dim), (parts,), jnp.float32, least / len(cuts), largest / len(cuts))
        return jnp.repeat(jnp.exp(draws), dims[dim] // parts).reshape((-1,) + (1,) * (len(dims) - dim - 1))

    factor_of = one(*cuts[0])
    for cut in cuts[1:]:
        factor_of = factor_of * one(*cut)
    return factor_of


def shared_out(rng, own, number, rows, count, top, limit, slope):
    sequence = jax.random.permutation(rng, count)
    heavy_load, usual = load_shares(count, rows * top, limit, slope, True), load_shares(count, rows * top, limit, slope, False)
    places = jnp.arange(count)

    def named(tallies, offset_by):
        used = int((tallies > 0).sum())
        fixed = max(1, used // 4)
        moved = fixed + (places - fixed + offset_by * (used - fixed)) % max(1, count - fixed)
        return jnp.zeros((count,), jnp.int32).at[sequence[jnp.where(places < fixed, places, moved)]].set(jnp.asarray(tallies, jnp.int32))

    tallies = jnp.where(number % 4 == 0, named(heavy_load, number // 4), named(usual, number - number // 4 - 1))
    mixed = jax.random.permutation(jax.random.fold_in(own, 3), count)
    source_of, receiver = mixed[0:count // 2 * 2:2], mixed[1:count // 2 * 2:2]
    slack = jnp.minimum(tallies[source_of] - 1, limit - tallies[receiver]) // 2
    slack = jnp.where((source_of == sequence[0]) | (receiver == sequence[0]) | (tallies[receiver] == 0), 0, jnp.maximum(slack, 0))
    moved = jax.random.randint(jax.random.fold_in(own, 4), (count // 2,), 0, 1 << 20) % (slack + 1)
    tallies = tallies.at[source_of].add(-moved).at[receiver].add(moved)
    labels = jnp.searchsorted(jnp.cumsum(tallies), jnp.arange(rows * top), side="right").astype(jnp.int32)
    table = labels.reshape(top, rows).T
    table = table[jax.random.permutation(jax.random.fold_in(own, 1), rows)]
    offset_by = jax.random.randint(jax.random.fold_in(own, 2), (rows, 1), 0, top)
    return jnp.take_along_axis(table, (jnp.arange(top)[None, :] + offset_by) % top, axis=1)


def load_shares(count, total, most, slope, full):
    loads = [(1 << 20) // math.isqrt(rank ** slope) + 1 for rank in range(1, count + 1)]
    largest = most if full else min(most, max(-(-total // count), total * loads[0] // sum(loads)))
    least = 1 if total - largest >= count - 1 else 0
    holding, spare = [largest] + [least] * (count - 1), total - largest - least * (count - 1)
    while spare > 0:
        candidates = [i for i in range(1, count) if holding[i] < largest] or [i for i in range(1, count) if holding[i] < most]
        mass, budget = sum([loads[i] for i in candidates]), spare
        for i in candidates:
            extra = min(most - holding[i], max(1, budget * loads[i] // mass), spare)
            holding[i] = holding[i] + extra
            spare = spare - extra
    return np.array(holding)


def scatter_about(key, dims, deviation, most, cuts=(), held_as=jnp.bfloat16):
    values = deviation * jax.random.normal(key, dims, jnp.float32)
    if cuts:
        values = values * block_levels(key, dims, cuts, -0.22, 0.18)
    return jnp.clip(values, -most, most).astype(held_as)


def setup_inputs(seed: int = 0) -> dict:
    splits = jax.random.split(jax.random.key(seed), 12)
    grad_columns = scatter_about(splits[0], (NF, S * L), 1.0, 6.0, ((0, 8), (1, 4)))
    grad_flux = scatter_about(splits[1], (S, NC), 1.0, 6.0, ((0, 4), (1, 8)), jnp.float32)
    remap_part_keys = jax.random.split(jax.random.fold_in(splits[2], 1), NC // CC)
    remap_part_turns = jax.random.permutation(jax.random.fold_in(splits[2], 3), NC // CC)
    remap_part = jax.vmap(lambda own, number: shared_out(jax.random.fold_in(splits[2], 2), own, number, CC, N_TILE, RB, CAP, 2))(remap_part_keys, remap_part_turns).reshape((NC, RB))
    remap_slot = set_ends(jax.random.randint(splits[3], (NC, RB), 0, CMAX), jax.random.fold_in(splits[3], 1), 0, CMAX - 1).astype(jnp.int32)
    remap_weight = jnp.clip(0.2 + 0.8 * jax.random.uniform(splits[4], (NC, RB), jnp.float32) ** block_levels(splits[4], (NC, RB), ((0, 8),), -0.2, 0.2), 0.2, 1.0)
    col_count = draw_col_count(jax.random.fold_in(splits[11], 71), 0)
    neighbors = draw_neighbors(jax.random.fold_in(splits[11], 71), 0)
    kappa = jnp.clip(jnp.exp(math.log(0.2) - 1.89712 * jax.random.uniform(splits[7], (S,), jnp.float32) ** block_levels(splits[7], (S,), ((0, 4),), -0.2, 0.2)), 0.03, 0.2)
    thickness = jnp.clip(jnp.exp(math.log(2.0) - 2.3025851 * jax.random.uniform(splits[8], (S, L), jnp.float32) ** block_levels(splits[8], (S, L), ((0, 4),), -0.2, 0.2)), 0.2, 2.0)
    vertical = scatter_about(splits[9], (S, L, L), L ** -0.5, 1.0, ((0, 4),))
    reaction = scatter_about(splits[10], (S, S), S ** -0.5, 1.5, ((1, 4),))
    return dict(grad_columns=grad_columns, grad_flux=grad_flux, remap_part=remap_part, remap_slot=remap_slot, remap_weight=remap_weight, col_count=col_count, neighbors=neighbors, kappa=kappa, thickness=thickness, vertical=vertical, reaction=reaction)


def neighbour_targets(neighbors):
    rows = jnp.arange(NF, dtype=jnp.int32)
    part_of = rows // CMAX
    codes = neighbors.astype(jnp.int32)
    excess = codes - CMAX
    own_target = part_of[:, None] * CMAX + codes
    prev_target = (part_of[:, None] - 1) * CMAX + HW + excess
    next_target = (part_of[:, None] + 1) * CMAX + excess - HW
    cross = jnp.where(excess < HW, prev_target, next_target)
    return jnp.where(codes < CMAX, own_target, cross).astype(jnp.int32)


def reference(grad_columns, grad_flux, remap_part, remap_slot, remap_weight, col_count, neighbors, kappa, thickness, vertical, reaction):
    live_mask = (jnp.arange(CMAX)[None, :] < col_count[:, None]).astype(jnp.float32).reshape(NF)
    target = (remap_part * CMAX + remap_slot).reshape(-1).astype(jnp.int32)
    entry_values = (remap_weight[None, :, :] * grad_flux[:, :, None]).reshape(S, NC * RB)
    injected = jnp.zeros((S, NF), jnp.float32).at[:, target].add(entry_values)
    adjoint = live_mask[:, None, None] * (grad_columns.astype(jnp.float32).reshape(NF, S, L) + thickness[None, :, :] * injected.T[:, :, None])
    slots_to = neighbour_targets(neighbors)
    rate = kappa[None, :, None]
    vertical_wide = vertical.astype(jnp.float32)
    for substep in range(SUB):
        spread = rate * adjoint
        bedload = adjoint - NB * rate * adjoint
        for column in range(NB):
            bedload = bedload + jax.ops.segment_sum(spread, slots_to[:, column], num_segments=NF)
        rounded = lax.optimization_barrier(bedload.astype(jnp.bfloat16)).astype(jnp.float32)
        adjoint = jnp.einsum("jsl,slm->jsm", rounded, vertical_wide)
    rounded = lax.optimization_barrier(adjoint.astype(jnp.bfloat16)).astype(jnp.float32)
    mixed = jnp.einsum("jsl,st->jtl", rounded, reaction.astype(jnp.float32))
    grad_state = mixed.reshape(NF, S * L).astype(jnp.bfloat16)
    top_layer = mixed[:, :, 0]
    picked = top_layer[target].reshape(NC, RB, S)
    grad_bottom = jnp.sum(picked * remap_weight[:, :, None], axis=1).T
    return grad_state, grad_bottom
```

```python
import functools

import jax
import jax.numpy as jnp
from jax import lax
from jax.experimental import pallas as pl
from jax.experimental.pallas import tpu as pltpu
from jax.sharding import PartitionSpec as P

SUB = 4
LANES = 128
WIDE = 256
ROWS = 32
F32 = jnp.float32
BF16 = jnp.bfloat16
VMEM = pl.BlockSpec(memory_space=pltpu.VMEM)
SMEM = pl.BlockSpec(memory_space=pltpu.SMEM)
LIMIT = 48 * 1024 * 1024


def shifted(block, axis, distance):
    devices = range(lax.axis_size(axis))
    route = [(i - distance, i) for i in devices if i - distance in devices]
    return lax.ppermute(block, axis, route)


def call(kernel, outs, specs, scratch=(), flops=0, moved=0):
    return pl.pallas_call(
        kernel,
        out_shape=outs,
        in_specs=specs,
        out_specs=[VMEM] * len(outs),
        scratch_shapes=scratch,
        compiler_params=pltpu.CompilerParams(vmem_limit_bytes=LIMIT),
        cost_estimate=pl.CostEstimate(flops=flops, bytes_accessed=moved, transcendentals=0),
    )


def nt(a, b, precision=None):
    return lax.dot_general(
        a, b, (((1,), (1,)), ((), ())), precision=precision, preferred_element_type=F32
    )


def nn(a, b, precision=None):
    return lax.dot_general(
        a, b, (((1,), (0,)), ((), ())), precision=precision, preferred_element_type=F32
    )


def row_ids(rows, cols):
    return lax.broadcasted_iota(jnp.int32, (rows, cols), 0)


def chosen(key, rows):
    hit = row_ids(rows, key.shape[1]) == key
    return jnp.where(hit, 1.0, 0.0).astype(BF16)


def rate_column(kappa_ref, rows, group):
    ids = row_ids(rows, 1)
    out = jnp.zeros((rows, 1), F32)
    for s in range(kappa_ref.shape[0]):
        out = jnp.where((ids // group) % kappa_ref.shape[0] == s, kappa_ref[s], out)
    return out


def prepare(
    count_ref, gc_ref, vert_ref, thick_ref, flux_ref, part_ref, slot_ref, weight_ref, nbr_ref,
    payload_ref, w_ref, tv_ref,
):
    species, layers, _ = vert_ref.shape
    width = species * layers
    col_max = gc_ref.shape[0]
    v = vert_ref[...].astype(F32).reshape(width, layers)
    v = jnp.concatenate([v] * species, axis=1)
    rows = row_ids(width, width) // layers
    cols = lax.broadcasted_iota(jnp.int32, (width, width), 1) // layers
    vt = jnp.where(rows == cols, v, 0.0).T
    hi = lax.Precision.HIGHEST
    v2 = nn(vt, vt, hi)
    v4 = nn(v2, v2, hi)
    th = jnp.concatenate([thick_ref[s : s + 1, :] for s in range(species)], axis=1)
    tv_ref[...] = jnp.sum(v4 * th, axis=1, keepdims=True)
    live = lax.broadcasted_iota(jnp.int32, (1, col_max), 1) < count_ref[0]
    w = jnp.where(live, nt(v4.astype(BF16), gc_ref[...]), 0.0)
    w_ref[...] = w
    top = [w[s * layers : s * layers + 1, :] for s in range(species)]
    slot = slot_ref[...]
    nbr = nbr_ref[...]
    code = (nbr // LANES) * 4 + slot // WIDE
    pieces = top + [
        flux_ref[...],
        weight_ref[...],
        part_ref[...].astype(F32),
        (slot % WIDE).astype(F32),
        code.astype(F32),
        (nbr % LANES).astype(F32),
        jnp.where(live, 1.0, 0.0),
        jnp.zeros((ROWS - 7 * 4 - 1, col_max), F32),
    ]
    payload_ref[...] = jnp.concatenate(pieces, axis=0).astype(BF16)


def spread_out(x, kcol, counts):
    ext = nt((kcol * x).astype(BF16), counts)
    col_max = x.shape[1]
    return (
        (1.0 - 4.0 * kcol) * x + ext[:, :col_max],
        ext[:, col_max : col_max + LANES].astype(BF16),
        ext[:, col_max + LANES :].astype(BF16),
    )


def first_step(kappa_ref, nbr_ref, w_ref, counts_ref, x_ref, prev_ref, next_ref):
    width, col_max = w_ref.shape
    nbr = nbr_ref[...]
    high, low = nbr // LANES, nbr % LANES
    for h in range(counts_ref.shape[0] // LANES):
        block = jnp.zeros((LANES, col_max), F32)
        for n in range(nbr.shape[0]):
            key = jnp.where(high[n : n + 1] == h, low[n : n + 1], -1)
            block = block + jnp.where(row_ids(LANES, col_max) == key, 1.0, 0.0)
        counts_ref[h * LANES : (h + 1) * LANES, :] = block.astype(BF16)
    kcol = rate_column(kappa_ref, width, width // kappa_ref.shape[0])
    x_ref[...], prev_ref[...], next_ref[...] = spread_out(w_ref[...], kcol, counts_ref[...])


def joined(part, from_prev, from_next):
    return jnp.concatenate(
        [
            part[:, :LANES] + from_prev.astype(F32),
            part[:, LANES : 2 * LANES] + from_next.astype(F32),
            part[:, 2 * LANES :],
        ],
        axis=1,
    )


def next_step(kappa_ref, counts_ref, part_ref, from_prev, from_next, x_ref, prev_ref, next_ref):
    width = part_ref.shape[0]
    x = joined(part_ref[...], from_prev[...], from_next[...])
    kcol = rate_column(kappa_ref, width, width // kappa_ref.shape[0])
    x_ref[...], prev_ref[...], next_ref[...] = spread_out(x, kcol, counts_ref[...])


def chain(tiles, kappa_ref, tv_ref, data_ref, out_ref, x_ref, table_ref):
    col_max = data_ref.shape[1]
    species = kappa_ref.shape[0]
    layers = tv_ref.shape[0] // species
    subs = col_max // WIDE
    groups = tiles * subs // 2
    second = jnp.where(row_ids(8, 1) >= 4, 1, 0)

    table_ref[...] = jnp.zeros_like(table_ref)

    def gather(q, carry):
        block = data_ref[pl.ds(pl.multiple_of(q * ROWS, ROWS), ROWS), :].astype(F32)
        ints = block[12:28].astype(jnp.int32)
        part, low, code = ints[0:4], ints[4:8], ints[8:12]
        high = part * subs + (code & 3)
        total = jnp.zeros(table_ref.shape, F32)
        for r in range(4):
            value = block[4:8] * block[8 + r : 9 + r]
            value = jnp.concatenate([value, value], axis=0)
            key = high[r : r + 1] - second
            rows = [jnp.where(key == 2 * g, value, 0.0) for g in range(groups)]
            total = total + nt(
                jnp.concatenate(rows, axis=0).astype(BF16), chosen(low[r : r + 1], WIDE)
            )
        table_ref[...] += total
        return carry

    lax.fori_loop(0, tiles, gather, 0)

    tv0 = jnp.concatenate([tv_ref[s * layers : s * layers + 1, :] for s in range(4)], axis=0)
    for q in range(tiles):
        live = data_ref[q * ROWS + 28 : q * ROWS + 29, :].astype(F32)
        inj = [table_ref[(q * subs + h) * 4 : (q * subs + h) * 4 + 4, :] for h in range(subs)]
        inj = jnp.concatenate(inj, axis=1) * live
        top = data_ref[q * ROWS : q * ROWS + 4, :].astype(F32)
        x_ref[0, q] = jnp.concatenate([top + tv0 * inj, inj], axis=0)

    kcol = rate_column(kappa_ref, 8, 1)
    high_count = col_max // LANES + 2
    pairs = high_count // 2
    second16 = jnp.where(row_ids(16, 1) >= 8, 1, 0)
    for step in range(SUB):
        here, there = step % 2, (step + 1) % 2
        for q in range(tiles):
            x_ref[there, q] = (1.0 - 4.0 * kcol) * x_ref[here, q]

        def apply(q, carry):
            block = data_ref[pl.ds(pl.multiple_of(q * ROWS, ROWS), ROWS), :].astype(F32)
            ints = block[20:28].astype(jnp.int32)
            high, low = ints[0:4] // 4, ints[4:8]
            value = kcol * x_ref[here, q]
            value = jnp.concatenate([value, value], axis=0)
            total = jnp.zeros((high_count * 8, LANES), F32)
            for n in range(4):
                key = high[n : n + 1] - second16
                rows = [jnp.where(key == 2 * g, value, 0.0) for g in range(pairs)]
                total = total + nt(
                    jnp.concatenate(rows, axis=0).astype(BF16), chosen(low[n : n + 1], LANES)
                )
            own = [total[h * 8 : h * 8 + 8] for h in range(high_count - 2)]
            x_ref[there, q] += jnp.concatenate(own, axis=1)
            before, after = jnp.maximum(q - 1, 0), jnp.minimum(q + 1, tiles - 1)
            to_prev = jnp.where(q > 0, total[8 * (high_count - 2) : 8 * (high_count - 1)], 0.0)
            to_next = jnp.where(q < tiles - 1, total[8 * (high_count - 1) :], 0.0)
            x_ref[there, before, :, LANES : 2 * LANES] += to_prev
            x_ref[there, after, :, :LANES] += to_next
            return carry

        lax.fori_loop(0, tiles, apply, 0)
    out_ref[...] = x_ref[SUB % 2]


def finish(
    tiles, part_ref, from_prev, from_next, tv_ref, chain_ref, rpart_ref, slot_ref, weight_ref,
    out_ref, y_ref, u_ref,
):
    width, col_max = part_ref.shape
    species = 4
    layers = width // species
    me = lax.axis_index("tile")
    x = joined(part_ref[...], from_prev[...], from_next[...])
    inj = chain_ref[me][4:8]
    inj = jnp.concatenate(
        [jnp.broadcast_to(inj[s : s + 1], (layers, col_max)) for s in range(species)], axis=0
    )
    out_ref[:width, :] = (x + tv_ref[...] * inj).astype(BF16)
    subs = col_max // WIDE
    half = tiles * subs // 2
    for i in range(half):
        first, other = i, i + half
        a = chain_ref[first // subs, 0:4, (first % subs) * WIDE : (first % subs + 1) * WIDE]
        b = chain_ref[other // subs, 0:4, (other % subs) * WIDE : (other % subs + 1) * WIDE]
        y_ref[i * 8 : i * 8 + 8, :] = jnp.concatenate([a, b], axis=0)
    y = y_ref[...].astype(BF16)
    slot = slot_ref[...]
    high = rpart_ref[...] * subs + slot // WIDE
    low = slot % WIDE
    offset = jnp.where(row_ids(8, 1) >= 4, half, 0)
    total = jnp.zeros((8, col_max), F32)
    for r in range(4):
        u_ref[...] = nn(y, chosen(low[r : r + 1], WIDE))
        key = high[r : r + 1] - offset
        found = jnp.zeros((8, col_max), F32)
        for i in range(half):
            found = jnp.where(key == i, u_ref[i * 8 : i * 8 + 8, :], found)
        total = total + found * weight_ref[r : r + 1, :]
    bottom = total[0:4] + total[4:8]
    out_ref[width:, :] = jnp.concatenate(
        [bottom, jnp.zeros((out_ref.shape[0] - width - 4, col_max), F32)], axis=0
    ).astype(BF16)


def combine(layers, reaction_ref, all_ref, state_ref, bottom_ref):
    parts, rows, col_max = all_ref.shape
    out_species, species = reaction_ref.shape
    own = species // parts
    wide = own * layers
    width = out_species * layers
    mix = reaction_ref[...].astype(BF16)
    left = jnp.where(
        row_ids(width, out_species) // layers
        == lax.broadcasted_iota(jnp.int32, (width, out_species), 1),
        1.0,
        0.0,
    ).astype(BF16)
    right = jnp.where(
        row_ids(species, species * layers)
        == lax.broadcasted_iota(jnp.int32, (species, species * layers), 1) // layers,
        1.0,
        0.0,
    ).astype(BF16)
    full = nn(nn(left, mix).astype(BF16), right)
    same = (
        row_ids(width, species * layers) % layers
        == lax.broadcasted_iota(jnp.int32, (width, species * layers), 1) % layers
    )
    full = jnp.where(same, full, 0.0).astype(BF16)
    mixed = jnp.zeros((width, col_max), F32)
    bottom = jnp.zeros((out_species, col_max), F32)
    mix = mix.astype(F32)
    for k in range(parts):
        mixed = mixed + nn(full[:, k * wide : (k + 1) * wide], all_ref[k, :wide, :])
        tail = all_ref[k, wide:, :].astype(F32)
        for s in range(own):
            col = k * own + s
            bottom = bottom + mix[:, col : col + 1] * tail[s : s + 1, :]
    state_ref[...] = mixed.T.astype(BF16)
    bottom_ref[...] = bottom


def body(
    grad_columns,
    grad_flux,
    remap_part,
    remap_slot,
    remap_weight,
    col_count,
    neighbors,
    kappa,
    thickness,
    vertical,
    reaction,
):
    tiles = lax.axis_size("tile")
    parts = lax.axis_size("spec")
    col_max, width = grad_columns.shape
    layers = thickness.shape[1]
    part_t, slot_t, weight_t, nbr_t = remap_part.T, remap_slot.T, remap_weight.T, neighbors.T
    shape = jax.ShapeDtypeStruct
    payload, w, tv = call(
        prepare,
        [shape((ROWS, col_max), BF16), shape((width, col_max), F32), shape((width, 1), F32)],
        [SMEM] + [VMEM] * 8,
        flops=4 * 10**7,
        moved=10**6,
    )(col_count, grad_columns, vertical, thickness, grad_flux, part_t, slot_t, weight_t, nbr_t)
    data = lax.all_gather(payload, "tile", axis=0, tiled=True)
    rim = shape((width, LANES), BF16)
    counts, x, to_prev, to_next = call(
        first_step,
        [shape((col_max + 2 * LANES, col_max), BF16), shape((width, col_max), F32), rim, rim],
        [SMEM] + [VMEM] * 2,
        flops=10**9,
        moved=4 * 10**6,
    )(kappa, nbr_t, w)
    for step in range(1, SUB):
        from_next = shifted(to_prev, "tile", -1)
        from_prev = shifted(to_next, "tile", 1)
        x, to_prev, to_next = call(
            next_step,
            [shape((width, col_max), F32), rim, rim],
            [SMEM] + [VMEM] * 4,
            flops=4 * 10**8,
            moved=4 * 10**6,
        )(kappa, counts, x, from_prev, from_next)
    from_next = shifted(to_prev, "tile", -1)
    from_prev = shifted(to_next, "tile", 1)
    state = call(
        functools.partial(chain, tiles),
        [shape((tiles, 8, col_max), F32)],
        [SMEM] + [VMEM] * 2,
        scratch=[
            pltpu.VMEM((2, tiles, 8, col_max), F32),
            pltpu.VMEM((tiles * col_max // WIDE * 4, WIDE), F32),
        ],
        flops=10**10,
        moved=10**6,
    )(kappa, tv, data)[0]
    tail = 16
    mine = call(
        functools.partial(finish, tiles),
        [shape((width + tail, col_max), BF16)],
        [VMEM] * 8,
        scratch=[
            pltpu.VMEM((tiles * col_max // WIDE * 4, WIDE), F32),
            pltpu.VMEM((tiles * col_max // WIDE * 4, col_max), F32),
        ],
        flops=10**9,
        moved=10**6,
    )(x, from_prev, from_next, tv, state, part_t, slot_t, weight_t)[0]
    every = lax.all_gather(mine, "spec", axis=0, tiled=False)
    grad_state, grad_bottom = call(
        functools.partial(combine, layers),
        [shape((col_max, width), BF16), shape((reaction.shape[1], col_max), F32)],
        [VMEM] * 2,
        flops=2 * 10**8,
        moved=2 * 10**6,
    )(reaction.T, every)
    return grad_state, grad_bottom


def solution(mesh):
    placed = (
        P("tile", "spec"),
        P("spec", "tile"),
        P("tile", None),
        P("tile", None),
        P("tile", None),
        P("tile"),
        P("tile", None),
        P("spec"),
        P("spec", None),
        P("spec", None, None),
        P(None, "spec"),
    )
    return jax.shard_map(
        body,
        mesh=mesh,
        in_specs=placed,
        out_specs=(P("tile", "spec"), P("spec", "tile")),
        check_vma=False,
    )
```

```python
import functools

import jax
import jax.numpy as jnp
from jax import lax
from jax.experimental import pallas as pl
from jax.experimental.pallas import tpu as pltpu
from jax.sharding import PartitionSpec as P

SUB = 4
LANES = 128
WIDE = 256
OWN = 16
DEAD = 7
F32 = jnp.float32
BF16 = jnp.bfloat16
VMEM = pl.BlockSpec(memory_space=pltpu.VMEM)
ANY = pl.BlockSpec(memory_space=pl.ANY)
SMEM = pl.BlockSpec(memory_space=pltpu.SMEM)
LIMIT = 48 * 1024 * 1024


def call(kernel, outs, specs, scratch=(), flops=0, moved=0):
    return pl.pallas_call(
        kernel,
        out_shape=outs,
        in_specs=specs,
        out_specs=[VMEM] * len(outs),
        scratch_shapes=scratch,
        compiler_params=pltpu.CompilerParams(vmem_limit_bytes=LIMIT),
        cost_estimate=pl.CostEstimate(flops=flops, bytes_accessed=moved, transcendentals=0),
    )


def nt(a, b, precision=None):
    return lax.dot_general(
        a, b, (((1,), (1,)), ((), ())), precision=precision, preferred_element_type=F32
    )


def nn(a, b, precision=None):
    return lax.dot_general(
        a, b, (((1,), (0,)), ((), ())), precision=precision, preferred_element_type=F32
    )


def row_ids(rows, cols):
    return lax.broadcasted_iota(jnp.int32, (rows, cols), 0)


def fetch(pairs, sems):
    copies = [pltpu.make_async_copy(a, b, sems.at[i]) for i, (a, b) in enumerate(pairs)]
    for copy in copies:
        copy.start()
    for copy in copies:
        copy.wait()


def prepare(
    count_ref, gc_any, vert_any, thick_any, flux_any, part_any, slot_any, weight_any, nbr_any,
    payload_ref, tv_ref,
    gc_ref, vert_ref, thick_ref, flux_ref, part_ref, slot_ref, weight_ref, nbr_ref, sems,
):
    fetch(
        [
            (gc_any, gc_ref),
            (vert_any, vert_ref),
            (thick_any, thick_ref),
            (flux_any, flux_ref),
            (part_any, part_ref),
            (slot_any, slot_ref),
            (weight_any, weight_ref),
            (nbr_any, nbr_ref),
        ],
        sems,
    )
    tiles, block_rows, col_max = payload_ref.shape
    species, layers, _ = vert_ref.shape
    width = species * layers
    v = vert_ref[...].astype(F32).reshape(width, layers)
    v = jnp.concatenate([v] * species, axis=1)
    rows = row_ids(width, width) // layers
    cols = lax.broadcasted_iota(jnp.int32, (width, width), 1) // layers
    vt = jnp.where(rows == cols, v, 0.0).T
    hi = lax.Precision.HIGHEST
    v2 = nn(vt, vt, hi)
    v4 = nn(v2, v2, hi)
    th = jnp.concatenate([thick_ref[s : s + 1, :] for s in range(species)], axis=1)
    tv_ref[...] = nt(jnp.broadcast_to(th, (8, width)), v4, hi)
    live = lax.broadcasted_iota(jnp.int32, (1, col_max), 1) < count_ref[0]
    w = jnp.where(live, nt(v4.astype(BF16), gc_ref[...]), 0.0)
    top = [w[s * layers : s * layers + 1, :] for s in range(species)]
    slot, nbr = slot_ref[...], nbr_ref[...]
    power = (slot // WIDE) * 8 + jnp.where(live, nbr // WIDE, DEAD)
    code = 128.0 + part_ref[...].astype(F32)
    for bit in range(5):
        code = code * jnp.where((power >> bit) & 1 == 1, float(2 ** (2**bit)), 1.0)
    common = top + [
        flux_ref[...],
        weight_ref[...],
        (slot % WIDE).astype(F32),
        (nbr % WIDE).astype(F32),
        code,
    ]
    own = width // tiles
    pad = [] if own == OWN else [jnp.zeros((OWN - own, col_max), F32)]
    common = jnp.concatenate(common, axis=0).astype(BF16)
    for q in range(tiles):
        mine = jnp.concatenate([w[q * own : (q + 1) * own]] + pad, axis=0).astype(BF16)
        payload_ref[q] = jnp.concatenate([mine, common], axis=0)


def decoded(code):
    power = jnp.zeros(code.shape, jnp.int32)
    for bit in (16, 8, 4, 2, 1):
        large = code >= 128.0 * 2.0**bit
        code = jnp.where(large, code * 2.0**-bit, code)
        power = power + jnp.where(large, bit, 0)
    return code - 128.0, power


def hot(key, ids):
    return jnp.where(ids == key, jnp.ones((), BF16), jnp.zeros((), BF16))


def picked(keys, value, target):
    return jnp.where(keys == jnp.asarray(target, BF16), value, jnp.zeros((), BF16))


def chain(
    tiles, own, layers, keep, kappa_ref, tv_ref, data_ref, back_ref, y_ref, x_ref, table_ref, hot_ref
):
    col_max = data_ref.shape[2]
    subs = col_max // WIDE
    me = lax.axis_index("tile")
    ids = row_ids(WIDE, 1).astype(F32).astype(BF16)
    quarter = row_ids(16, 1) // 4

    table_ref[...] = jnp.zeros_like(table_ref)

    def gather(q, carry):
        block = data_ref[q].astype(F32)
        part, power = decoded(block[OWN + 20 : OWN + 24])
        sub = power >> 3
        for r in range(4):
            value = block[OWN + 4 : OWN + 8] * block[OWN + 8 + r : OWN + 9 + r]
            value = jnp.concatenate([value] * 4, axis=0).astype(BF16)
            key = jnp.where(sub[r : r + 1] == quarter, part[r : r + 1], -1.0).astype(BF16)
            rows = jnp.concatenate([picked(key, value, g) for g in range(tiles)], axis=0)
            low = block[OWN + 12 + r : OWN + 13 + r].astype(BF16)
            table_ref[...] += nt(rows, hot(low, ids))
        return carry

    lax.fori_loop(0, tiles, gather, 0)

    lane = lax.broadcasted_iota(jnp.int32, (OWN, tv_ref.shape[1]), 1)
    row = row_ids(OWN, 1)
    tv_own = jnp.sum(
        jnp.where((lane == me * own + row) & (row < own), tv_ref[0:1], 0.0), axis=1, keepdims=True
    )
    tv_top = jnp.sum(jnp.where(lane == row * layers, tv_ref[0:1], 0.0), axis=1, keepdims=True)[0:4]
    mine = me * own // layers
    for q in range(tiles):
        block = data_ref[q].astype(F32)
        live = decoded(block[OWN + 20 : OWN + 21])[1] & 7 != DEAD
        inj = [table_ref[q * 16 + h * 4 : q * 16 + h * 4 + 4, :] for h in range(subs)]
        inj = jnp.where(live, jnp.concatenate(inj, axis=1), 0.0)
        chosen_inj = jnp.zeros((1, col_max), F32)
        for s in range(4):
            chosen_inj = jnp.where(mine == s, inj[s : s + 1], chosen_inj)
        x_ref[0, q, 0:OWN] = block[0:OWN] + tv_own * chosen_inj
        x_ref[0, q, OWN : OWN + 4] = block[OWN : OWN + 4] + tv_top * inj

    k_own = kappa_ref[mine]
    k_top = jnp.zeros((4, 1), F32)
    for s in range(4):
        k_top = jnp.where(row_ids(4, 1) == s, kappa_ref[s], k_top)
    k_col = jnp.concatenate([jnp.full((OWN, 1), k_own, F32), k_top], axis=0)
    total_rows = OWN + 4

    for step in range(SUB):
        here, there = step % 2, (step + 1) % 2
        for q in range(tiles):
            x_ref[there, q] = (1.0 - 4.0 * k_col) * x_ref[here, q]

        def apply(q, carry):
            block = data_ref[q].astype(F32)
            power = decoded(block[OWN + 20 : OWN + 24])[1]
            high = power & 7
            value = k_col * x_ref[here, q]
            wide = value[0:OWN].astype(BF16)
            small = jnp.concatenate([value[OWN:total_rows]] * 4, axis=0).astype(BF16)
            total = jnp.zeros((7 * 16, WIDE), F32)
            for n in range(4):
                key = jnp.broadcast_to(high[n : n + 1].astype(F32), (16, col_max)).astype(BF16)
                skew = (high[n : n + 1] - quarter).astype(F32).astype(BF16)
                rows = [picked(key, wide, h) for h in range(5)]
                rows += [picked(skew, small, 0), picked(skew, small, 4)]
                rows = jnp.concatenate(rows, axis=0)
                low = block[OWN + 16 + n : OWN + 17 + n].astype(BF16)
                if not keep:
                    ones = hot(low, ids)
                elif step == 0:
                    ones = hot(low, ids)
                    hot_ref[q * 4 + n] = ones
                else:
                    ones = hot_ref[q * 4 + n]
                total = total + nt(rows, ones)
            for h in range(subs):
                cols = slice(h * WIDE, (h + 1) * WIDE)
                x_ref[there, q, 0:OWN, cols] += total[h * 16 : h * 16 + 16]
                x_ref[there, q, OWN:total_rows, cols] += total[80 + 4 * h : 84 + 4 * h]
            cross = jnp.concatenate([total[64:80], total[96:100]], axis=0)
            before, after = jnp.maximum(q - 1, 0), jnp.minimum(q + 1, tiles - 1)
            x_ref[there, before, :, LANES : 2 * LANES] += jnp.where(q > 0, cross[:, :LANES], 0.0)
            x_ref[there, after, :, :LANES] += jnp.where(q < tiles - 1, cross[:, LANES:], 0.0)
            return carry

        lax.fori_loop(0, tiles, apply, 0)
    for q in range(tiles):
        back_ref[q] = x_ref[SUB % 2, q, 0:own].astype(BF16)
        y_ref[q] = x_ref[SUB % 2, q, OWN:total_rows]


def gather_bottom(
    tiles, y_ref, part_any, slot_any, weight_any, out_ref, table_ref, found_ref,
    part_ref, slot_ref, weight_ref, sems,
):
    fetch([(part_any, part_ref), (slot_any, slot_ref), (weight_any, weight_ref)], sems)
    col_max = part_ref.shape[1]
    subs = col_max // WIDE
    half = tiles * subs // 2
    for i in range(half):
        first, other = i, i + half
        a = y_ref[first // subs, :, (first % subs) * WIDE : (first % subs + 1) * WIDE]
        b = y_ref[other // subs, :, (other % subs) * WIDE : (other % subs + 1) * WIDE]
        table_ref[i * 8 : i * 8 + 8, :] = jnp.concatenate([a, b], axis=0)
    table = table_ref[...].astype(BF16)
    slot = slot_ref[...]
    high = part_ref[...] * subs + slot // WIDE
    low = (slot % WIDE).astype(F32).astype(BF16)
    ids = row_ids(WIDE, 1).astype(F32).astype(BF16)
    offset = jnp.where(row_ids(8, 1) >= 4, half, 0)
    total = jnp.zeros((8, col_max), F32)
    for r in range(4):
        found_ref[...] = nn(table, hot(low[r : r + 1], ids))
        key = high[r : r + 1] - offset
        found = jnp.zeros((8, col_max), F32)
        for i in range(half):
            found = jnp.where(key == i, found_ref[i * 8 : i * 8 + 8, :], found)
        total = total + found * weight_ref[r : r + 1, :]
    bottom = total[0:4] + total[4:8]
    out_ref[...] = jnp.concatenate(
        [bottom, jnp.zeros((out_ref.shape[0] - 4, col_max), F32)], axis=0
    ).astype(BF16)


def combine(layers, reaction_ref, all_ref, tail_ref, state_ref, bottom_ref):
    parts, wide, col_max = all_ref.shape
    out_species, species = reaction_ref.shape
    own = species // parts
    width = out_species * layers
    mix = reaction_ref[...].astype(BF16)
    left = jnp.where(
        row_ids(width, out_species) // layers
        == lax.broadcasted_iota(jnp.int32, (width, out_species), 1),
        1.0,
        0.0,
    ).astype(BF16)
    right = jnp.where(
        row_ids(species, species * layers)
        == lax.broadcasted_iota(jnp.int32, (species, species * layers), 1) // layers,
        1.0,
        0.0,
    ).astype(BF16)
    full = nn(nn(left, mix).astype(BF16), right)
    same = (
        row_ids(width, species * layers) % layers
        == lax.broadcasted_iota(jnp.int32, (width, species * layers), 1) % layers
    )
    full = jnp.where(same, full, 0.0).astype(BF16)
    mixed = jnp.zeros((width, col_max), F32)
    bottom = jnp.zeros((out_species, col_max), F32)
    mix = mix.astype(F32)
    for k in range(parts):
        mixed = mixed + nn(full[:, k * wide : (k + 1) * wide], all_ref[k])
        tail = tail_ref[k].astype(F32)
        for s in range(own):
            col = k * own + s
            bottom = bottom + mix[:, col : col + 1] * tail[s : s + 1, :]
    state_ref[...] = mixed.T.astype(BF16)
    bottom_ref[...] = bottom


def body(
    grad_columns,
    grad_flux,
    remap_part,
    remap_slot,
    remap_weight,
    col_count,
    neighbors,
    kappa,
    thickness,
    vertical,
    reaction,
):
    tiles = lax.axis_size("tile")
    col_max, width = grad_columns.shape
    layers = thickness.shape[1]
    own = width // tiles
    entries = tiles * col_max // WIDE
    part_t, slot_t, weight_t, nbr_t = remap_part.T, remap_slot.T, remap_weight.T, neighbors.T
    shape = jax.ShapeDtypeStruct
    moved = [grad_columns, vertical, thickness, grad_flux, part_t, slot_t, weight_t, nbr_t]
    payload, tv = call(
        prepare,
        [shape((tiles, OWN + 24, col_max), BF16), shape((8, width), F32)],
        [SMEM] + [ANY] * 8,
        scratch=[pltpu.VMEM(a.shape, a.dtype) for a in moved] + [pltpu.SemaphoreType.DMA((8,))],
        flops=4 * 10**7,
        moved=10**6,
    )(col_count, *moved)
    data = lax.all_to_all(payload, "tile", split_axis=0, concat_axis=0, tiled=True)
    keep = tiles * 4 * WIDE * col_max * 2 <= 2**24
    back, y = call(
        functools.partial(chain, tiles, own, layers, keep),
        [shape((tiles, own, col_max), BF16), shape((tiles, 4, col_max), F32)],
        [SMEM] + [VMEM] * 2,
        scratch=[
            pltpu.VMEM((2, tiles, OWN + 4, col_max), F32),
            pltpu.VMEM((tiles * 16, WIDE), F32),
            pltpu.VMEM((tiles * 4 if keep else 1, WIDE, col_max), BF16),
        ],
        flops=10**10,
        moved=10**6,
    )(kappa, tv, data)
    home = lax.all_to_all(back, "tile", split_axis=0, concat_axis=0, tiled=True)
    remaps = [part_t, slot_t, weight_t]
    bottom = call(
        functools.partial(gather_bottom, tiles),
        [shape((16, col_max), BF16)],
        [VMEM] + [ANY] * 3,
        scratch=[pltpu.VMEM((entries * 4, WIDE), F32), pltpu.VMEM((entries * 4, col_max), F32)]
        + [pltpu.VMEM(a.shape, a.dtype) for a in remaps]
        + [pltpu.SemaphoreType.DMA((3,))],
        flops=10**9,
        moved=10**6,
    )(y, *remaps)[0]
    every_bottom = lax.all_gather(bottom, "spec", axis=0, tiled=False)
    every = lax.all_gather(home.reshape(width, col_max), "spec", axis=0, tiled=False)
    grad_state, grad_bottom = call(
        functools.partial(combine, layers),
        [shape((col_max, width), BF16), shape((reaction.shape[1], col_max), F32)],
        [VMEM] * 3,
        flops=2 * 10**8,
        moved=2 * 10**6,
    )(reaction.T, every, every_bottom)
    return grad_state, grad_bottom


def solution(mesh):
    placed = (
        P("tile", "spec"),
        P("spec", "tile"),
        P("tile", None),
        P("tile", None),
        P("tile", None),
        P("tile"),
        P("tile", None),
        P("spec"),
        P("spec", None),
        P("spec", None, None),
        P(None, "spec"),
    )
    return jax.shard_map(
        body,
        mesh=mesh,
        in_specs=placed,
        out_specs=(P("tile", "spec"), P("spec", "tile")),
        check_vma=False,
    )
```

```python
import functools

import jax
import jax.numpy as jnp
from jax import lax
from jax.experimental import pallas as pl
from jax.experimental.pallas import tpu as pltpu
from jax.sharding import PartitionSpec as P

SUB = 4
LANES = 128
WIDE = 256
OWN = 16
DEAD = 7
F32 = jnp.float32
BF16 = jnp.bfloat16
VMEM = pl.BlockSpec(memory_space=pltpu.VMEM)
HBM = pl.BlockSpec(memory_space=pltpu.HBM)
SMEM = pl.BlockSpec(memory_space=pltpu.SMEM)
LIMIT = 48 * 1024 * 1024


def call(kernel, outs, specs, scratch=(), flops=0, moved=0):
    return pl.pallas_call(
        kernel,
        out_shape=outs,
        in_specs=specs,
        out_specs=[VMEM] * len(outs),
        scratch_shapes=scratch,
        compiler_params=pltpu.CompilerParams(vmem_limit_bytes=LIMIT),
        cost_estimate=pl.CostEstimate(flops=flops, bytes_accessed=moved, transcendentals=0),
    )


def nt(a, b, precision=None):
    return lax.dot_general(
        a, b, (((1,), (1,)), ((), ())), precision=precision, preferred_element_type=F32
    )


def nn(a, b, precision=None):
    return lax.dot_general(
        a, b, (((1,), (0,)), ((), ())), precision=precision, preferred_element_type=F32
    )


def row_ids(rows, cols):
    return lax.broadcasted_iota(jnp.int32, (rows, cols), 0)


def fetch(pairs, sems):
    copies = [pltpu.make_async_copy(a, b, sems.at[i]) for i, (a, b) in enumerate(pairs)]
    for copy in copies:
        copy.start()
    for copy in copies:
        copy.wait()


def prepare(
    count_ref, gc_any, vert_any, thick_any, flux_any, part_any, slot_any, weight_any, nbr_any,
    payload_ref, tv_ref,
    gc_ref, vert_ref, thick_ref, flux_ref, part_ref, slot_ref, weight_ref, nbr_ref, sems,
):
    fetch(
        [
            (gc_any, gc_ref),
            (vert_any, vert_ref),
            (thick_any, thick_ref),
            (flux_any, flux_ref),
            (part_any, part_ref),
            (slot_any, slot_ref),
            (weight_any, weight_ref),
            (nbr_any, nbr_ref),
        ],
        sems,
    )
    tiles, block_rows, col_max = payload_ref.shape
    species, layers, _ = vert_ref.shape
    width = species * layers
    v = vert_ref[...].astype(F32).reshape(width, layers)
    v = jnp.concatenate([v] * species, axis=1)
    rows = row_ids(width, width) // layers
    cols = lax.broadcasted_iota(jnp.int32, (width, width), 1) // layers
    vt = jnp.where(rows == cols, v, 0.0).T
    hi = lax.Precision.HIGHEST
    v2 = nn(vt, vt, hi)
    v4 = nn(v2, v2, hi)
    th = jnp.concatenate([thick_ref[s : s + 1, :] for s in range(species)], axis=1)
    tv_ref[...] = nt(jnp.broadcast_to(th, (8, width)), v4, hi)
    live = lax.broadcasted_iota(jnp.int32, (1, col_max), 1) < count_ref[0]
    w = jnp.where(live, nt(v4.astype(BF16), gc_ref[...]), 0.0)
    top = [w[s * layers : s * layers + 1, :] for s in range(species)]
    slot, nbr = slot_ref[...], nbr_ref[...]
    power = (slot // WIDE) * 8 + jnp.where(live, nbr // WIDE, DEAD)
    code = 128.0 + part_ref[...].astype(F32)
    for bit in range(5):
        code = code * jnp.where((power >> bit) & 1 == 1, float(2 ** (2**bit)), 1.0)
    common = top + [
        flux_ref[...],
        weight_ref[...],
        (slot % WIDE).astype(F32),
        (nbr % WIDE).astype(F32),
        code,
    ]
    own = width // tiles
    pad = [] if own == OWN else [jnp.zeros((OWN - own, col_max), F32)]
    common = jnp.concatenate(common, axis=0).astype(BF16)
    for q in range(tiles):
        mine = jnp.concatenate([w[q * own : (q + 1) * own]] + pad, axis=0).astype(BF16)
        payload_ref[q] = jnp.concatenate([mine, common], axis=0)


def decoded(code):
    power = jnp.zeros(code.shape, jnp.int32)
    for bit in (16, 8, 4, 2, 1):
        large = code >= 128.0 * 2.0**bit
        code = jnp.where(large, code * 2.0**-bit, code)
        power = power + jnp.where(large, bit, 0)
    return code - 128.0, power


def hot(key, ids):
    return jnp.where(ids == key, jnp.ones((), BF16), jnp.zeros((), BF16))


def picked(keys, value, target):
    return jnp.where(keys == jnp.asarray(target, BF16), value, jnp.zeros((), BF16))


def chain(
    tiles, own, layers, keep, kappa_ref, tv_ref, data_ref, back_ref, y_ref, x_ref, table_ref, hot_ref
):
    col_max = data_ref.shape[2]
    subs = col_max // WIDE
    me = lax.axis_index("tile")
    ids = row_ids(WIDE, 1).astype(F32).astype(BF16)
    quarter = row_ids(16, 1) // 4

    table_ref[...] = jnp.zeros_like(table_ref)

    def gather(q, carry):
        block = data_ref[q].astype(F32)
        part, power = decoded(block[OWN + 20 : OWN + 24])
        sub = power >> 3
        for r in range(4):
            value = block[OWN + 4 : OWN + 8] * block[OWN + 8 + r : OWN + 9 + r]
            value = jnp.concatenate([value] * 4, axis=0).astype(BF16)
            key = jnp.where(sub[r : r + 1] == quarter, part[r : r + 1], -1.0).astype(BF16)
            rows = jnp.concatenate([picked(key, value, g) for g in range(tiles)], axis=0)
            low = block[OWN + 12 + r : OWN + 13 + r].astype(BF16)
            table_ref[...] += nt(hot(low, ids), rows)
        return carry

    lax.fori_loop(0, tiles, gather, 0)

    lane = lax.broadcasted_iota(jnp.int32, (OWN, tv_ref.shape[1]), 1)
    row = row_ids(OWN, 1)
    tv_own = jnp.sum(
        jnp.where((lane == me * own + row) & (row < own), tv_ref[0:1], 0.0), axis=1, keepdims=True
    )
    tv_top = jnp.sum(jnp.where(lane == row * layers, tv_ref[0:1], 0.0), axis=1, keepdims=True)[0:4]
    mine = me * own // layers
    table = table_ref[...].T
    for q in range(tiles):
        block = data_ref[q].astype(F32)
        live = decoded(block[OWN + 20 : OWN + 21])[1] & 7 != DEAD
        inj = [table[q * 16 + h * 4 : q * 16 + h * 4 + 4, :] for h in range(subs)]
        inj = jnp.where(live, jnp.concatenate(inj, axis=1), 0.0)
        chosen_inj = jnp.zeros((1, col_max), F32)
        for s in range(4):
            chosen_inj = jnp.where(mine == s, inj[s : s + 1], chosen_inj)
        x_ref[0, q, 0:OWN] = block[0:OWN] + tv_own * chosen_inj
        x_ref[0, q, OWN : OWN + 4] = block[OWN : OWN + 4] + tv_top * inj

    k_own = kappa_ref[mine]
    k_top = jnp.zeros((4, 1), F32)
    for s in range(4):
        k_top = jnp.where(row_ids(4, 1) == s, kappa_ref[s], k_top)
    k_col = jnp.concatenate([jnp.full((OWN, 1), k_own, F32), k_top], axis=0)
    total_rows = OWN + 4

    for step in range(SUB):
        here, there = step % 2, (step + 1) % 2
        for q in range(tiles):
            x_ref[there, q] = (1.0 - 4.0 * k_col) * x_ref[here, q]

        def apply(q, carry):
            block = data_ref[q].astype(F32)
            power = decoded(block[OWN + 20 : OWN + 24])[1]
            high = power & 7
            value = k_col * x_ref[here, q]
            wide = value[0:OWN].astype(BF16)
            small = jnp.concatenate([value[OWN:total_rows]] * 4, axis=0).astype(BF16)
            total = jnp.zeros((WIDE, 8 * 16), F32)
            for n in range(4):
                key = jnp.broadcast_to(high[n : n + 1].astype(F32), (16, col_max)).astype(BF16)
                skew = (high[n : n + 1] - quarter).astype(F32).astype(BF16)
                rows = [picked(key, wide, h) for h in range(5)]
                rows += [picked(skew, small, 0), picked(skew, small, 4), jnp.zeros((16, col_max), BF16)]
                rows = jnp.concatenate(rows, axis=0)
                low = block[OWN + 16 + n : OWN + 17 + n].astype(BF16)
                if not keep:
                    ones = hot(low, ids)
                elif step == 0:
                    ones = hot(low, ids)
                    hot_ref[q * 4 + n] = ones
                else:
                    ones = hot_ref[q * 4 + n]
                total = total + nt(ones, rows)
            total = total.T
            for h in range(subs):
                cols = slice(h * WIDE, (h + 1) * WIDE)
                x_ref[there, q, 0:OWN, cols] += total[h * 16 : h * 16 + 16]
                x_ref[there, q, OWN:total_rows, cols] += total[80 + 4 * h : 84 + 4 * h]
            cross = jnp.concatenate([total[64:80], total[96:100]], axis=0)
            before, after = jnp.maximum(q - 1, 0), jnp.minimum(q + 1, tiles - 1)
            x_ref[there, before, :, LANES : 2 * LANES] += jnp.where(q > 0, cross[:, :LANES], 0.0)
            x_ref[there, after, :, :LANES] += jnp.where(q < tiles - 1, cross[:, LANES:], 0.0)
            return carry

        lax.fori_loop(0, tiles, apply, 0)
    for q in range(tiles):
        back_ref[q] = x_ref[SUB % 2, q, 0:own].astype(BF16)
        y_ref[q] = x_ref[SUB % 2, q, OWN:total_rows]


def gather_bottom(
    tiles, y_ref, part_any, slot_any, weight_any, out_ref, table_ref, found_ref,
    part_ref, slot_ref, weight_ref, sems,
):
    fetch([(part_any, part_ref), (slot_any, slot_ref), (weight_any, weight_ref)], sems)
    col_max = part_ref.shape[1]
    subs = col_max // WIDE
    half = tiles * subs // 2
    for i in range(half):
        first, other = i, i + half
        a = y_ref[first // subs, :, (first % subs) * WIDE : (first % subs + 1) * WIDE]
        b = y_ref[other // subs, :, (other % subs) * WIDE : (other % subs + 1) * WIDE]
        table_ref[i * 8 : i * 8 + 8, :] = jnp.concatenate([a, b], axis=0)
    table = table_ref[...].astype(BF16)
    slot = slot_ref[...]
    high = part_ref[...] * subs + slot // WIDE
    low = (slot % WIDE).astype(F32).astype(BF16)
    ids = row_ids(WIDE, 1).astype(F32).astype(BF16)
    offset = jnp.where(row_ids(8, 1) >= 4, half, 0)
    total = jnp.zeros((8, col_max), F32)
    for r in range(4):
        found_ref[...] = nn(table, hot(low[r : r + 1], ids))
        key = high[r : r + 1] - offset
        found = jnp.zeros((8, col_max), F32)
        for i in range(half):
            found = jnp.where(key == i, found_ref[i * 8 : i * 8 + 8, :], found)
        total = total + found * weight_ref[r : r + 1, :]
    bottom = total[0:4] + total[4:8]
    out_ref[...] = jnp.concatenate(
        [bottom, jnp.zeros((out_ref.shape[0] - 4, col_max), F32)], axis=0
    ).astype(BF16)


def combine(layers, reaction_ref, all_ref, tail_ref, state_ref, bottom_ref):
    parts, wide, col_max = all_ref.shape
    out_species, species = reaction_ref.shape
    own = species // parts
    width = out_species * layers
    mix = reaction_ref[...].astype(BF16)
    left = jnp.where(
        row_ids(width, out_species) // layers
        == lax.broadcasted_iota(jnp.int32, (width, out_species), 1),
        1.0,
        0.0,
    ).astype(BF16)
    right = jnp.where(
        row_ids(species, species * layers)
        == lax.broadcasted_iota(jnp.int32, (species, species * layers), 1) // layers,
        1.0,
        0.0,
    ).astype(BF16)
    full = nn(nn(left, mix).astype(BF16), right)
    same = (
        row_ids(width, species * layers) % layers
        == lax.broadcasted_iota(jnp.int32, (width, species * layers), 1) % layers
    )
    full = jnp.where(same, full, 0.0).astype(BF16)
    mixed = jnp.zeros((width, col_max), F32)
    bottom = jnp.zeros((out_species, col_max), F32)
    mix = mix.astype(F32)
    for k in range(parts):
        mixed = mixed + nn(full[:, k * wide : (k + 1) * wide], all_ref[k])
        tail = tail_ref[k].astype(F32)
        for s in range(own):
            col = k * own + s
            bottom = bottom + mix[:, col : col + 1] * tail[s : s + 1, :]
    state_ref[...] = mixed.T.astype(BF16)
    bottom_ref[...] = bottom


def body(
    grad_columns,
    grad_flux,
    remap_part,
    remap_slot,
    remap_weight,
    col_count,
    neighbors,
    kappa,
    thickness,
    vertical,
    reaction,
):
    tiles = lax.axis_size("tile")
    col_max, width = grad_columns.shape
    layers = thickness.shape[1]
    own = width // tiles
    entries = tiles * col_max // WIDE
    part_t, slot_t, weight_t, nbr_t = remap_part.T, remap_slot.T, remap_weight.T, neighbors.T
    shape = jax.ShapeDtypeStruct
    moved = [grad_columns, vertical, thickness, grad_flux, part_t, slot_t, weight_t, nbr_t]
    payload, tv = call(
        prepare,
        [shape((tiles, OWN + 24, col_max), BF16), shape((8, width), F32)],
        [SMEM] + [HBM] * 8,
        scratch=[pltpu.VMEM(a.shape, a.dtype) for a in moved] + [pltpu.SemaphoreType.DMA((8,))],
        flops=4 * 10**7,
        moved=10**6,
    )(col_count, *moved)
    data = lax.all_to_all(payload, "tile", split_axis=0, concat_axis=0, tiled=True)
    keep = tiles * 4 * WIDE * col_max * 2 <= 2**24
    back, y = call(
        functools.partial(chain, tiles, own, layers, keep),
        [shape((tiles, own, col_max), BF16), shape((tiles, 4, col_max), F32)],
        [SMEM] + [VMEM] * 2,
        scratch=[
            pltpu.VMEM((2, tiles, OWN + 4, col_max), F32),
            pltpu.VMEM((WIDE, tiles * 16), F32),
            pltpu.VMEM((tiles * 4 if keep else 1, WIDE, col_max), BF16),
        ],
        flops=10**10,
        moved=10**6,
    )(kappa, tv, data)
    home = lax.all_to_all(back, "tile", split_axis=0, concat_axis=0, tiled=True)
    remaps = [part_t, slot_t, weight_t]
    bottom = call(
        functools.partial(gather_bottom, tiles),
        [shape((16, col_max), BF16)],
        [VMEM] + [HBM] * 3,
        scratch=[pltpu.VMEM((entries * 4, WIDE), F32), pltpu.VMEM((entries * 4, col_max), F32)]
        + [pltpu.VMEM(a.shape, a.dtype) for a in remaps]
        + [pltpu.SemaphoreType.DMA((3,))],
        flops=10**9,
        moved=10**6,
    )(y, *remaps)[0]
    every_bottom = lax.all_gather(bottom, "spec", axis=0, tiled=False)
    every = lax.all_gather(home.reshape(width, col_max), "spec", axis=0, tiled=False)
    grad_state, grad_bottom = call(
        functools.partial(combine, layers),
        [shape((col_max, width), BF16), shape((reaction.shape[1], col_max), F32)],
        [VMEM] * 3,
        flops=2 * 10**8,
        moved=2 * 10**6,
    )(reaction.T, every, every_bottom)
    return grad_state, grad_bottom


def solution(mesh):
    placed = (
        P("tile", "spec"),
        P("spec", "tile"),
        P("tile", None),
        P("tile", None),
        P("tile", None),
        P("tile"),
        P("tile", None),
        P("spec"),
        P("spec", None),
        P("spec", None, None),
        P(None, "spec"),
    )
    return jax.shard_map(
        body,
        mesh=mesh,
        in_specs=placed,
        out_specs=(P("tile", "spec"), P("spec", "tile")),
        check_vma=False,
    )
```

```python
import functools

import jax
import jax.numpy as jnp
from jax import lax
from jax.experimental import pallas as pl
from jax.experimental.pallas import tpu as pltpu
from jax.sharding import PartitionSpec as P

SUB = 4
LANES = 128
WIDE = 256
OWN = 16
DEAD = 7
F32 = jnp.float32
BF16 = jnp.bfloat16
VMEM = pl.BlockSpec(memory_space=pltpu.VMEM)
HBM = pl.BlockSpec(memory_space=pltpu.HBM)
SMEM = pl.BlockSpec(memory_space=pltpu.SMEM)
LIMIT = 40 * 1024 * 1024
MOST = 60 * 1024 * 1024


def call(kernel, outs, specs, scratch=(), flops=0, moved=0, limit=LIMIT):
    return pl.pallas_call(
        kernel,
        out_shape=outs,
        in_specs=specs,
        out_specs=[VMEM] * len(outs),
        scratch_shapes=scratch,
        compiler_params=pltpu.CompilerParams(vmem_limit_bytes=limit),
        cost_estimate=pl.CostEstimate(flops=flops, bytes_accessed=moved, transcendentals=0),
    )


def nt(a, b, precision=None):
    return lax.dot_general(
        a, b, (((1,), (1,)), ((), ())), precision=precision, preferred_element_type=F32
    )


def nn(a, b, precision=None):
    return lax.dot_general(
        a, b, (((1,), (0,)), ((), ())), precision=precision, preferred_element_type=F32
    )


def row_ids(rows, cols):
    return lax.broadcasted_iota(jnp.int32, (rows, cols), 0)


def fetch(pairs, sems):
    copies = [pltpu.make_async_copy(a, b, sems.at[i]) for i, (a, b) in enumerate(pairs)]
    for copy in copies:
        copy.start()
    for copy in copies:
        copy.wait()


def prepare(
    count_ref, kappa_ref, gc_any, vert_any, thick_any, flux_any, part_any, slot_any, weight_any,
    nbr_any, payload_ref, misc_ref,
    gc_ref, vert_ref, thick_ref, flux_ref, part_ref, slot_ref, weight_ref, nbr_ref, sems,
):
    fetch(
        [
            (gc_any, gc_ref),
            (vert_any, vert_ref),
            (thick_any, thick_ref),
            (flux_any, flux_ref),
            (part_any, part_ref),
            (slot_any, slot_ref),
            (weight_any, weight_ref),
            (nbr_any, nbr_ref),
        ],
        sems,
    )
    tiles, block_rows, col_max = payload_ref.shape
    species, layers, _ = vert_ref.shape
    width = species * layers
    v = vert_ref[...].astype(F32).reshape(width, layers)
    v = jnp.concatenate([v] * species, axis=1)
    rows = row_ids(width, width) // layers
    cols = lax.broadcasted_iota(jnp.int32, (width, width), 1) // layers
    vt = jnp.where(rows == cols, v, 0.0).T
    hi = lax.Precision.HIGHEST
    v2 = nn(vt, vt, hi)
    v4 = nn(v2, v2, hi)
    th = jnp.concatenate([thick_ref[s : s + 1, :] for s in range(species)], axis=1)
    misc_ref[0:8] = nt(jnp.broadcast_to(th, (8, width)), v4, hi)
    rates = [jnp.full((1, width), kappa_ref[s], F32) for s in range(species)]
    misc_ref[8:16] = jnp.concatenate(rates + rates, axis=0)
    live = lax.broadcasted_iota(jnp.int32, (1, col_max), 1) < count_ref[0]
    w = jnp.where(live, nt(v4.astype(BF16), gc_ref[...]), 0.0)
    slot, nbr = slot_ref[...], nbr_ref[...]
    power = (slot // WIDE) * 8 + jnp.where(live, nbr // WIDE, DEAD)
    code = 128.0 + part_ref[...].astype(F32)
    for bit in range(5):
        code = code * jnp.where((power >> bit) & 1 == 1, float(2 ** (2**bit)), 1.0)
    common = [(slot % WIDE).astype(F32), (nbr % WIDE).astype(F32), code]
    common = jnp.concatenate(common, axis=0)
    own = width // tiles
    pad = [] if own == OWN else [jnp.zeros((OWN - own, col_max), F32)]
    flux, weight = flux_ref[...], weight_ref[...]
    for q in range(tiles):
        s = q * own // layers
        pieces = [w[q * own : (q + 1) * own]] + pad + [flux[s : s + 1] * weight, common]
        payload_ref[q] = jnp.concatenate(pieces, axis=0).astype(BF16)


def decoded(code):
    power = jnp.zeros(code.shape, jnp.int32)
    for bit in (16, 8, 4, 2, 1):
        large = code >= 128.0 * 2.0**bit
        code = jnp.where(large, code * 2.0**-bit, code)
        power = power + jnp.where(large, bit, 0)
    return code - 128.0, power


def hot(key, ids):
    return jnp.where(ids == key, jnp.ones((), BF16), jnp.zeros((), BF16))


def picked(keys, value, target):
    return jnp.where(keys == jnp.asarray(target, BF16), value, jnp.zeros((), BF16))


def narrow(ints):
    return ints.astype(F32).astype(BF16)


def each(count, step):
    if count <= 8:
        for q in range(count):
            step(q, 0)
    else:
        lax.fori_loop(0, count, step, 0)


def chain(tiles, own, layers, keep, misc_ref, data_ref, *refs):
    back_ref, rest = refs[0], refs[1:]
    if not keep:
        y_ref, rest = rest[0], rest[1:]
    x_ref, table_ref, hot_ref = rest
    col_max = data_ref.shape[2]
    blocks = col_max // LANES
    me = lax.axis_index("tile")
    ids = narrow(row_ids(LANES, 1))
    half = row_ids(16, 1) // blocks
    within = row_ids(16, 1) % blocks

    table_ref[...] = jnp.zeros_like(table_ref)

    def gather(q, carry):
        block = data_ref[q].astype(F32)
        part, power = decoded(block[OWN + 12 : OWN + 16])
        low = block[OWN + 4 : OWN + 8].astype(jnp.int32)
        sub = (power >> 3) * 2 + (low >> 7)
        low = narrow(low & 127)
        total = jnp.zeros(table_ref.shape, F32)
        for r in range(4):
            value = block[OWN + r : OWN + r + 1]
            value = jnp.broadcast_to(value, (16, col_max)).astype(BF16)
            key = jnp.where(sub[r : r + 1] == within, part[r : r + 1] - half.astype(F32), -3.0)
            key = key.astype(BF16)
            rows = jnp.concatenate([picked(key, value, 2 * g) for g in range(tiles // 2)], axis=0)
            total = total + nt(rows, hot(low[r : r + 1], ids))
        table_ref[...] += total
        return carry

    each(tiles, gather)

    lane = lax.broadcasted_iota(jnp.int32, (OWN, misc_ref.shape[1]), 1)
    row = row_ids(OWN, 1)
    tv_own = jnp.sum(
        jnp.where((lane == me * own + row) & (row < own), misc_ref[0:1], 0.0), axis=1, keepdims=True
    )
    mine = me * own // layers
    rate = jnp.zeros((1, 1), F32)
    for s in range(4):
        rate = jnp.where(mine == s, misc_ref[8 + s : 9 + s, 0:1], rate)

    def start(q, carry):
        block = data_ref[q].astype(F32)
        live = decoded(block[OWN + 12 : OWN + 13])[1] & 7 != DEAD
        piece = table_ref[pl.ds(q * blocks, blocks), :]
        inj = jnp.concatenate([piece[h : h + 1] for h in range(blocks)], axis=1)
        x_ref[0, q] = block[0:OWN] + tv_own * jnp.where(live, inj, 0.0)
        return carry

    each(tiles, start)

    for step in range(SUB):
        here, there = step % 2, (step + 1) % 2
        for q in range(tiles):
            x_ref[there, q] = (1.0 - 4.0 * rate) * x_ref[here, q]

        def apply(q, carry):
            block = data_ref[q].astype(F32)
            low = block[OWN + 8 : OWN + 12].astype(jnp.int32)
            high = (decoded(block[OWN + 12 : OWN + 16])[1] & 7) * 2 + (low >> 7)
            value = (rate * x_ref[here, q]).astype(BF16)
            total = jnp.zeros(((blocks + 2) * OWN, LANES), F32)
            for n in range(4):
                key = narrow(jnp.broadcast_to(high[n : n + 1], (OWN, col_max)))
                rows = [picked(key, value, h) for h in range(blocks + 2)]
                if not keep or step == 0:
                    ones = hot(narrow(low[n : n + 1] & 127), ids)
                else:
                    ones = hot_ref[q * 4 + n]
                if keep and step == 0:
                    hot_ref[q * 4 + n] = ones
                total = total + nt(jnp.concatenate(rows, axis=0), ones)
            mine_rows = [total[h * OWN : (h + 1) * OWN] for h in range(blocks)]
            x_ref[there, q] += jnp.concatenate(mine_rows, axis=1)
            cross = [total[(blocks + k) * OWN : (blocks + k + 1) * OWN] for k in range(2)]
            if isinstance(q, int):
                if q > 0:
                    x_ref[there, q - 1, :, LANES : 2 * LANES] += cross[0]
                if q < tiles - 1:
                    x_ref[there, q + 1, :, :LANES] += cross[1]
            else:
                before, after = jnp.maximum(q - 1, 0), jnp.minimum(q + 1, tiles - 1)
                x_ref[there, before, :, LANES : 2 * LANES] += jnp.where(q > 0, cross[0], 0.0)
                x_ref[there, after, :, :LANES] += jnp.where(q < tiles - 1, cross[1], 0.0)
            return carry

        each(tiles, apply)
    last = SUB % 2
    top = jnp.concatenate([x_ref[last, q, 0:1] for q in range(tiles)], axis=0)
    for q in range(tiles):
        if keep:
            back_ref[q] = jnp.concatenate([x_ref[last, q], top], axis=0).astype(BF16)
        else:
            back_ref[q] = x_ref[last, q, 0:own].astype(BF16)
    if not keep:
        y_ref[...] = top


def gather_bottom(
    tiles, keep, y_ref, part_any, slot_any, weight_any, out_ref, found_ref,
    part_ref, slot_ref, weight_ref, sems,
):
    fetch([(part_any, part_ref), (slot_any, slot_ref), (weight_any, weight_ref)], sems)
    col_max = part_ref.shape[1]
    subs = col_max // WIDE
    table = []
    for s in range(4):
        y = (y_ref[s * tiles // 4].astype(F32)[OWN:] if keep else y_ref[s].astype(F32))
        table += [y[:, h * WIDE : (h + 1) * WIDE] for h in range(subs)]
    table = jnp.concatenate(table, axis=0).astype(BF16)
    slot, part = slot_ref[...], part_ref[...]
    sub = slot // WIDE
    low = narrow(slot % WIDE)
    ids = narrow(row_ids(WIDE, 1))
    places = row_ids(tiles, 1)
    totals = [jnp.zeros((tiles, col_max), F32) for s in range(4)]
    for r in range(4):
        found_ref[...] = nn(table, hot(low[r : r + 1], ids))
        key = jnp.where(part[r : r + 1] == places, sub[r : r + 1], -1)
        weight = weight_ref[r : r + 1, :]
        for s in range(4):
            found = jnp.zeros((tiles, col_max), F32)
            for h in range(subs):
                at = (s * subs + h) * tiles
                found = jnp.where(key == h, found_ref[at : at + tiles, :], found)
            totals[s] = totals[s] + found * weight
    rows = [jnp.sum(total, axis=0, keepdims=True) for total in totals]
    rows.append(jnp.zeros((out_ref.shape[0] - 4, col_max), F32))
    out_ref[...] = jnp.concatenate(rows, axis=0).astype(BF16)


def combine(layers, reaction_ref, all_ref, tail_ref, state_ref, bottom_ref):
    parts, wide, col_max = all_ref.shape
    out_species, species = reaction_ref.shape
    own = species // parts
    width = out_species * layers
    mix = reaction_ref[...].astype(BF16)
    left = jnp.where(
        row_ids(width, out_species) // layers
        == lax.broadcasted_iota(jnp.int32, (width, out_species), 1),
        1.0,
        0.0,
    ).astype(BF16)
    right = jnp.where(
        row_ids(species, species * layers)
        == lax.broadcasted_iota(jnp.int32, (species, species * layers), 1) // layers,
        1.0,
        0.0,
    ).astype(BF16)
    full = nn(nn(left, mix).astype(BF16), right)
    same = (
        row_ids(width, species * layers) % layers
        == lax.broadcasted_iota(jnp.int32, (width, species * layers), 1) % layers
    )
    full = jnp.where(same, full, 0.0).astype(BF16)
    mixed = jnp.zeros((width, col_max), F32)
    bottom = jnp.zeros((out_species, col_max), F32)
    mix = mix.astype(F32)
    for k in range(parts):
        mixed = mixed + nn(full[:, k * wide : (k + 1) * wide], all_ref[k])
        tail = tail_ref[k].astype(F32)
        for s in range(own):
            col = k * own + s
            bottom = bottom + mix[:, col : col + 1] * tail[s : s + 1, :]
    state_ref[...] = mixed.T.astype(BF16)
    bottom_ref[...] = bottom


def body(
    grad_columns,
    grad_flux,
    remap_part,
    remap_slot,
    remap_weight,
    col_count,
    neighbors,
    kappa,
    thickness,
    vertical,
    reaction,
):
    tiles = lax.axis_size("tile")
    col_max, width = grad_columns.shape
    layers = thickness.shape[1]
    own = width // tiles
    entries = tiles * col_max // WIDE
    part_t, slot_t, weight_t, nbr_t = remap_part.T, remap_slot.T, remap_weight.T, neighbors.T
    shape = jax.ShapeDtypeStruct
    moved = [grad_columns, vertical, thickness, grad_flux, part_t, slot_t, weight_t, nbr_t]
    payload, misc = call(
        prepare,
        [shape((tiles, OWN + 16, col_max), BF16), shape((16, width), F32)],
        [SMEM] * 2 + [HBM] * 8,
        scratch=[pltpu.VMEM(a.shape, a.dtype) for a in moved] + [pltpu.SemaphoreType.DMA((8,))],
        flops=4 * 10**7,
        moved=10**6,
        limit=MOST,
    )(col_count, kappa, *moved)
    data = lax.all_to_all(payload, "tile", split_axis=0, concat_axis=0, tiled=True)
    keep = tiles == 8
    sent = OWN + tiles if keep else own
    backs = [shape((tiles, sent, col_max), BF16)]
    if not keep:
        backs.append(shape((tiles, col_max), F32))
    back = call(
        functools.partial(chain, tiles, own, layers, keep),
        backs,
        [VMEM] * 2,
        scratch=[
            pltpu.VMEM((2, tiles, OWN, col_max), F32),
            pltpu.VMEM((tiles * col_max // LANES, LANES), F32),
            pltpu.VMEM((tiles * 4 if keep else 1, LANES, col_max), BF16),
        ],
        flops=10**10,
        moved=10**6,
    )(misc, data)
    home = lax.all_to_all(back[0], "tile", split_axis=0, concat_axis=0, tiled=True)
    if keep:
        y = home
    else:
        place = lax.axis_index("tile") * own
        mark = jnp.arange(4)[:, None, None] * layers == place
        y = lax.psum(jnp.where(mark, back[1][None], 0.0).astype(BF16), "tile")
    remaps = [part_t, slot_t, weight_t]
    bottom = call(
        functools.partial(gather_bottom, tiles, keep),
        [shape((16, col_max), BF16)],
        [VMEM] + [HBM] * 3,
        scratch=[pltpu.VMEM((entries * 4, col_max), F32)]
        + [pltpu.VMEM(a.shape, a.dtype) for a in remaps]
        + [pltpu.SemaphoreType.DMA((3,))],
        flops=10**9,
        moved=10**6,
    )(y, *remaps)[0]
    every_bottom = lax.all_gather(bottom, "spec", axis=0, tiled=False)
    every = lax.all_gather(home[:, :own].reshape(width, col_max), "spec", axis=0, tiled=False)
    grad_state, grad_bottom = call(
        functools.partial(combine, layers),
        [shape((col_max, width), BF16), shape((reaction.shape[1], col_max), F32)],
        [VMEM] * 3,
        flops=2 * 10**8,
        moved=2 * 10**6,
    )(reaction.T, every, every_bottom)
    return grad_state, grad_bottom


def solution(mesh):
    placed = (
        P("tile", "spec"),
        P("spec", "tile"),
        P("tile", None),
        P("tile", None),
        P("tile", None),
        P("tile"),
        P("tile", None),
        P("spec"),
        P("spec", None),
        P("spec", None, None),
        P(None, "spec"),
    )
    return jax.shard_map(
        body,
        mesh=mesh,
        in_specs=placed,
        out_specs=(P("tile", "spec"), P("spec", "tile")),
        check_vma=False,
    )
```

```python
import functools

import jax
import jax.numpy as jnp
from jax import lax
from jax.experimental import pallas as pl
from jax.experimental.pallas import tpu as pltpu
from jax.sharding import PartitionSpec as P

SUB = 4
LANES = 128
WIDE = 256
OWN = 16
DEAD = 7
F32 = jnp.float32
BF16 = jnp.bfloat16
VMEM = pl.BlockSpec(memory_space=pltpu.VMEM)
HBM = pl.BlockSpec(memory_space=pltpu.HBM)
SMEM = pl.BlockSpec(memory_space=pltpu.SMEM)
LIMIT = 40 * 1024 * 1024
MOST = 60 * 1024 * 1024


def call(kernel, outs, specs, scratch=(), flops=0, moved=0, limit=LIMIT):
    return pl.pallas_call(
        kernel,
        out_shape=outs,
        in_specs=specs,
        out_specs=[VMEM] * len(outs),
        scratch_shapes=scratch,
        compiler_params=pltpu.CompilerParams(vmem_limit_bytes=limit),
        cost_estimate=pl.CostEstimate(flops=flops, bytes_accessed=moved, transcendentals=0),
    )


def nt(a, b, precision=None):
    return lax.dot_general(
        a, b, (((1,), (1,)), ((), ())), precision=precision, preferred_element_type=F32
    )


def nn(a, b, precision=None):
    return lax.dot_general(
        a, b, (((1,), (0,)), ((), ())), precision=precision, preferred_element_type=F32
    )


def row_ids(rows, cols):
    return lax.broadcasted_iota(jnp.int32, (rows, cols), 0)


def fetch(pairs, sems):
    copies = [pltpu.make_async_copy(a, b, sems.at[i]) for i, (a, b) in enumerate(pairs)]
    for copy in copies:
        copy.start()
    for copy in copies:
        copy.wait()


def prepare(
    count_ref, kappa_ref, gc_any, vert_any, thick_any, flux_any, part_any, slot_any, weight_any,
    nbr_any, reaction_any, payload_ref, misc_ref, remap_ref,
    gc_ref, vert_ref, thick_ref, flux_ref, part_ref, slot_ref, weight_ref, nbr_ref, reaction_ref,
    sems,
):
    fetch(
        [
            (gc_any, gc_ref),
            (vert_any, vert_ref),
            (thick_any, thick_ref),
            (flux_any, flux_ref),
            (part_any, part_ref),
            (slot_any, slot_ref),
            (weight_any, weight_ref),
            (nbr_any, nbr_ref),
            (reaction_any, reaction_ref),
        ],
        sems,
    )
    tiles, block_rows, col_max = payload_ref.shape
    species, layers, _ = vert_ref.shape
    width = species * layers
    v = vert_ref[...].astype(F32).reshape(width, layers)
    v = jnp.concatenate([v] * species, axis=1)
    rows = row_ids(width, width) // layers
    cols = lax.broadcasted_iota(jnp.int32, (width, width), 1) // layers
    vt = jnp.where(rows == cols, v, 0.0).T
    hi = lax.Precision.HIGHEST
    v2 = nn(vt, vt, hi)
    v4 = nn(v2, v2, hi)
    th = jnp.concatenate([thick_ref[s : s + 1, :] for s in range(species)], axis=1)
    misc_ref[0:8] = nt(jnp.broadcast_to(th, (8, width)), v4, hi)
    rates = [jnp.full((1, width), kappa_ref[s], F32) for s in range(species)]
    mix = reaction_ref[...].astype(F32)
    mix = jnp.concatenate([mix, jnp.zeros((4, width - mix.shape[1]), F32)], axis=1)
    misc_ref[8:16] = jnp.concatenate(rates + [mix], axis=0)
    live = lax.broadcasted_iota(jnp.int32, (1, col_max), 1) < count_ref[0]
    w = jnp.where(live, nt(v4.astype(BF16), gc_ref[...]), 0.0)
    slot, nbr = slot_ref[...], nbr_ref[...]
    power = (slot // WIDE) * 8 + jnp.where(live, nbr // WIDE, DEAD)
    code = 128.0 + part_ref[...].astype(F32)
    for bit in range(5):
        code = code * jnp.where((power >> bit) & 1 == 1, float(2 ** (2**bit)), 1.0)
    common = [(slot % WIDE).astype(F32), (nbr % WIDE).astype(F32), code]
    common = jnp.concatenate(common, axis=0)
    own = width // tiles
    pad = [] if own == OWN else [jnp.zeros((OWN - own, col_max), F32)]
    flux, weight = flux_ref[...], weight_ref[...]
    subs = (slot // WIDE).astype(F32)
    remap_ref[...] = jnp.concatenate([common[0:4], part_ref[...].astype(F32), subs, weight], axis=0)
    for q in range(tiles):
        s = q * own // layers
        pieces = [w[q * own : (q + 1) * own]] + pad + [flux[s : s + 1] * weight, common]
        payload_ref[q] = jnp.concatenate(pieces, axis=0).astype(BF16)


def decoded(code):
    power = jnp.zeros(code.shape, jnp.int32)
    for bit in (16, 8, 4, 2, 1):
        large = code >= 128.0 * 2.0**bit
        code = jnp.where(large, code * 2.0**-bit, code)
        power = power + jnp.where(large, bit, 0)
    return code - 128.0, power


def hot(key, ids):
    return jnp.where(ids == key, jnp.ones((), BF16), jnp.zeros((), BF16))


def picked(keys, value, target):
    return jnp.where(keys == jnp.asarray(target, BF16), value, jnp.zeros((), BF16))


def narrow(ints):
    return ints.astype(F32).astype(BF16)


def each(count, step):
    if count <= 8:
        for q in range(count):
            step(q, 0)
    else:
        lax.fori_loop(0, count, step, 0)


def chain(tiles, own, layers, keep, misc_ref, data_ref, *refs):
    back_ref, rest = refs[0], refs[1:]
    if not keep:
        y_ref, rest = rest[0], rest[1:]
    x_ref, table_ref, hot_ref = rest
    col_max = data_ref.shape[2]
    blocks = col_max // LANES
    me = lax.axis_index("tile")
    ids = narrow(row_ids(LANES, 1))
    half = row_ids(16, 1) // blocks
    within = row_ids(16, 1) % blocks

    table_ref[...] = jnp.zeros_like(table_ref)

    def gather(q, carry):
        block = data_ref[q].astype(F32)
        part, power = decoded(block[OWN + 12 : OWN + 16])
        low = block[OWN + 4 : OWN + 8].astype(jnp.int32)
        sub = (power >> 3) * 2 + (low >> 7)
        low = narrow(low & 127)
        total = jnp.zeros(table_ref.shape, F32)
        for r in range(4):
            value = block[OWN + r : OWN + r + 1]
            value = jnp.broadcast_to(value, (16, col_max)).astype(BF16)
            key = jnp.where(sub[r : r + 1] == within, part[r : r + 1] - half.astype(F32), -3.0)
            key = key.astype(BF16)
            rows = jnp.concatenate([picked(key, value, 2 * g) for g in range(tiles // 2)], axis=0)
            total = total + nt(rows, hot(low[r : r + 1], ids))
        table_ref[...] += total
        return carry

    each(tiles, gather)

    lane = lax.broadcasted_iota(jnp.int32, (OWN, misc_ref.shape[1]), 1)
    row = row_ids(OWN, 1)
    tv_own = jnp.sum(
        jnp.where((lane == me * own + row) & (row < own), misc_ref[0:1], 0.0), axis=1, keepdims=True
    )
    mine = me * own // layers
    rate = jnp.zeros((1, 1), F32)
    for s in range(4):
        rate = jnp.where(mine == s, misc_ref[8 + s : 9 + s, 0:1], rate)

    def start(q, carry):
        block = data_ref[q].astype(F32)
        live = decoded(block[OWN + 12 : OWN + 13])[1] & 7 != DEAD
        piece = table_ref[pl.ds(q * blocks, blocks), :]
        inj = jnp.concatenate([piece[h : h + 1] for h in range(blocks)], axis=1)
        x_ref[0, q] = block[0:OWN] + tv_own * jnp.where(live, inj, 0.0)
        return carry

    each(tiles, start)

    for step in range(SUB):
        here, there = step % 2, (step + 1) % 2
        for q in range(tiles):
            x_ref[there, q] = (1.0 - 4.0 * rate) * x_ref[here, q]

        def apply(q, carry):
            block = data_ref[q].astype(F32)
            low = block[OWN + 8 : OWN + 12].astype(jnp.int32)
            high = (decoded(block[OWN + 12 : OWN + 16])[1] & 7) * 2 + (low >> 7)
            value = (rate * x_ref[here, q]).astype(BF16)
            total = jnp.zeros(((blocks + 2) * OWN, LANES), F32)
            for n in range(4):
                key = narrow(jnp.broadcast_to(high[n : n + 1], (OWN, col_max)))
                rows = [picked(key, value, h) for h in range(blocks + 2)]
                if not keep or step == 0:
                    ones = hot(narrow(low[n : n + 1] & 127), ids)
                else:
                    ones = hot_ref[q * 4 + n]
                if keep and step == 0:
                    hot_ref[q * 4 + n] = ones
                total = total + nt(jnp.concatenate(rows, axis=0), ones)
            mine_rows = [total[h * OWN : (h + 1) * OWN] for h in range(blocks)]
            x_ref[there, q] += jnp.concatenate(mine_rows, axis=1)
            cross = [total[(blocks + k) * OWN : (blocks + k + 1) * OWN] for k in range(2)]
            if isinstance(q, int):
                if q > 0:
                    x_ref[there, q - 1, :, LANES : 2 * LANES] += cross[0]
                if q < tiles - 1:
                    x_ref[there, q + 1, :, :LANES] += cross[1]
            else:
                before, after = jnp.maximum(q - 1, 0), jnp.minimum(q + 1, tiles - 1)
                x_ref[there, before, :, LANES : 2 * LANES] += jnp.where(q > 0, cross[0], 0.0)
                x_ref[there, after, :, :LANES] += jnp.where(q < tiles - 1, cross[1], 0.0)
            return carry

        each(tiles, apply)
    last = SUB % 2
    top = jnp.concatenate([x_ref[last, q, 0:1] for q in range(tiles)], axis=0)
    for q in range(tiles):
        if keep:
            back_ref[q] = jnp.concatenate([x_ref[last, q], top], axis=0).astype(BF16)
        else:
            back_ref[q] = x_ref[last, q, 0:own].astype(BF16)
    if not keep:
        y_ref[...] = top


def gather_bottom(tiles, own, parts, keep, y_ref, home_ref, remap_ref, out_ref, found_ref):
    col_max = remap_ref.shape[1]
    width = tiles * own
    subs = col_max // WIDE
    table = []
    for s in range(4):
        y = y_ref[s * tiles // 4, OWN:] if keep else y_ref[s]
        table += [y[:, h * WIDE : (h + 1) * WIDE] for h in range(subs)]
    table = jnp.concatenate([piece.astype(F32) for piece in table], axis=0).astype(BF16)
    low = remap_ref[0:4].astype(BF16)
    part = remap_ref[4:8].astype(jnp.int32)
    sub = remap_ref[8:12].astype(jnp.int32)
    ids = narrow(row_ids(WIDE, 1))
    places = row_ids(tiles, 1)
    totals = [jnp.zeros((tiles, col_max), F32) for s in range(4)]
    for r in range(4):
        found_ref[...] = nn(table, hot(low[r : r + 1], ids))
        key = jnp.where(part[r : r + 1] == places, sub[r : r + 1], -1)
        weight = remap_ref[12 + r : 13 + r]
        for s in range(4):
            found = jnp.zeros((tiles, col_max), F32)
            for h in range(subs):
                at = (s * subs + h) * tiles
                found = jnp.where(key == h, found_ref[at : at + tiles, :], found)
            totals[s] = totals[s] + found * weight
    rows = [jnp.sum(total, axis=0, keepdims=True) for total in totals]
    rows.append(jnp.zeros((16 - 4, col_max), F32))
    rows = jnp.concatenate(rows, axis=0).astype(BF16)
    for k in range(parts):
        if keep:
            for q in range(tiles):
                out_ref[k, q * own : (q + 1) * own] = home_ref[q, :own]
        else:
            out_ref[k, :width] = home_ref[...]
        out_ref[k, width:] = rows


def combine(layers, misc_ref, all_ref, state_ref, bottom_ref):
    parts, rows, col_max = all_ref.shape
    wide = rows - 16
    own = wide // layers
    out_species, species = own, parts * own
    width = out_species * layers
    mix = misc_ref[12 : 12 + out_species, 0:species]
    left = jnp.where(
        row_ids(width, out_species) // layers
        == lax.broadcasted_iota(jnp.int32, (width, out_species), 1),
        1.0,
        0.0,
    ).astype(BF16)
    right = jnp.where(
        row_ids(species, species * layers)
        == lax.broadcasted_iota(jnp.int32, (species, species * layers), 1) // layers,
        1.0,
        0.0,
    ).astype(BF16)
    full = nn(nn(left, mix.astype(BF16)).astype(BF16), right)
    same = (
        row_ids(width, species * layers) % layers
        == lax.broadcasted_iota(jnp.int32, (width, species * layers), 1) % layers
    )
    full = jnp.where(same, full, 0.0).astype(BF16)
    mixed = jnp.zeros((width, col_max), F32)
    bottom = jnp.zeros((out_species, col_max), F32)
    for k in range(parts):
        mixed = mixed + nn(full[:, k * wide : (k + 1) * wide], all_ref[k, :wide, :])
        tail = all_ref[k, wide:, :].astype(F32)
        for s in range(own):
            col = k * own + s
            bottom = bottom + mix[:, col : col + 1] * tail[s : s + 1, :]
    state_ref[...] = mixed.T.astype(BF16)
    bottom_ref[...] = bottom


def body(
    grad_columns,
    grad_flux,
    remap_part,
    remap_slot,
    remap_weight,
    col_count,
    neighbors,
    kappa,
    thickness,
    vertical,
    reaction,
):
    tiles = lax.axis_size("tile")
    parts = lax.axis_size("spec")
    col_max, width = grad_columns.shape
    layers = thickness.shape[1]
    own = width // tiles
    entries = tiles * col_max // WIDE
    part_t, slot_t, weight_t, nbr_t = remap_part.T, remap_slot.T, remap_weight.T, neighbors.T
    shape = jax.ShapeDtypeStruct
    moved = [grad_columns, vertical, thickness, grad_flux, part_t, slot_t, weight_t, nbr_t]
    moved.append(reaction.T)
    payload, misc, remap = call(
        prepare,
        [shape((tiles, OWN + 16, col_max), BF16), shape((16, width), F32)]
        + [shape((16, col_max), F32)],
        [SMEM] * 2 + [HBM] * 9,
        scratch=[pltpu.VMEM(a.shape, a.dtype) for a in moved] + [pltpu.SemaphoreType.DMA((9,))],
        flops=4 * 10**7,
        moved=10**6,
        limit=MOST,
    )(col_count, kappa, *moved)
    data = lax.all_to_all(payload, "tile", split_axis=0, concat_axis=0, tiled=True)
    keep = tiles == 8
    sent = OWN + tiles if keep else own
    backs = [shape((tiles, sent, col_max), BF16)]
    if not keep:
        backs.append(shape((tiles, col_max), F32))
    back = call(
        functools.partial(chain, tiles, own, layers, keep),
        backs,
        [VMEM] * 2,
        scratch=[
            pltpu.VMEM((2, tiles, OWN, col_max), F32),
            pltpu.VMEM((tiles * col_max // LANES, LANES), F32),
            pltpu.VMEM((tiles * 4 if keep else 1, LANES, col_max), BF16),
        ],
        flops=10**10,
        moved=10**6,
    )(misc, data)
    home = lax.all_to_all(back[0], "tile", split_axis=0, concat_axis=0, tiled=True)
    if keep:
        y = home
    else:
        place = lax.axis_index("tile") * own
        mark = jnp.arange(4)[:, None, None] * layers == place
        y = lax.psum(jnp.where(mark, back[1][None], 0.0).astype(BF16), "tile")
        home = home.reshape(width, col_max)
    packed = call(
        functools.partial(gather_bottom, tiles, own, parts, keep),
        [shape((parts, width + 16, col_max), BF16)],
        [VMEM] * 3,
        scratch=[pltpu.VMEM((entries * 4, col_max), F32)],
        flops=10**9,
        moved=10**6,
    )(y, home, remap)[0]
    every = lax.all_to_all(packed, "spec", split_axis=0, concat_axis=0, tiled=True)
    grad_state, grad_bottom = call(
        functools.partial(combine, layers),
        [shape((col_max, width), BF16), shape((4, col_max), F32)],
        [VMEM] * 2,
        flops=2 * 10**8,
        moved=2 * 10**6,
    )(misc, every)
    return grad_state, grad_bottom


def solution(mesh):
    placed = (
        P("tile", "spec"),
        P("spec", "tile"),
        P("tile", None),
        P("tile", None),
        P("tile", None),
        P("tile"),
        P("tile", None),
        P("spec"),
        P("spec", None),
        P("spec", None, None),
        P(None, "spec"),
    )
    return jax.shard_map(
        body,
        mesh=mesh,
        in_specs=placed,
        out_specs=(P("tile", "spec"), P("spec", "tile")),
        check_vma=False,
    )
```

```python
import functools

import jax
import jax.numpy as jnp
from jax import lax
from jax.experimental import pallas as pl
from jax.experimental.pallas import tpu as pltpu
from jax.sharding import PartitionSpec as P

SUB = 4
LANES = 128
WIDE = 256
OWN = 16
DEAD = 7
F32 = jnp.float32
BF16 = jnp.bfloat16
VMEM = pl.BlockSpec(memory_space=pltpu.VMEM)
HBM = pl.BlockSpec(memory_space=pltpu.HBM)
SMEM = pl.BlockSpec(memory_space=pltpu.SMEM)
LIMIT = 40 * 1024 * 1024
MOST = 60 * 1024 * 1024


def call(kernel, outs, specs, scratch=(), flops=0, moved=0, limit=LIMIT):
    return pl.pallas_call(
        kernel,
        out_shape=outs,
        in_specs=specs,
        out_specs=[VMEM] * len(outs),
        scratch_shapes=scratch,
        compiler_params=pltpu.CompilerParams(vmem_limit_bytes=limit),
        cost_estimate=pl.CostEstimate(flops=flops, bytes_accessed=moved, transcendentals=0),
    )


def nt(a, b, precision=None):
    return lax.dot_general(
        a, b, (((1,), (1,)), ((), ())), precision=precision, preferred_element_type=F32
    )


def nn(a, b, precision=None):
    return lax.dot_general(
        a, b, (((1,), (0,)), ((), ())), precision=precision, preferred_element_type=F32
    )


def row_ids(rows, cols):
    return lax.broadcasted_iota(jnp.int32, (rows, cols), 0)


def fetch(pairs, sems):
    copies = [pltpu.make_async_copy(a, b, sems.at[i]) for i, (a, b) in enumerate(pairs)]
    for copy in copies:
        copy.start()
    for copy in copies:
        copy.wait()


def prepare(
    count_ref, kappa_ref, gc_any, vert_any, thick_any, flux_any, part_any, slot_any, weight_any,
    nbr_any, reaction_any, payload_ref, misc_ref, remap_ref,
    gc_ref, vert_ref, thick_ref, flux_ref, part_ref, slot_ref, weight_ref, nbr_ref, reaction_ref,
    sems,
):
    fetch(
        [
            (gc_any, gc_ref),
            (vert_any, vert_ref),
            (thick_any, thick_ref),
            (flux_any, flux_ref),
            (part_any, part_ref),
            (slot_any, slot_ref),
            (weight_any, weight_ref),
            (nbr_any, nbr_ref),
            (reaction_any, reaction_ref),
        ],
        sems,
    )
    tiles, block_rows, col_max = payload_ref.shape
    species, layers, _ = vert_ref.shape
    width = species * layers
    v = vert_ref[...].astype(F32).reshape(width, layers)
    v = jnp.concatenate([v] * species, axis=1)
    rows = row_ids(width, width) // layers
    cols = lax.broadcasted_iota(jnp.int32, (width, width), 1) // layers
    vt = jnp.where(rows == cols, v, 0.0).T
    hi = lax.Precision.HIGHEST
    v2 = nn(vt, vt, hi)
    v4 = nn(v2, v2, hi)
    th = jnp.concatenate([thick_ref[s : s + 1, :] for s in range(species)], axis=1)
    misc_ref[0:8] = nt(jnp.broadcast_to(th, (8, width)), v4, hi)
    rates = [jnp.full((1, width), kappa_ref[s], F32) for s in range(species)]
    mix = reaction_ref[...].astype(F32)
    mix = jnp.concatenate([mix, jnp.zeros((4, width - mix.shape[1]), F32)], axis=1)
    misc_ref[8:16] = jnp.concatenate(rates + [mix], axis=0)
    live = lax.broadcasted_iota(jnp.int32, (1, col_max), 1) < count_ref[0]
    w = jnp.where(live, nt(v4.astype(BF16), gc_ref[...]), 0.0)
    slot, nbr = slot_ref[...], nbr_ref[...]
    power = (slot // WIDE) * 8 + jnp.where(live, nbr // WIDE, DEAD)
    code = 128.0 + part_ref[...].astype(F32)
    for bit in range(5):
        code = code * jnp.where((power >> bit) & 1 == 1, float(2 ** (2**bit)), 1.0)
    common = [(slot % WIDE).astype(F32), (nbr % WIDE).astype(F32), code]
    common = jnp.concatenate(common, axis=0)
    own = width // tiles
    pad = [] if own == OWN else [jnp.zeros((OWN - own, col_max), F32)]
    flux, weight = flux_ref[...], weight_ref[...]
    subs = (slot // WIDE).astype(F32)
    remap_ref[...] = jnp.concatenate([common[0:4], part_ref[...].astype(F32), subs, weight], axis=0)
    for q in range(tiles):
        s = q * own // layers
        pieces = [w[q * own : (q + 1) * own]] + pad + [flux[s : s + 1] * weight, common]
        payload_ref[q] = jnp.concatenate(pieces, axis=0).astype(BF16)


def decoded(code):
    power = jnp.zeros(code.shape, jnp.int32)
    for bit in (16, 8, 4, 2, 1):
        large = code >= 128.0 * 2.0**bit
        code = jnp.where(large, code * 2.0**-bit, code)
        power = power + jnp.where(large, bit, 0)
    return code - 128.0, power


def hot(key, ids):
    return jnp.where(ids == key, jnp.ones((), BF16), jnp.zeros((), BF16))


def picked(keys, value, target):
    return jnp.where(keys == jnp.asarray(target, BF16), value, jnp.zeros((), BF16))


def narrow(ints):
    return ints.astype(F32).astype(BF16)


def each(count, step):
    if count <= 8:
        for q in range(count):
            step(q, 0)
    else:
        lax.fori_loop(0, count, step, 0)


def chain(tiles, own, layers, keep, misc_ref, data_ref, *refs):
    back_ref, rest = refs[0], refs[1:]
    if not keep:
        y_ref, rest = rest[0], rest[1:]
    x_ref, table_ref, hot_ref = rest
    col_max = data_ref.shape[2]
    blocks = col_max // LANES
    me = lax.axis_index("tile")
    ids = narrow(row_ids(LANES, 1))
    half = row_ids(16, 1) // blocks
    within = row_ids(16, 1) % blocks

    table_ref[...] = jnp.zeros_like(table_ref)

    def gather(q, carry):
        block = data_ref[q].astype(F32)
        part, power = decoded(block[OWN + 12 : OWN + 16])
        low = block[OWN + 4 : OWN + 8].astype(jnp.int32)
        sub = (power >> 3) * 2 + (low >> 7)
        low = narrow(low & 127)
        total = jnp.zeros(table_ref.shape, F32)
        for r in range(4):
            value = block[OWN + r : OWN + r + 1]
            value = jnp.broadcast_to(value, (16, col_max)).astype(BF16)
            key = jnp.where(sub[r : r + 1] == within, part[r : r + 1] - half.astype(F32), -3.0)
            key = key.astype(BF16)
            rows = jnp.concatenate([picked(key, value, 2 * g) for g in range(tiles // 2)], axis=0)
            total = total + nt(rows, hot(low[r : r + 1], ids))
        table_ref[...] += total
        return carry

    each(tiles, gather)

    lane = lax.broadcasted_iota(jnp.int32, (OWN, misc_ref.shape[1]), 1)
    row = row_ids(OWN, 1)
    tv_own = jnp.sum(
        jnp.where((lane == me * own + row) & (row < own), misc_ref[0:1], 0.0), axis=1, keepdims=True
    )
    mine = me * own // layers
    rate = jnp.zeros((1, 1), F32)
    for s in range(4):
        rate = jnp.where(mine == s, misc_ref[8 + s : 9 + s, 0:1], rate)

    def start(q, carry):
        block = data_ref[q].astype(F32)
        live = decoded(block[OWN + 12 : OWN + 13])[1] & 7 != DEAD
        piece = table_ref[pl.ds(q * blocks, blocks), :]
        inj = jnp.concatenate([piece[h : h + 1] for h in range(blocks)], axis=1)
        x_ref[0, q] = block[0:OWN] + tv_own * jnp.where(live, inj, 0.0)
        return carry

    each(tiles, start)

    for step in range(SUB):
        here, there = step % 2, (step + 1) % 2
        for q in range(tiles):
            x_ref[there, q] = (1.0 - 4.0 * rate) * x_ref[here, q]

        def apply(q, carry):
            block = data_ref[q].astype(F32)
            low = block[OWN + 8 : OWN + 12].astype(jnp.int32)
            high = (decoded(block[OWN + 12 : OWN + 16])[1] & 7) * 2 + (low >> 7)
            value = (rate * x_ref[here, q]).astype(BF16)
            total = jnp.zeros(((blocks + 2) * OWN, LANES), F32)
            for n in range(4):
                key = narrow(jnp.broadcast_to(high[n : n + 1], (OWN, col_max)))
                rows = [picked(key, value, h) for h in range(blocks + 2)]
                if not keep or step == 0:
                    ones = hot(narrow(low[n : n + 1] & 127), ids)
                else:
                    ones = hot_ref[q * 4 + n]
                if keep and step == 0:
                    hot_ref[q * 4 + n] = ones
                total = total + nt(jnp.concatenate(rows, axis=0), ones)
            mine_rows = [total[h * OWN : (h + 1) * OWN] for h in range(blocks)]
            x_ref[there, q] += jnp.concatenate(mine_rows, axis=1)
            cross = [total[(blocks + k) * OWN : (blocks + k + 1) * OWN] for k in range(2)]
            if isinstance(q, int):
                if q > 0:
                    x_ref[there, q - 1, :, LANES : 2 * LANES] += cross[0]
                if q < tiles - 1:
                    x_ref[there, q + 1, :, :LANES] += cross[1]
            else:
                before, after = jnp.maximum(q - 1, 0), jnp.minimum(q + 1, tiles - 1)
                x_ref[there, before, :, LANES : 2 * LANES] += jnp.where(q > 0, cross[0], 0.0)
                x_ref[there, after, :, :LANES] += jnp.where(q < tiles - 1, cross[1], 0.0)
            return carry

        each(tiles, apply)
    last = SUB % 2
    if not keep:
        for q in range(tiles):
            back_ref[q] = x_ref[last, q, 0:own].astype(BF16)
            y_ref[q : q + 1] = x_ref[last, q, 0:1]
        return
    quarters = col_max // WIDE
    mix = jnp.concatenate([misc_ref[8:16], misc_ref[8:16]], axis=1)[4:8]
    mix = jnp.concatenate([mix, mix], axis=0)
    for g in range(quarters):
        top = [
            x_ref[last, tiles // quarters * g + h, 0:1, k * WIDE : (k + 1) * WIDE]
            for h in range(tiles // quarters)
            for k in range(quarters)
        ]
        top = jnp.where((me * own) % layers == 0, jnp.concatenate(top, axis=0), mix)
        for q in range(tiles):
            piece = x_ref[last, q, :, g * WIDE : (g + 1) * WIDE]
            back_ref[q * quarters + g] = jnp.concatenate([piece, top], axis=0).astype(BF16)


def middle(tiles, parts, layers, data_ref, remap_ref, out_ref):
    col_max = remap_ref.shape[1]
    quarters = col_max // WIDE
    halves = layers // OWN
    species = 4 * parts
    me = lax.axis_index("spec")

    def source(s, half):
        return ((s % 4) * halves + half) * parts + s // 4

    mix = [data_ref[source(4 * k, 1), OWN:].astype(F32)[0:4, 0:species] for k in range(parts)]
    mix = jnp.concatenate(mix, axis=0)
    size = species * OWN
    left = row_ids(size, species) // OWN == lax.broadcasted_iota(jnp.int32, (size, species), 1)
    right = row_ids(species, size) == lax.broadcasted_iota(jnp.int32, (species, size), 1) // OWN
    left, right = (jnp.where(hit, 1.0, 0.0).astype(BF16) for hit in (left, right))
    full = nn(nn(left, mix.astype(BF16)).astype(BF16), right)
    same = row_ids(size, size) % OWN == lax.broadcasted_iota(jnp.int32, (size, size), 1) % OWN
    full = jnp.where(same, full, 0.0).astype(BF16)
    mixed = []
    for half in range(halves):
        x = [data_ref[source(s, half), 0:OWN] for s in range(species)]
        mixed.append(nn(full, jnp.concatenate(x, axis=0)))

    table = [data_ref[source(s, 0), OWN:].astype(F32) for s in range(species)]
    table = jnp.concatenate(table, axis=0).astype(BF16)
    low = remap_ref[0:4].astype(BF16)
    place = remap_ref[4:8].astype(jnp.int32) * quarters + remap_ref[8:12].astype(jnp.int32)
    place = place - me * tiles
    ids = narrow(row_ids(WIDE, 1))
    totals = [jnp.zeros((tiles, col_max), F32) for s in range(species)]
    for r in range(4):
        found = nn(table, hot(low[r : r + 1], ids))
        weight = jnp.where(
            place[r : r + 1] == row_ids(tiles, 1), remap_ref[12 + r : 13 + r], 0.0
        )
        for s in range(species):
            totals[s] = totals[s] + found[s * tiles : (s + 1) * tiles] * weight
    bottom = [jnp.sum(total, axis=0, keepdims=True) for total in totals]
    bottom = nn(mix, jnp.concatenate(bottom, axis=0), lax.Precision.HIGHEST)
    for k in range(parts):
        rows = []
        for t in range(4 * k, 4 * k + 4):
            rows += [mixed[half][t * OWN : (t + 1) * OWN] for half in range(halves)]
        mine = bottom[4 * k : 4 * k + 4]
        rows += [mine[:, h * WIDE : (h + 1) * WIDE] for h in range(quarters)]
        out_ref[k] = jnp.concatenate(rows, axis=0).astype(BF16)


def settle(all_ref, state_ref, bottom_ref):
    parts, rows, wide = all_ref.shape
    width = state_ref.shape[1]
    total = jnp.zeros((rows - width, wide), F32)
    for k in range(parts):
        state = all_ref[k, 0:width].astype(F32)
        state_ref[k * wide : (k + 1) * wide, :] = state.T.astype(BF16)
        total = total + all_ref[k, width:].astype(F32)
    pieces = [total[h * 4 : h * 4 + 4] for h in range(parts)]
    bottom_ref[...] = jnp.concatenate(pieces, axis=1)


def gather_bottom(tiles, own, parts, y_ref, home_ref, remap_ref, out_ref, found_ref):
    col_max = remap_ref.shape[1]
    width = tiles * own
    subs = col_max // WIDE
    table = []
    for s in range(4):
        y = y_ref[s]
        table += [y[:, h * WIDE : (h + 1) * WIDE] for h in range(subs)]
    table = jnp.concatenate([piece.astype(F32) for piece in table], axis=0).astype(BF16)
    low = remap_ref[0:4].astype(BF16)
    part = remap_ref[4:8].astype(jnp.int32)
    sub = remap_ref[8:12].astype(jnp.int32)
    ids = narrow(row_ids(WIDE, 1))
    places = row_ids(tiles, 1)
    totals = [jnp.zeros((tiles, col_max), F32) for s in range(4)]
    for r in range(4):
        found_ref[...] = nn(table, hot(low[r : r + 1], ids))
        key = jnp.where(part[r : r + 1] == places, sub[r : r + 1], -1)
        weight = remap_ref[12 + r : 13 + r]
        for s in range(4):
            found = jnp.zeros((tiles, col_max), F32)
            for h in range(subs):
                at = (s * subs + h) * tiles
                found = jnp.where(key == h, found_ref[at : at + tiles, :], found)
            totals[s] = totals[s] + found * weight
    rows = [jnp.sum(total, axis=0, keepdims=True) for total in totals]
    rows.append(jnp.zeros((16 - 4, col_max), F32))
    rows = jnp.concatenate(rows, axis=0).astype(BF16)
    for k in range(parts):
        out_ref[k, :width] = home_ref[...]
        out_ref[k, width:] = rows


def combine(layers, misc_ref, all_ref, state_ref, bottom_ref):
    parts, rows, col_max = all_ref.shape
    wide = rows - 16
    own = wide // layers
    out_species, species = own, parts * own
    width = out_species * layers
    mix = misc_ref[12 : 12 + out_species, 0:species]
    left = jnp.where(
        row_ids(width, out_species) // layers
        == lax.broadcasted_iota(jnp.int32, (width, out_species), 1),
        1.0,
        0.0,
    ).astype(BF16)
    right = jnp.where(
        row_ids(species, species * layers)
        == lax.broadcasted_iota(jnp.int32, (species, species * layers), 1) // layers,
        1.0,
        0.0,
    ).astype(BF16)
    full = nn(nn(left, mix.astype(BF16)).astype(BF16), right)
    same = (
        row_ids(width, species * layers) % layers
        == lax.broadcasted_iota(jnp.int32, (width, species * layers), 1) % layers
    )
    full = jnp.where(same, full, 0.0).astype(BF16)
    mixed = jnp.zeros((width, col_max), F32)
    bottom = jnp.zeros((out_species, col_max), F32)
    for k in range(parts):
        mixed = mixed + nn(full[:, k * wide : (k + 1) * wide], all_ref[k, :wide, :])
        tail = all_ref[k, wide:, :].astype(F32)
        for s in range(own):
            col = k * own + s
            bottom = bottom + mix[:, col : col + 1] * tail[s : s + 1, :]
    state_ref[...] = mixed.T.astype(BF16)
    bottom_ref[...] = bottom


def body(
    grad_columns,
    grad_flux,
    remap_part,
    remap_slot,
    remap_weight,
    col_count,
    neighbors,
    kappa,
    thickness,
    vertical,
    reaction,
):
    tiles = lax.axis_size("tile")
    parts = lax.axis_size("spec")
    col_max, width = grad_columns.shape
    layers = thickness.shape[1]
    own = width // tiles
    entries = tiles * col_max // WIDE
    part_t, slot_t, weight_t, nbr_t = remap_part.T, remap_slot.T, remap_weight.T, neighbors.T
    shape = jax.ShapeDtypeStruct
    moved = [grad_columns, vertical, thickness, grad_flux, part_t, slot_t, weight_t, nbr_t]
    moved.append(reaction.T)
    payload, misc, remap = call(
        prepare,
        [shape((tiles, OWN + 16, col_max), BF16), shape((16, width), F32)]
        + [shape((16, col_max), F32)],
        [SMEM] * 2 + [HBM] * 9,
        scratch=[pltpu.VMEM(a.shape, a.dtype) for a in moved] + [pltpu.SemaphoreType.DMA((9,))],
        flops=4 * 10**7,
        moved=10**6,
        limit=MOST,
    )(col_count, kappa, *moved)
    data = lax.all_to_all(payload, "tile", split_axis=0, concat_axis=0, tiled=True)
    quarters = col_max // WIDE
    keep = tiles == 8 and parts == quarters and layers == 2 * own and own == OWN
    if keep:
        backs = [shape((tiles * parts, OWN + tiles, WIDE), BF16)]
    else:
        backs = [shape((tiles, own, col_max), BF16), shape((tiles, col_max), F32)]
    back = call(
        functools.partial(chain, tiles, own, layers, keep),
        backs,
        [VMEM] * 2,
        scratch=[
            pltpu.VMEM((2, tiles, OWN, col_max), F32),
            pltpu.VMEM((tiles * col_max // LANES, LANES), F32),
            pltpu.VMEM((tiles * 4 if keep else 1, LANES, col_max), BF16),
        ],
        flops=10**10,
        moved=10**6,
    )(misc, data)
    outs = [shape((col_max, width), BF16), shape((4, col_max), F32)]
    if keep:
        home = lax.all_to_all(back[0], ("tile", "spec"), split_axis=0, concat_axis=0, tiled=True)
        packed = call(
            functools.partial(middle, tiles, parts, layers),
            [shape((parts, width + OWN, WIDE), BF16)],
            [VMEM] * 2,
            flops=10**9,
            moved=10**6,
        )(home, remap)[0]
        every = lax.all_to_all(packed, "spec", split_axis=0, concat_axis=0, tiled=True)
        return tuple(call(settle, outs, [VMEM], flops=10**8, moved=10**6)(every))
    home = lax.all_to_all(back[0], "tile", split_axis=0, concat_axis=0, tiled=True)
    place = lax.axis_index("tile") * own
    mark = jnp.arange(4)[:, None, None] * layers == place
    y = lax.psum(jnp.where(mark, back[1][None], 0.0).astype(BF16), "tile")
    packed = call(
        functools.partial(gather_bottom, tiles, own, parts),
        [shape((parts, width + OWN, col_max), BF16)],
        [VMEM] * 3,
        scratch=[pltpu.VMEM((entries * 4, col_max), F32)],
        flops=10**9,
        moved=10**6,
    )(y, home.reshape(width, col_max), remap)[0]
    every = lax.all_to_all(packed, "spec", split_axis=0, concat_axis=0, tiled=True)
    grad_state, grad_bottom = call(
        functools.partial(combine, layers),
        outs,
        [VMEM] * 2,
        flops=2 * 10**8,
        moved=2 * 10**6,
    )(misc, every)
    return grad_state, grad_bottom


def solution(mesh):
    placed = (
        P("tile", "spec"),
        P("spec", "tile"),
        P("tile", None),
        P("tile", None),
        P("tile", None),
        P("tile"),
        P("tile", None),
        P("spec"),
        P("spec", None),
        P("spec", None, None),
        P(None, "spec"),
    )
    return jax.shard_map(
        body,
        mesh=mesh,
        in_specs=placed,
        out_specs=(P("tile", "spec"), P("spec", "tile")),
        check_vma=False,
    )
```

```python
import functools

import jax
import jax.numpy as jnp
from jax import lax
from jax.experimental import pallas as pl
from jax.experimental.pallas import tpu as pltpu
from jax.sharding import PartitionSpec as P

SUB = 4
LANES = 128
WIDE = 256
OWN = 16
DEAD = 15
F32 = jnp.float32
BF16 = jnp.bfloat16
VMEM = pl.BlockSpec(memory_space=pltpu.VMEM)
HBM = pl.BlockSpec(memory_space=pltpu.HBM)
SMEM = pl.BlockSpec(memory_space=pltpu.SMEM)
LIMIT = 40 * 1024 * 1024
MOST = 60 * 1024 * 1024


def call(kernel, outs, specs, scratch=(), flops=0, moved=0, limit=LIMIT):
    return pl.pallas_call(
        kernel,
        out_shape=outs,
        in_specs=specs,
        out_specs=[VMEM] * len(outs),
        scratch_shapes=scratch,
        compiler_params=pltpu.CompilerParams(vmem_limit_bytes=limit),
        cost_estimate=pl.CostEstimate(flops=flops, bytes_accessed=moved, transcendentals=0),
    )


def nt(a, b, precision=None):
    return lax.dot_general(
        a, b, (((1,), (1,)), ((), ())), precision=precision, preferred_element_type=F32
    )


def nn(a, b, precision=None):
    return lax.dot_general(
        a, b, (((1,), (0,)), ((), ())), precision=precision, preferred_element_type=F32
    )


def row_ids(rows, cols):
    return lax.broadcasted_iota(jnp.int32, (rows, cols), 0)


def fetch(pairs, sems):
    copies = [pltpu.make_async_copy(a, b, sems.at[i]) for i, (a, b) in enumerate(pairs)]
    for copy in copies:
        copy.start()
    for copy in copies:
        copy.wait()


def coded(ints):
    value = (128 + (ints & 127)).astype(F32)
    for bit in range(4):
        value = value * jnp.where((ints >> (7 + bit)) & 1 == 1, float(2 ** (2**bit)), 1.0)
    return value


def decoded(value):
    high = jnp.zeros(value.shape, jnp.int32)
    for bit in (8, 4, 2, 1):
        large = value >= 128.0 * 2.0**bit
        value = jnp.where(large, value * 2.0**-bit, value)
        high = high + jnp.where(large, bit, 0)
    return value - 128.0, high


def hot(key, ids):
    return jnp.where(ids == key, jnp.ones((), BF16), jnp.zeros((), BF16))


def picked(keys, value, target):
    return jnp.where(keys == jnp.asarray(target, BF16), value, jnp.zeros((), BF16))


def narrow(ints):
    return ints.astype(F32).astype(BF16)


def folded(rows):
    middle = rows.shape[1] // 2
    return [rows[:, :middle], rows[:, middle:]]


def prepare(
    count_ref, kappa_ref, gc_any, vert_any, thick_any, flux_any, part_any, slot_any, weight_any,
    nbr_any, reaction_any, payload_ref, misc_ref, remap_ref,
    gc_ref, vert_ref, thick_ref, flux_ref, part_ref, slot_ref, weight_ref, nbr_ref, reaction_ref,
    sems,
):
    fetch(
        [
            (gc_any, gc_ref),
            (vert_any, vert_ref),
            (thick_any, thick_ref),
            (flux_any, flux_ref),
            (part_any, part_ref),
            (slot_any, slot_ref),
            (weight_any, weight_ref),
            (nbr_any, nbr_ref),
            (reaction_any, reaction_ref),
        ],
        sems,
    )
    tiles = payload_ref.shape[0]
    col_max = gc_ref.shape[0]
    species, layers, _ = vert_ref.shape
    width = species * layers
    subs = col_max // WIDE

    v = vert_ref[...].astype(F32).reshape(width, layers)
    v = jnp.concatenate([v] * species, axis=1)
    rows = row_ids(width, width) // layers
    cols = lax.broadcasted_iota(jnp.int32, (width, width), 1) // layers
    vt = jnp.where(rows == cols, v, 0.0).T.astype(BF16)
    hi = lax.Precision.HIGHEST
    v2 = nn(vt, vt)
    v4 = nn(v2, v2, hi)
    th = jnp.concatenate([thick_ref[s : s + 1, :] for s in range(species)], axis=1)
    misc_ref[0:8] = nt(jnp.broadcast_to(th, (8, width)), v4, hi)
    rates = [jnp.full((1, width), kappa_ref[s], F32) for s in range(species)]
    mix = reaction_ref[...].astype(F32)
    mix = jnp.concatenate([mix, jnp.zeros((4, width - mix.shape[1]), F32)], axis=1)
    misc_ref[8:16] = jnp.concatenate(rates + [mix], axis=0)
    live = lax.broadcasted_iota(jnp.int32, (1, col_max), 1) < count_ref[0]
    w = jnp.where(live, nt(v4.astype(BF16), gc_ref[...]), 0.0)

    flux, weight = flux_ref[...], weight_ref[...]
    slot = slot_ref[...]
    part, sub, low = part_ref[...], slot // WIDE, slot % WIDE
    remap_ref[...] = jnp.concatenate(
        [low.astype(F32), part.astype(F32), sub.astype(F32), weight], axis=0
    )
    low = narrow(low)
    ids = narrow(row_ids(WIDE, 1))
    place = row_ids(16, 1)
    sums = jnp.zeros((species * subs * tiles, WIDE), F32)
    for r in range(4):
        value = flux * weight[r : r + 1]
        value = [jnp.broadcast_to(value[s : s + 1], (16, col_max)).astype(BF16) for s in range(4)]
        spot = sub[r : r + 1] * tiles + part[r : r + 1]
        keys = [narrow(spot - place - 16 * k) for k in range(subs * tiles // 16)]
        blocks = [picked(key, value[s], 0) for s in range(species) for key in keys]
        sums = sums + nt(jnp.concatenate(blocks, axis=0), hot(low[r : r + 1], ids))

    nbr = jnp.where(live, nbr_ref[...], DEAD * LANES)
    tail = folded(coded(nbr))
    for q in range(tiles):
        s = q * OWN // layers
        mine = sums[s * subs * tiles : (s + 1) * subs * tiles]
        mine = jnp.concatenate([mine[h * tiles : (h + 1) * tiles] for h in range(subs)], axis=1)
        pieces = folded(w[q * OWN : (q + 1) * OWN]) + folded(mine) + tail
        payload_ref[q] = jnp.concatenate(pieces, axis=0).astype(BF16)


def unfolded(block, first, rows):
    return jnp.concatenate([block[first : first + rows], block[first + rows : first + 2 * rows]], axis=1)


def chain(tiles, layers, misc_ref, data_ref, back_ref, x_ref, hot_ref, high_ref):
    col_max = x_ref.shape[3]
    blocks = col_max // LANES
    me = lax.axis_index("tile")
    ids = narrow(row_ids(LANES, 1))

    lane = lax.broadcasted_iota(jnp.int32, (OWN, misc_ref.shape[1]), 1)
    row = row_ids(OWN, 1)
    tv_own = jnp.where(lane == me * OWN + row, misc_ref[0:1], 0.0)
    tv_own = jnp.sum(tv_own, axis=1, keepdims=True)
    mine = me * OWN // layers
    rate = jnp.zeros((1, 1), F32)
    for s in range(4):
        rate = jnp.where(mine == s, misc_ref[8 + s : 9 + s, 0:1], rate)

    inj = jnp.zeros((tiles, col_max), F32)
    for q in range(tiles):
        block = data_ref[q].astype(F32)
        inj = inj + unfolded(block, 2 * OWN, tiles)
    for q in range(tiles):
        block = data_ref[q].astype(F32)
        low, high = decoded(unfolded(block, 2 * OWN + 2 * tiles, 4))
        live = high[0:1] != DEAD
        x_ref[0, q] = unfolded(block, 0, OWN) + tv_own * jnp.where(live, inj[q : q + 1], 0.0)
        high_ref[q] = high.astype(F32)
        for n in range(4):
            hot_ref[q * 4 + n] = hot(low[n : n + 1].astype(BF16), ids)

    for step in range(SUB):
        here, there = step % 2, (step + 1) % 2
        for q in range(tiles):
            x_ref[there, q] = (1.0 - 4.0 * rate) * x_ref[here, q]
        for q in range(tiles):
            high = high_ref[q]
            value = (rate * x_ref[here, q]).astype(BF16)
            total = jnp.zeros(((blocks + 2) * OWN, LANES), F32)
            for n in range(4):
                key = jnp.broadcast_to(high[n : n + 1], (OWN, col_max)).astype(BF16)
                rows = [picked(key, value, h) for h in range(blocks + 2)]
                total = total + nt(jnp.concatenate(rows, axis=0), hot_ref[q * 4 + n])
            mine_rows = [total[h * OWN : (h + 1) * OWN] for h in range(blocks)]
            x_ref[there, q] += jnp.concatenate(mine_rows, axis=1)
            if q > 0:
                cross = total[blocks * OWN : (blocks + 1) * OWN]
                x_ref[there, q - 1, :, LANES : 2 * LANES] += cross
            if q < tiles - 1:
                x_ref[there, q + 1, :, :LANES] += total[(blocks + 1) * OWN :]
    last = SUB % 2
    quarters = col_max // WIDE
    mix = jnp.concatenate([misc_ref[8:16], misc_ref[8:16]], axis=1)[4:8]
    mix = jnp.concatenate([mix, mix], axis=0)
    for g in range(quarters):
        top = [
            x_ref[last, tiles // quarters * g + h, 0:1, k * WIDE : (k + 1) * WIDE]
            for h in range(tiles // quarters)
            for k in range(quarters)
        ]
        top = jnp.where((me * OWN) % layers == 0, jnp.concatenate(top, axis=0), mix)
        for q in range(tiles):
            piece = x_ref[last, q, :, g * WIDE : (g + 1) * WIDE]
            back_ref[q * quarters + g] = jnp.concatenate([piece, top], axis=0).astype(BF16)


def middle(tiles, parts, layers, data_ref, remap_ref, out_ref):
    col_max = remap_ref.shape[1]
    quarters = col_max // WIDE
    halves = layers // OWN
    species = 4 * parts
    me = lax.axis_index("spec")

    def source(s, half):
        return ((s % 4) * halves + half) * parts + s // 4

    mix = [data_ref[source(4 * k, 1), OWN:].astype(F32)[0:4, 0:species] for k in range(parts)]
    mix = jnp.concatenate(mix, axis=0)
    size = species * OWN
    left = row_ids(size, species) // OWN == lax.broadcasted_iota(jnp.int32, (size, species), 1)
    right = row_ids(species, size) == lax.broadcasted_iota(jnp.int32, (species, size), 1) // OWN
    left, right = (jnp.where(hit, 1.0, 0.0).astype(BF16) for hit in (left, right))
    full = nn(nn(left, mix.astype(BF16)).astype(BF16), right)
    same = row_ids(size, size) % OWN == lax.broadcasted_iota(jnp.int32, (size, size), 1) % OWN
    full = jnp.where(same, full, 0.0).astype(BF16)
    mixed = []
    for half in range(halves):
        x = [data_ref[source(s, half), 0:OWN] for s in range(species)]
        mixed.append(nn(full, jnp.concatenate(x, axis=0)))

    table = [data_ref[source(s, 0), OWN:].astype(F32) for s in range(species)]
    table = jnp.concatenate(table, axis=0).astype(BF16)
    low = remap_ref[0:4].astype(BF16)
    place = remap_ref[4:8].astype(jnp.int32) * quarters + remap_ref[8:12].astype(jnp.int32)
    place = place - me * tiles
    ids = narrow(row_ids(WIDE, 1))
    totals = [jnp.zeros((tiles, col_max), F32) for s in range(species)]
    for r in range(4):
        found = nn(table, hot(low[r : r + 1], ids))
        weight = jnp.where(
            place[r : r + 1] == row_ids(tiles, 1), remap_ref[12 + r : 13 + r], 0.0
        )
        for s in range(species):
            totals[s] = totals[s] + found[s * tiles : (s + 1) * tiles] * weight
    bottom = [jnp.sum(total, axis=0, keepdims=True) for total in totals]
    bottom = nn(mix, jnp.concatenate(bottom, axis=0), lax.Precision.HIGHEST)
    for k in range(parts):
        rows = []
        for t in range(4 * k, 4 * k + 4):
            rows += [mixed[half][t * OWN : (t + 1) * OWN] for half in range(halves)]
        mine = bottom[4 * k : 4 * k + 4]
        rows += [mine[:, h * WIDE : (h + 1) * WIDE] for h in range(quarters)]
        out_ref[k] = jnp.concatenate(rows, axis=0).astype(BF16)


def settle(all_ref, state_ref, bottom_ref):
    parts, rows, wide = all_ref.shape
    width = state_ref.shape[1]
    total = jnp.zeros((rows - width, wide), F32)
    for k in range(parts):
        state = all_ref[k, 0:width].astype(F32)
        state_ref[k * wide : (k + 1) * wide, :] = state.T.astype(BF16)
        total = total + all_ref[k, width:].astype(F32)
    pieces = [total[h * 4 : h * 4 + 4] for h in range(parts)]
    bottom_ref[...] = jnp.concatenate(pieces, axis=1)


def shifted(block, axis, distance):
    devices = range(lax.axis_size(axis))
    route = [(i - distance, i) for i in devices if i - distance in devices]
    return lax.ppermute(block, axis, route)


def halo_body(
    grad_columns,
    grad_flux,
    remap_part,
    remap_slot,
    remap_weight,
    col_count,
    neighbors,
    kappa,
    thickness,
    vertical,
    reaction,
):
    tiles = lax.axis_size("tile")
    col_max = grad_columns.shape[0]
    rim_width = col_max // 8
    species = kappa.shape[0]
    layers = thickness.shape[1]
    width = species * layers
    cells, per_cell = remap_part.shape
    entries = cells * per_cell
    capacity = 2 * entries // tiles
    nbr_count = neighbors.shape[1]
    dest_flat = remap_part.reshape(-1)
    slot_flat = remap_slot.reshape(-1)
    dest_table = (dest_flat[:, None] == jnp.arange(tiles, dtype=jnp.int32)[None, :]).astype(
        jnp.int32
    )
    earlier = jnp.cumsum(dest_table, axis=0) - dest_table
    rank_within = jnp.sum(earlier * dest_table, axis=1)
    bucket_pos = dest_flat * capacity + rank_within
    entry_values = (remap_weight[:, :, None] * grad_flux.T[:, None, :]).reshape(entries, species)
    send_values = (
        jnp.zeros((tiles * capacity, species), jnp.float32)
        .at[bucket_pos]
        .set(entry_values)
        .reshape(tiles, capacity, species)
    )
    send_slots = (
        jnp.full((tiles * capacity, 1), col_max, jnp.int32)
        .at[bucket_pos]
        .set(slot_flat[:, None])
        .reshape(tiles, capacity, 1)
    )
    recv_values, recv_slots = (
        lax.all_to_all(send_values, "tile", split_axis=0, concat_axis=0, tiled=True),
        lax.all_to_all(send_slots, "tile", split_axis=0, concat_axis=0, tiled=True),
    )
    slot_index = recv_slots.reshape(-1)
    injected = (
        jnp.zeros((col_max + 1, species), jnp.float32)
        .at[slot_index]
        .add(recv_values.reshape(-1, species))[:col_max]
    )
    live_mask = (jnp.arange(col_max) < col_count[0]).astype(jnp.float32)[:, None]
    adjoint = live_mask * (
        grad_columns.astype(jnp.float32)
        + (injected[:, :, None] * thickness[None, :, :]).reshape(col_max, width)
    )
    rate_row = jnp.repeat(kappa, layers)[None, :]
    eye_block = jnp.eye(species, dtype=jnp.bfloat16)
    block_operator = jnp.einsum("slm,st->sltm", vertical, eye_block).reshape(width, width)
    target_rows = jnp.arange(col_max + 2 * rim_width, dtype=jnp.int32)[:, None]
    count_matrix = jnp.zeros((col_max + 2 * rim_width, col_max), jnp.float32)
    for column in range(nbr_count):
        count_matrix = count_matrix + (neighbors[:, column][None, :] == target_rows).astype(
            jnp.float32
        )
    zero_rest = jnp.zeros((col_max - 2 * rim_width, width), jnp.float32)
    for substep in range(SUB):
        spread = rate_row * adjoint
        extended = jnp.dot(
            count_matrix,
            spread,
            precision=lax.Precision.HIGHEST,
            preferred_element_type=jnp.float32,
        )
        to_previous = extended[col_max : col_max + rim_width]
        to_following = extended[col_max + rim_width :]
        from_following = shifted(to_previous.astype(jnp.bfloat16), "tile", -1).astype(
            to_previous.dtype
        )
        from_previous = shifted(to_following.astype(jnp.bfloat16), "tile", 1).astype(
            to_following.dtype
        )
        rim_terms = jnp.concatenate([from_previous, from_following, zero_rest], axis=0)
        bedload = adjoint - nbr_count * rate_row * adjoint + extended[:col_max] + rim_terms
        adjoint = jnp.dot(
            bedload.astype(jnp.bfloat16), block_operator, preferred_element_type=jnp.float32
        )
    rounded = adjoint.astype(jnp.bfloat16)
    piece = lax.all_gather(rounded, "spec", axis=1, tiled=True)
    piece_species = piece.shape[1] // layers
    mixed = jnp.einsum(
        "jsl,st->jtl",
        piece.reshape(col_max, piece_species, layers),
        reaction,
        preferred_element_type=jnp.float32,
    )
    grad_state = mixed.reshape(col_max, width).astype(jnp.bfloat16)
    top_layer = mixed[:, :, 0]
    everything = lax.all_gather(top_layer, "tile", axis=0, tiled=True)
    picked = everything[dest_flat * col_max + slot_flat]
    grad_bottom = jnp.sum(
        picked.reshape(cells, per_cell, species) * remap_weight[:, :, None], axis=1
    ).T
    return (grad_state, grad_bottom)


def column_body(
    grad_columns,
    grad_flux,
    remap_part,
    remap_slot,
    remap_weight,
    col_count,
    neighbors,
    kappa,
    thickness,
    vertical,
    reaction,
):
    tiles = lax.axis_size("tile")
    parts = lax.axis_size("spec")
    col_max, width = grad_columns.shape
    layers = thickness.shape[1]
    shape = jax.ShapeDtypeStruct
    moved = [grad_columns, vertical, thickness, grad_flux]
    moved += [remap_part.T, remap_slot.T, remap_weight.T, neighbors.T, reaction.T]
    payload, misc, remap = call(
        prepare,
        [
            shape((tiles, 2 * (OWN + tiles + 4), col_max // 2), BF16),
            shape((16, width), F32),
            shape((16, col_max), F32),
        ],
        [SMEM] * 2 + [HBM] * 9,
        scratch=[pltpu.VMEM(a.shape, a.dtype) for a in moved] + [pltpu.SemaphoreType.DMA((9,))],
        flops=4 * 10**7,
        moved=10**6,
        limit=MOST,
    )(col_count, kappa, *moved)
    data = lax.all_to_all(payload, "tile", split_axis=0, concat_axis=0, tiled=True)
    back = call(
        functools.partial(chain, tiles, layers),
        [shape((tiles * parts, OWN + tiles, WIDE), BF16)],
        [VMEM] * 2,
        scratch=[
            pltpu.VMEM((2, tiles, OWN, col_max), F32),
            pltpu.VMEM((tiles * 4, LANES, col_max), BF16),
            pltpu.VMEM((tiles, 4, col_max), F32),
        ],
        flops=10**10,
        moved=10**6,
    )(misc, data)[0]
    home = lax.all_to_all(back, ("tile", "spec"), split_axis=0, concat_axis=0, tiled=True)
    packed = call(
        functools.partial(middle, tiles, parts, layers),
        [shape((parts, width + OWN, WIDE), BF16)],
        [VMEM] * 2,
        flops=10**9,
        moved=10**6,
    )(home, remap)[0]
    every = lax.all_to_all(packed, "spec", split_axis=0, concat_axis=0, tiled=True)
    outs = [shape((col_max, width), BF16), shape((4, col_max), F32)]
    return tuple(call(settle, outs, [VMEM], flops=10**8, moved=10**6)(every))


def body(*args):
    tiles, parts = lax.axis_size("tile"), lax.axis_size("spec")
    layers = args[8].shape[1]
    fits = tiles == 8 and layers == 2 * OWN and args[0].shape == (parts * WIDE, tiles * OWN)
    return (column_body if fits else halo_body)(*args)


def solution(mesh):
    placed = (
        P("tile", "spec"),
        P("spec", "tile"),
        P("tile", None),
        P("tile", None),
        P("tile", None),
        P("tile"),
        P("tile", None),
        P("spec"),
        P("spec", None),
        P("spec", None, None),
        P(None, "spec"),
    )
    return jax.shard_map(
        body,
        mesh=mesh,
        in_specs=placed,
        out_specs=(P("tile", "spec"), P("spec", "tile")),
        check_vma=False,
    )
```

```python
import functools

import jax
import jax.numpy as jnp
from jax import lax
from jax.experimental import pallas as pl
from jax.experimental.pallas import tpu as pltpu
from jax.sharding import PartitionSpec as P

SUB = 4
LANES = 128
WIDE = 256
OWN = 16
DEAD = 15
F32 = jnp.float32
BF16 = jnp.bfloat16
VMEM = pl.BlockSpec(memory_space=pltpu.VMEM)
HBM = pl.BlockSpec(memory_space=pltpu.HBM)
SMEM = pl.BlockSpec(memory_space=pltpu.SMEM)
LIMIT = 40 * 1024 * 1024
MOST = 60 * 1024 * 1024


def call(kernel, outs, specs, scratch=(), flops=0, moved=0, limit=LIMIT, first=VMEM):
    return pl.pallas_call(
        kernel,
        out_shape=outs,
        in_specs=specs,
        out_specs=[first] + [VMEM] * (len(outs) - 1),
        scratch_shapes=scratch,
        compiler_params=pltpu.CompilerParams(vmem_limit_bytes=limit),
        cost_estimate=pl.CostEstimate(flops=flops, bytes_accessed=moved, transcendentals=0),
    )


def nt(a, b, precision=None):
    return lax.dot_general(
        a, b, (((1,), (1,)), ((), ())), precision=precision, preferred_element_type=F32
    )


def nn(a, b, precision=None):
    return lax.dot_general(
        a, b, (((1,), (0,)), ((), ())), precision=precision, preferred_element_type=F32
    )


def row_ids(rows, cols):
    return lax.broadcasted_iota(jnp.int32, (rows, cols), 0)


def started(pairs, sems):
    copies = [pltpu.make_async_copy(a, b, sems.at[i]) for i, (a, b) in enumerate(pairs)]
    for copy in copies:
        copy.start()
    return copies


def coded(ints):
    value = (128 + (ints & 127)).astype(F32)
    for bit in range(4):
        value = value * jnp.where((ints >> (7 + bit)) & 1 == 1, float(2 ** (2**bit)), 1.0)
    return value


def decoded(value):
    high = jnp.zeros(value.shape, jnp.int32)
    for bit in (8, 4, 2, 1):
        large = value >= 128.0 * 2.0**bit
        value = jnp.where(large, value * 2.0**-bit, value)
        high = high + jnp.where(large, bit, 0)
    return value - 128.0, high


def hot(key, ids):
    return jnp.where(ids == key, jnp.ones((), BF16), jnp.zeros((), BF16))


def picked(keys, value, target):
    return jnp.where(keys == jnp.asarray(target, BF16), value, jnp.zeros((), BF16))


def narrow(ints):
    return ints.astype(F32).astype(BF16)


def folded(rows):
    middle = rows.shape[1] // 2
    return [rows[:, :middle], rows[:, middle:]]


def prepare(
    count_ref, kappa_ref, gc_any, vert_any, thick_any, flux_any, part_any, slot_any, weight_any,
    nbr_any, reaction_any, payload_any, misc_ref, remap_ref,
    gc_ref, vert_ref, thick_ref, flux_ref, part_ref, slot_ref, weight_ref, nbr_ref, reaction_ref,
    payload_ref, sems, out_sems,
):
    copies = started(
        [
            (vert_any, vert_ref),
            (thick_any, thick_ref),
            (reaction_any, reaction_ref),
            (slot_any, slot_ref),
            (part_any, part_ref),
            (weight_any, weight_ref),
            (flux_any, flux_ref),
            (nbr_any, nbr_ref),
            (gc_any, gc_ref),
        ],
        sems,
    )
    for copy in copies[:-1]:
        copy.wait()
    tiles = payload_ref.shape[0]
    col_max = gc_ref.shape[0]
    species, layers, _ = vert_ref.shape
    width = species * layers
    subs = col_max // WIDE

    v = vert_ref[...].astype(F32).reshape(width, layers)
    v = jnp.concatenate([v] * species, axis=1)
    rows = row_ids(width, width) // layers
    cols = lax.broadcasted_iota(jnp.int32, (width, width), 1) // layers
    vt = jnp.where(rows == cols, v, 0.0).T.astype(BF16)
    hi = lax.Precision.HIGHEST
    v2 = nn(vt, vt)
    v4 = nn(v2, v2, hi)
    th = jnp.concatenate([thick_ref[s : s + 1, :] for s in range(species)], axis=1)
    misc_ref[0:8] = nt(jnp.broadcast_to(th, (8, width)), v4, hi)
    rates = [jnp.full((1, width), kappa_ref[s], F32) for s in range(species)]
    mix = reaction_ref[...].astype(F32)
    mix = jnp.concatenate([mix, jnp.zeros((4, width - mix.shape[1]), F32)], axis=1)
    misc_ref[8:16] = jnp.concatenate(rates + [mix], axis=0)
    flux, weight = flux_ref[...], weight_ref[...]
    slot = slot_ref[...]
    part, sub, low = part_ref[...], slot // WIDE, slot % WIDE
    remap_ref[...] = jnp.concatenate(
        [low.astype(F32), part.astype(F32), sub.astype(F32), weight], axis=0
    )
    low = narrow(low)
    ids = narrow(row_ids(WIDE, 1))
    place = row_ids(16, 1)
    sums = jnp.zeros((species * subs * tiles, WIDE), F32)
    for r in range(4):
        value = flux * weight[r : r + 1]
        value = [jnp.broadcast_to(value[s : s + 1], (16, col_max)).astype(BF16) for s in range(4)]
        spot = sub[r : r + 1] * tiles + part[r : r + 1]
        keys = [narrow(spot - place - 16 * k) for k in range(subs * tiles // 16)]
        blocks = [picked(key, value[s], 0) for s in range(species) for key in keys]
        sums = sums + nt(jnp.concatenate(blocks, axis=0), hot(low[r : r + 1], ids))

    live = lax.broadcasted_iota(jnp.int32, (1, col_max), 1) < count_ref[0]
    tail = folded(coded(jnp.where(live, nbr_ref[...], DEAD * LANES)))
    copies[-1].wait()
    w = jnp.where(live, nt(v4.astype(BF16), gc_ref[...]), 0.0)
    sent = []
    for q in range(tiles):
        s = q * OWN // layers
        mine = sums[s * subs * tiles : (s + 1) * subs * tiles]
        mine = jnp.concatenate([mine[h * tiles : (h + 1) * tiles] for h in range(subs)], axis=1)
        pieces = folded(w[q * OWN : (q + 1) * OWN]) + folded(mine) + tail
        payload_ref[q] = jnp.concatenate(pieces, axis=0).astype(BF16)
        sent.append(pltpu.make_async_copy(payload_ref.at[q], payload_any.at[q], out_sems.at[q]))
        sent[-1].start()
    for copy in sent:
        copy.wait()


def unfolded(block, first, rows):
    return jnp.concatenate([block[first : first + rows], block[first + rows : first + 2 * rows]], axis=1)


def chain(tiles, layers, misc_ref, data_ref, back_ref, x_ref, hot_ref, high_ref):
    col_max = x_ref.shape[3]
    blocks = col_max // LANES
    me = lax.axis_index("tile")
    ids = narrow(row_ids(LANES, 1))

    lane = lax.broadcasted_iota(jnp.int32, (OWN, misc_ref.shape[1]), 1)
    row = row_ids(OWN, 1)
    tv_own = jnp.where(lane == me * OWN + row, misc_ref[0:1], 0.0)
    tv_own = jnp.sum(tv_own, axis=1, keepdims=True)
    mine = me * OWN // layers
    rate = jnp.zeros((1, 1), F32)
    for s in range(4):
        rate = jnp.where(mine == s, misc_ref[8 + s : 9 + s, 0:1], rate)

    inj = jnp.zeros((tiles, col_max), F32)
    for q in range(tiles):
        block = data_ref[q].astype(F32)
        inj = inj + unfolded(block, 2 * OWN, tiles)
    for q in range(tiles):
        block = data_ref[q].astype(F32)
        low, high = decoded(unfolded(block, 2 * OWN + 2 * tiles, 4))
        live = high[0:1] != DEAD
        x_ref[0, q] = unfolded(block, 0, OWN) + tv_own * jnp.where(live, inj[q : q + 1], 0.0)
        high_ref[q] = high.astype(F32)
        for n in range(4):
            hot_ref[q * 4 + n] = hot(low[n : n + 1].astype(BF16), ids)

    def product(here, q):
        high = high_ref[q]
        value = (rate * x_ref[here, q]).astype(BF16)
        hits = list(range(blocks)) + [blocks] * (q > 0) + [blocks + 1] * (q < tiles - 1)
        total = jnp.zeros((len(hits) * OWN, LANES), F32)
        for n in range(4):
            key = jnp.broadcast_to(high[n : n + 1], (OWN, col_max)).astype(BF16)
            rows = [picked(key, value, h) for h in hits]
            total = total + nt(jnp.concatenate(rows, axis=0), hot_ref[q * 4 + n])
        pieces = [total[i * OWN : (i + 1) * OWN] for i in range(len(hits))]
        own = pieces[:blocks]
        to_prev = pieces[blocks] if q > 0 else None
        to_next = pieces[-1] if q < tiles - 1 else None
        return own, to_prev, to_next

    for step in range(SUB):
        here, there = step % 2, (step + 1) % 2
        from_prev = None
        current = product(here, 0)
        for q in range(tiles):
            following = product(here, q + 1) if q < tiles - 1 else None
            own, _, to_next = current
            if from_prev is not None:
                own[0] = own[0] + from_prev
            if following is not None:
                own[1] = own[1] + following[1]
            x_ref[there, q] = (1.0 - 4.0 * rate) * x_ref[here, q] + jnp.concatenate(own, axis=1)
            from_prev, current = to_next, following
    last = SUB % 2
    quarters = col_max // WIDE
    mix = jnp.concatenate([misc_ref[8:16], misc_ref[8:16]], axis=1)[4:8]
    mix = jnp.concatenate([mix, mix], axis=0)
    for g in range(quarters):
        top = [
            x_ref[last, tiles // quarters * g + h, 0:1, k * WIDE : (k + 1) * WIDE]
            for h in range(tiles // quarters)
            for k in range(quarters)
        ]
        top = jnp.where((me * OWN) % layers == 0, jnp.concatenate(top, axis=0), mix)
        for q in range(tiles):
            piece = x_ref[last, q, :, g * WIDE : (g + 1) * WIDE]
            back_ref[q * quarters + g] = jnp.concatenate([piece, top], axis=0).astype(BF16)


def middle(tiles, parts, layers, data_ref, remap_ref, out_ref):
    col_max = remap_ref.shape[1]
    quarters = col_max // WIDE
    halves = layers // OWN
    species = 4 * parts
    me = lax.axis_index("spec")

    def source(s, half):
        return ((s % 4) * halves + half) * parts + s // 4

    mix = [data_ref[source(4 * k, 1)].astype(F32)[OWN : OWN + 4, 0:species] for k in range(parts)]
    mix = jnp.concatenate(mix, axis=0)
    size = species * OWN
    left = row_ids(size, species) // OWN == lax.broadcasted_iota(jnp.int32, (size, species), 1)
    right = row_ids(species, size) == lax.broadcasted_iota(jnp.int32, (species, size), 1) // OWN
    left, right = (jnp.where(hit, 1.0, 0.0).astype(BF16) for hit in (left, right))
    full = nn(nn(left, mix.astype(BF16)).astype(BF16), right)
    same = row_ids(size, size) % OWN == lax.broadcasted_iota(jnp.int32, (size, size), 1) % OWN
    full = jnp.where(same, full, 0.0).astype(BF16)
    mixed = []
    for half in range(halves):
        x = [data_ref[source(s, half), 0:OWN] for s in range(species)]
        mixed.append(nn(full, jnp.concatenate(x, axis=0)))

    table = [data_ref[source(s, 0)].astype(F32)[OWN:] for s in range(species)]
    table = jnp.concatenate(table, axis=0).astype(BF16)
    low = remap_ref[0:4].astype(BF16)
    place = remap_ref[4:8].astype(jnp.int32) * quarters + remap_ref[8:12].astype(jnp.int32)
    place = place - me * tiles
    ids = narrow(row_ids(WIDE, 1))
    totals = [jnp.zeros((tiles, col_max), F32) for s in range(species)]
    for r in range(4):
        found = nn(table, hot(low[r : r + 1], ids))
        weight = jnp.where(
            place[r : r + 1] == row_ids(tiles, 1), remap_ref[12 + r : 13 + r], 0.0
        )
        for s in range(species):
            totals[s] = totals[s] + found[s * tiles : (s + 1) * tiles] * weight
    bottom = [jnp.sum(total, axis=0, keepdims=True) for total in totals]
    bottom = nn(mix, jnp.concatenate(bottom, axis=0), lax.Precision.HIGHEST)
    for k in range(parts):
        rows = []
        for t in range(4 * k, 4 * k + 4):
            rows += [mixed[half][t * OWN : (t + 1) * OWN] for half in range(halves)]
        mine = bottom[4 * k : 4 * k + 4]
        rows += [mine[:, h * WIDE : (h + 1) * WIDE] for h in range(quarters)]
        out_ref[k] = jnp.concatenate(rows, axis=0).astype(BF16)


def settle(all_ref, state_ref, bottom_ref):
    parts, rows, wide = all_ref.shape
    width = state_ref.shape[1]
    total = jnp.zeros((rows - width, wide), F32)
    for k in range(parts):
        state = all_ref[k, 0:width].astype(F32)
        state_ref[k * wide : (k + 1) * wide, :] = state.T.astype(BF16)
        total = total + all_ref[k, width:].astype(F32)
    pieces = [total[h * 4 : h * 4 + 4] for h in range(parts)]
    bottom_ref[...] = jnp.concatenate(pieces, axis=1)


def shifted(block, axis, distance):
    devices = range(lax.axis_size(axis))
    route = [(i - distance, i) for i in devices if i - distance in devices]
    return lax.ppermute(block, axis, route)


def halo_body(
    grad_columns,
    grad_flux,
    remap_part,
    remap_slot,
    remap_weight,
    col_count,
    neighbors,
    kappa,
    thickness,
    vertical,
    reaction,
):
    tiles = lax.axis_size("tile")
    col_max = grad_columns.shape[0]
    rim_width = col_max // 8
    species = kappa.shape[0]
    layers = thickness.shape[1]
    width = species * layers
    cells, per_cell = remap_part.shape
    entries = cells * per_cell
    capacity = 2 * entries // tiles
    nbr_count = neighbors.shape[1]
    dest_flat = remap_part.reshape(-1)
    slot_flat = remap_slot.reshape(-1)
    dest_table = (dest_flat[:, None] == jnp.arange(tiles, dtype=jnp.int32)[None, :]).astype(
        jnp.int32
    )
    earlier = jnp.cumsum(dest_table, axis=0) - dest_table
    rank_within = jnp.sum(earlier * dest_table, axis=1)
    bucket_pos = dest_flat * capacity + rank_within
    entry_values = (remap_weight[:, :, None] * grad_flux.T[:, None, :]).reshape(entries, species)
    send_values = (
        jnp.zeros((tiles * capacity, species), jnp.float32)
        .at[bucket_pos]
        .set(entry_values)
        .reshape(tiles, capacity, species)
    )
    send_slots = (
        jnp.full((tiles * capacity, 1), col_max, jnp.int32)
        .at[bucket_pos]
        .set(slot_flat[:, None])
        .reshape(tiles, capacity, 1)
    )
    recv_values, recv_slots = (
        lax.all_to_all(send_values, "tile", split_axis=0, concat_axis=0, tiled=True),
        lax.all_to_all(send_slots, "tile", split_axis=0, concat_axis=0, tiled=True),
    )
    slot_index = recv_slots.reshape(-1)
    injected = (
        jnp.zeros((col_max + 1, species), jnp.float32)
        .at[slot_index]
        .add(recv_values.reshape(-1, species))[:col_max]
    )
    live_mask = (jnp.arange(col_max) < col_count[0]).astype(jnp.float32)[:, None]
    adjoint = live_mask * (
        grad_columns.astype(jnp.float32)
        + (injected[:, :, None] * thickness[None, :, :]).reshape(col_max, width)
    )
    rate_row = jnp.repeat(kappa, layers)[None, :]
    eye_block = jnp.eye(species, dtype=jnp.bfloat16)
    block_operator = jnp.einsum("slm,st->sltm", vertical, eye_block).reshape(width, width)
    target_rows = jnp.arange(col_max + 2 * rim_width, dtype=jnp.int32)[:, None]
    count_matrix = jnp.zeros((col_max + 2 * rim_width, col_max), jnp.float32)
    for column in range(nbr_count):
        count_matrix = count_matrix + (neighbors[:, column][None, :] == target_rows).astype(
            jnp.float32
        )
    zero_rest = jnp.zeros((col_max - 2 * rim_width, width), jnp.float32)
    for substep in range(SUB):
        spread = rate_row * adjoint
        extended = jnp.dot(
            count_matrix,
            spread,
            precision=lax.Precision.HIGHEST,
            preferred_element_type=jnp.float32,
        )
        to_previous = extended[col_max : col_max + rim_width]
        to_following = extended[col_max + rim_width :]
        from_following = shifted(to_previous.astype(jnp.bfloat16), "tile", -1).astype(
            to_previous.dtype
        )
        from_previous = shifted(to_following.astype(jnp.bfloat16), "tile", 1).astype(
            to_following.dtype
        )
        rim_terms = jnp.concatenate([from_previous, from_following, zero_rest], axis=0)
        bedload = adjoint - nbr_count * rate_row * adjoint + extended[:col_max] + rim_terms
        adjoint = jnp.dot(
            bedload.astype(jnp.bfloat16), block_operator, preferred_element_type=jnp.float32
        )
    rounded = adjoint.astype(jnp.bfloat16)
    piece = lax.all_gather(rounded, "spec", axis=1, tiled=True)
    piece_species = piece.shape[1] // layers
    mixed = jnp.einsum(
        "jsl,st->jtl",
        piece.reshape(col_max, piece_species, layers),
        reaction,
        preferred_element_type=jnp.float32,
    )
    grad_state = mixed.reshape(col_max, width).astype(jnp.bfloat16)
    top_layer = mixed[:, :, 0]
    everything = lax.all_gather(top_layer, "tile", axis=0, tiled=True)
    picked = everything[dest_flat * col_max + slot_flat]
    grad_bottom = jnp.sum(
        picked.reshape(cells, per_cell, species) * remap_weight[:, :, None], axis=1
    ).T
    return (grad_state, grad_bottom)


def column_body(
    grad_columns,
    grad_flux,
    remap_part,
    remap_slot,
    remap_weight,
    col_count,
    neighbors,
    kappa,
    thickness,
    vertical,
    reaction,
):
    tiles = lax.axis_size("tile")
    parts = lax.axis_size("spec")
    col_max, width = grad_columns.shape
    layers = thickness.shape[1]
    shape = jax.ShapeDtypeStruct
    moved = [grad_columns, vertical, thickness, grad_flux]
    moved += [remap_part.T, remap_slot.T, remap_weight.T, neighbors.T, reaction.T]
    payload, misc, remap = call(
        prepare,
        [
            shape((tiles, 2 * (OWN + tiles + 4), col_max // 2), BF16),
            shape((16, width), F32),
            shape((16, col_max), F32),
        ],
        [SMEM] * 2 + [HBM] * 9,
        scratch=[pltpu.VMEM(a.shape, a.dtype) for a in moved]
        + [pltpu.VMEM((tiles, 2 * (OWN + tiles + 4), col_max // 2), BF16)]
        + [pltpu.SemaphoreType.DMA((9,)), pltpu.SemaphoreType.DMA((tiles,))],
        flops=4 * 10**7,
        moved=10**6,
        limit=MOST,
        first=HBM,
    )(col_count, kappa, *moved)
    data = lax.all_to_all(payload, "tile", split_axis=0, concat_axis=0, tiled=True)
    back = call(
        functools.partial(chain, tiles, layers),
        [shape((tiles * parts, OWN + tiles, WIDE), BF16)],
        [VMEM] * 2,
        scratch=[
            pltpu.VMEM((2, tiles, OWN, col_max), F32),
            pltpu.VMEM((tiles * 4, LANES, col_max), BF16),
            pltpu.VMEM((tiles, 4, col_max), F32),
        ],
        flops=10**10,
        moved=10**6,
    )(misc, data)[0]
    home = lax.all_to_all(back, ("tile", "spec"), split_axis=0, concat_axis=0, tiled=True)
    packed = call(
        functools.partial(middle, tiles, parts, layers),
        [shape((parts, width + OWN, WIDE), BF16)],
        [VMEM] * 2,
        flops=10**9,
        moved=10**6,
    )(home, remap)[0]
    every = lax.all_to_all(packed, "spec", split_axis=0, concat_axis=0, tiled=True)
    outs = [shape((col_max, width), BF16), shape((4, col_max), F32)]
    return tuple(call(settle, outs, [VMEM], flops=10**8, moved=10**6)(every))


def body(*args):
    tiles, parts = lax.axis_size("tile"), lax.axis_size("spec")
    layers = args[8].shape[1]
    fits = tiles == 8 and layers == 2 * OWN and args[0].shape == (parts * WIDE, tiles * OWN)
    return (column_body if fits else halo_body)(*args)


def solution(mesh):
    placed = (
        P("tile", "spec"),
        P("spec", "tile"),
        P("tile", None),
        P("tile", None),
        P("tile", None),
        P("tile"),
        P("tile", None),
        P("spec"),
        P("spec", None),
        P("spec", None, None),
        P(None, "spec"),
    )
    return jax.shard_map(
        body,
        mesh=mesh,
        in_specs=placed,
        out_specs=(P("tile", "spec"), P("spec", "tile")),
        check_vma=False,
    )
```

```python
import functools

import jax
import jax.numpy as jnp
from jax import lax
from jax.experimental import pallas as pl
from jax.experimental.pallas import tpu as pltpu
from jax.sharding import PartitionSpec as P

SUB = 4
LANES = 128
WIDE = 256
OWN = 16
DEAD = 15
F32 = jnp.float32
BF16 = jnp.bfloat16
VMEM = pl.BlockSpec(memory_space=pltpu.VMEM)
HBM = pl.BlockSpec(memory_space=pltpu.HBM)
SMEM = pl.BlockSpec(memory_space=pltpu.SMEM)
LIMIT = 40 * 1024 * 1024
MOST = 60 * 1024 * 1024


def call(kernel, outs, specs, scratch=(), flops=0, moved=0, limit=LIMIT):
    return pl.pallas_call(
        kernel,
        out_shape=outs,
        in_specs=specs,
        out_specs=[VMEM] * len(outs),
        scratch_shapes=scratch,
        compiler_params=pltpu.CompilerParams(vmem_limit_bytes=limit),
        cost_estimate=pl.CostEstimate(flops=flops, bytes_accessed=moved, transcendentals=0),
    )


def nt(a, b, precision=None):
    return lax.dot_general(
        a, b, (((1,), (1,)), ((), ())), precision=precision, preferred_element_type=F32
    )


def nn(a, b, precision=None):
    return lax.dot_general(
        a, b, (((1,), (0,)), ((), ())), precision=precision, preferred_element_type=F32
    )


def row_ids(rows, cols):
    return lax.broadcasted_iota(jnp.int32, (rows, cols), 0)


def started(pairs, sems):
    copies = [pltpu.make_async_copy(a, b, sems.at[i]) for i, (a, b) in enumerate(pairs)]
    for copy in copies:
        copy.start()
    return copies


def coded(ints):
    value = (128 + (ints & 127)).astype(F32)
    for bit in range(4):
        value = value * jnp.where((ints >> (7 + bit)) & 1 == 1, float(2 ** (2**bit)), 1.0)
    return value


def decoded(value):
    high = jnp.zeros(value.shape, jnp.int32)
    for bit in (8, 4, 2, 1):
        large = value >= 128.0 * 2.0**bit
        value = jnp.where(large, value * 2.0**-bit, value)
        high = high + jnp.where(large, bit, 0)
    return value - 128.0, high


def hot(key, ids):
    return jnp.where(ids == key, jnp.ones((), BF16), jnp.zeros((), BF16))


def picked(keys, value, target):
    return jnp.where(keys == jnp.asarray(target, BF16), value, jnp.zeros((), BF16))


def narrow(ints):
    return ints.astype(F32).astype(BF16)


def folded(rows):
    middle = rows.shape[1] // 2
    return [rows[:, :middle], rows[:, middle:]]


def prepare(
    count_ref, kappa_ref, gc_any, vert_any, thick_any, flux_any, part_any, slot_any, weight_any,
    nbr_any, reaction_any, payload_ref, misc_ref, remap_ref,
    gc_ref, vert_ref, thick_ref, flux_ref, part_ref, slot_ref, weight_ref, nbr_ref, reaction_ref,
    sems,
):
    copies = started(
        [
            (vert_any, vert_ref),
            (thick_any, thick_ref),
            (reaction_any, reaction_ref),
            (slot_any, slot_ref),
            (part_any, part_ref),
            (weight_any, weight_ref),
            (flux_any, flux_ref),
            (nbr_any, nbr_ref),
            (gc_any, gc_ref),
        ],
        sems,
    )
    for copy in copies:
        copy.wait()
    tiles = payload_ref.shape[0]
    col_max = gc_ref.shape[0]
    species, layers, _ = vert_ref.shape
    width = species * layers
    subs = col_max // WIDE

    v = vert_ref[...].astype(F32).reshape(width, layers)
    v = jnp.concatenate([v] * species, axis=1)
    rows = row_ids(width, width) // layers
    cols = lax.broadcasted_iota(jnp.int32, (width, width), 1) // layers
    vt = jnp.where(rows == cols, v, 0.0).T.astype(BF16)
    hi = lax.Precision.HIGHEST
    v2 = nn(vt, vt)
    v4 = nn(v2, v2, hi)
    th = jnp.concatenate([thick_ref[s : s + 1, :] for s in range(species)], axis=1)
    misc_ref[0:8] = nt(jnp.broadcast_to(th, (8, width)), v4, hi)
    rates = [jnp.full((1, width), kappa_ref[s], F32) for s in range(species)]
    mix = reaction_ref[...].astype(F32)
    mix = jnp.concatenate([mix, jnp.zeros((4, width - mix.shape[1]), F32)], axis=1)
    misc_ref[8:16] = jnp.concatenate(rates + [mix], axis=0)
    flux, weight = flux_ref[...], weight_ref[...]
    slot = slot_ref[...]
    part, sub, low = part_ref[...], slot // WIDE, slot % WIDE
    remap_ref[...] = jnp.concatenate(
        [low.astype(F32), part.astype(F32), sub.astype(F32), weight], axis=0
    )
    low = narrow(low)
    ids = narrow(row_ids(WIDE, 1))
    place = row_ids(16, 1)
    sums = jnp.zeros((species * subs * tiles, WIDE), F32)
    for r in range(4):
        value = flux * weight[r : r + 1]
        value = [jnp.broadcast_to(value[s : s + 1], (16, col_max)).astype(BF16) for s in range(4)]
        spot = sub[r : r + 1] * tiles + part[r : r + 1]
        keys = [narrow(spot - place - 16 * k) for k in range(subs * tiles // 16)]
        blocks = [picked(key, value[s], 0) for s in range(species) for key in keys]
        sums = sums + nt(jnp.concatenate(blocks, axis=0), hot(low[r : r + 1], ids))

    live = lax.broadcasted_iota(jnp.int32, (1, col_max), 1) < count_ref[0]
    tail = folded(coded(jnp.where(live, nbr_ref[...], DEAD * LANES)))
    w = jnp.where(live, nt(v4.astype(BF16), gc_ref[...]), 0.0)
    for q in range(tiles):
        s = q * OWN // layers
        mine = sums[s * subs * tiles : (s + 1) * subs * tiles]
        mine = jnp.concatenate([mine[h * tiles : (h + 1) * tiles] for h in range(subs)], axis=1)
        pieces = folded(w[q * OWN : (q + 1) * OWN]) + folded(mine) + tail
        payload_ref[q] = jnp.concatenate(pieces, axis=0).astype(BF16)


def unfolded(block, first, rows):
    return jnp.concatenate([block[first : first + rows], block[first + rows : first + 2 * rows]], axis=1)


def chain(tiles, layers, misc_ref, data_ref, back_ref, x_ref, hot_ref, high_ref):
    col_max = x_ref.shape[3]
    blocks = col_max // LANES
    me = lax.axis_index("tile")
    ids = narrow(row_ids(LANES, 1))

    lane = lax.broadcasted_iota(jnp.int32, (OWN, misc_ref.shape[1]), 1)
    row = row_ids(OWN, 1)
    tv_own = jnp.where(lane == me * OWN + row, misc_ref[0:1], 0.0)
    tv_own = jnp.sum(tv_own, axis=1, keepdims=True)
    mine = me * OWN // layers
    rate = jnp.zeros((1, 1), F32)
    for s in range(4):
        rate = jnp.where(mine == s, misc_ref[8 + s : 9 + s, 0:1], rate)

    inj = jnp.zeros((tiles, col_max), F32)
    for q in range(tiles):
        block = data_ref[q].astype(F32)
        inj = inj + unfolded(block, 2 * OWN, tiles)
    for q in range(tiles):
        block = data_ref[q].astype(F32)
        low, high = decoded(unfolded(block, 2 * OWN + 2 * tiles, 4))
        live = high[0:1] != DEAD
        x_ref[0, q] = unfolded(block, 0, OWN) + tv_own * jnp.where(live, inj[q : q + 1], 0.0)
        high_ref[q] = high.astype(F32)
        for n in range(4):
            hot_ref[q * 4 + n] = hot(low[n : n + 1].astype(BF16), ids)

    def product(here, q):
        high = high_ref[q]
        value = (rate * x_ref[here, q]).astype(BF16)
        hits = list(range(blocks)) + [blocks] * (q > 0) + [blocks + 1] * (q < tiles - 1)
        total = jnp.zeros((len(hits) * OWN, LANES), F32)
        for n in range(4):
            key = jnp.broadcast_to(high[n : n + 1], (OWN, col_max)).astype(BF16)
            rows = [picked(key, value, h) for h in hits]
            total = total + nt(jnp.concatenate(rows, axis=0), hot_ref[q * 4 + n])
        pieces = [total[i * OWN : (i + 1) * OWN] for i in range(len(hits))]
        own = pieces[:blocks]
        to_prev = pieces[blocks] if q > 0 else None
        to_next = pieces[-1] if q < tiles - 1 else None
        return own, to_prev, to_next

    for step in range(SUB):
        here, there = step % 2, (step + 1) % 2
        from_prev = None
        current = product(here, 0)
        for q in range(tiles):
            following = product(here, q + 1) if q < tiles - 1 else None
            own, _, to_next = current
            if from_prev is not None:
                own[0] = own[0] + from_prev
            if following is not None:
                own[1] = own[1] + following[1]
            x_ref[there, q] = (1.0 - 4.0 * rate) * x_ref[here, q] + jnp.concatenate(own, axis=1)
            from_prev, current = to_next, following
    last = SUB % 2
    quarters = col_max // WIDE
    mix = jnp.concatenate([misc_ref[8:16], misc_ref[8:16]], axis=1)[4:8]
    mix = jnp.concatenate([mix, mix], axis=0)
    for g in range(quarters):
        top = [
            x_ref[last, tiles // quarters * g + h, 0:1, k * WIDE : (k + 1) * WIDE]
            for h in range(tiles // quarters)
            for k in range(quarters)
        ]
        top = jnp.where((me * OWN) % layers == 0, jnp.concatenate(top, axis=0), mix)
        for q in range(tiles):
            piece = x_ref[last, q, :, g * WIDE : (g + 1) * WIDE]
            back_ref[q * quarters + g] = jnp.concatenate([piece, top], axis=0).astype(BF16)


def middle(tiles, parts, layers, data_ref, remap_ref, out_ref):
    col_max = remap_ref.shape[1]
    quarters = col_max // WIDE
    halves = layers // OWN
    species = 4 * parts
    me = lax.axis_index("spec")

    def source(s, half):
        return ((s % 4) * halves + half) * parts + s // 4

    mix = [data_ref[source(4 * k, 1)].astype(F32)[OWN : OWN + 4, 0:species] for k in range(parts)]
    mix = jnp.concatenate(mix, axis=0)
    size = species * OWN
    left = row_ids(size, species) // OWN == lax.broadcasted_iota(jnp.int32, (size, species), 1)
    right = row_ids(species, size) == lax.broadcasted_iota(jnp.int32, (species, size), 1) // OWN
    left, right = (jnp.where(hit, 1.0, 0.0).astype(BF16) for hit in (left, right))
    full = nn(nn(left, mix.astype(BF16)).astype(BF16), right)
    same = row_ids(size, size) % OWN == lax.broadcasted_iota(jnp.int32, (size, size), 1) % OWN
    full = jnp.where(same, full, 0.0).astype(BF16)
    mixed = []
    for half in range(halves):
        x = [data_ref[source(s, half), 0:OWN] for s in range(species)]
        mixed.append(nn(full, jnp.concatenate(x, axis=0)))

    table = [data_ref[source(s, 0)].astype(F32)[OWN:] for s in range(species)]
    table = jnp.concatenate(table, axis=0).astype(BF16)
    low = remap_ref[0:4].astype(BF16)
    place = remap_ref[4:8].astype(jnp.int32) * quarters + remap_ref[8:12].astype(jnp.int32)
    place = place - me * tiles
    ids = narrow(row_ids(WIDE, 1))
    totals = [jnp.zeros((tiles, col_max), F32) for s in range(species)]
    for r in range(4):
        found = nn(table, hot(low[r : r + 1], ids))
        weight = jnp.where(
            place[r : r + 1] == row_ids(tiles, 1), remap_ref[12 + r : 13 + r], 0.0
        )
        for s in range(species):
            totals[s] = totals[s] + found[s * tiles : (s + 1) * tiles] * weight
    bottom = [jnp.sum(total, axis=0, keepdims=True) for total in totals]
    bottom = nn(mix, jnp.concatenate(bottom, axis=0), lax.Precision.HIGHEST)
    for k in range(parts):
        rows = []
        for t in range(4 * k, 4 * k + 4):
            rows += [mixed[half][t * OWN : (t + 1) * OWN] for half in range(halves)]
        mine = bottom[4 * k : 4 * k + 4]
        rows += [mine[:, h * WIDE : (h + 1) * WIDE] for h in range(quarters)]
        out_ref[k] = jnp.concatenate(rows, axis=0).astype(BF16)


def settle(all_ref, state_ref, bottom_ref):
    parts, rows, wide = all_ref.shape
    width = state_ref.shape[1]
    total = jnp.zeros((rows - width, wide), F32)
    for k in range(parts):
        state = all_ref[k, 0:width].astype(F32)
        state_ref[k * wide : (k + 1) * wide, :] = state.T.astype(BF16)
        total = total + all_ref[k, width:].astype(F32)
    pieces = [total[h * 4 : h * 4 + 4] for h in range(parts)]
    bottom_ref[...] = jnp.concatenate(pieces, axis=1)


def shifted(block, axis, distance):
    devices = range(lax.axis_size(axis))
    route = [(i - distance, i) for i in devices if i - distance in devices]
    return lax.ppermute(block, axis, route)


def halo_body(
    grad_columns,
    grad_flux,
    remap_part,
    remap_slot,
    remap_weight,
    col_count,
    neighbors,
    kappa,
    thickness,
    vertical,
    reaction,
):
    tiles = lax.axis_size("tile")
    col_max = grad_columns.shape[0]
    rim_width = col_max // 8
    species = kappa.shape[0]
    layers = thickness.shape[1]
    width = species * layers
    cells, per_cell = remap_part.shape
    entries = cells * per_cell
    capacity = 2 * entries // tiles
    nbr_count = neighbors.shape[1]
    dest_flat = remap_part.reshape(-1)
    slot_flat = remap_slot.reshape(-1)
    dest_table = (dest_flat[:, None] == jnp.arange(tiles, dtype=jnp.int32)[None, :]).astype(
        jnp.int32
    )
    earlier = jnp.cumsum(dest_table, axis=0) - dest_table
    rank_within = jnp.sum(earlier * dest_table, axis=1)
    bucket_pos = dest_flat * capacity + rank_within
    entry_values = (remap_weight[:, :, None] * grad_flux.T[:, None, :]).reshape(entries, species)
    send_values = (
        jnp.zeros((tiles * capacity, species), jnp.float32)
        .at[bucket_pos]
        .set(entry_values)
        .reshape(tiles, capacity, species)
    )
    send_slots = (
        jnp.full((tiles * capacity, 1), col_max, jnp.int32)
        .at[bucket_pos]
        .set(slot_flat[:, None])
        .reshape(tiles, capacity, 1)
    )
    recv_values, recv_slots = (
        lax.all_to_all(send_values, "tile", split_axis=0, concat_axis=0, tiled=True),
        lax.all_to_all(send_slots, "tile", split_axis=0, concat_axis=0, tiled=True),
    )
    slot_index = recv_slots.reshape(-1)
    injected = (
        jnp.zeros((col_max + 1, species), jnp.float32)
        .at[slot_index]
        .add(recv_values.reshape(-1, species))[:col_max]
    )
    live_mask = (jnp.arange(col_max) < col_count[0]).astype(jnp.float32)[:, None]
    adjoint = live_mask * (
        grad_columns.astype(jnp.float32)
        + (injected[:, :, None] * thickness[None, :, :]).reshape(col_max, width)
    )
    rate_row = jnp.repeat(kappa, layers)[None, :]
    eye_block = jnp.eye(species, dtype=jnp.bfloat16)
    block_operator = jnp.einsum("slm,st->sltm", vertical, eye_block).reshape(width, width)
    target_rows = jnp.arange(col_max + 2 * rim_width, dtype=jnp.int32)[:, None]
    count_matrix = jnp.zeros((col_max + 2 * rim_width, col_max), jnp.float32)
    for column in range(nbr_count):
        count_matrix = count_matrix + (neighbors[:, column][None, :] == target_rows).astype(
            jnp.float32
        )
    zero_rest = jnp.zeros((col_max - 2 * rim_width, width), jnp.float32)
    for substep in range(SUB):
        spread = rate_row * adjoint
        extended = jnp.dot(
            count_matrix,
            spread,
            precision=lax.Precision.HIGHEST,
            preferred_element_type=jnp.float32,
        )
        to_previous = extended[col_max : col_max + rim_width]
        to_following = extended[col_max + rim_width :]
        from_following = shifted(to_previous.astype(jnp.bfloat16), "tile", -1).astype(
            to_previous.dtype
        )
        from_previous = shifted(to_following.astype(jnp.bfloat16), "tile", 1).astype(
            to_following.dtype
        )
        rim_terms = jnp.concatenate([from_previous, from_following, zero_rest], axis=0)
        bedload = adjoint - nbr_count * rate_row * adjoint + extended[:col_max] + rim_terms
        adjoint = jnp.dot(
            bedload.astype(jnp.bfloat16), block_operator, preferred_element_type=jnp.float32
        )
    rounded = adjoint.astype(jnp.bfloat16)
    piece = lax.all_gather(rounded, "spec", axis=1, tiled=True)
    piece_species = piece.shape[1] // layers
    mixed = jnp.einsum(
        "jsl,st->jtl",
        piece.reshape(col_max, piece_species, layers),
        reaction,
        preferred_element_type=jnp.float32,
    )
    grad_state = mixed.reshape(col_max, width).astype(jnp.bfloat16)
    top_layer = mixed[:, :, 0]
    everything = lax.all_gather(top_layer, "tile", axis=0, tiled=True)
    picked = everything[dest_flat * col_max + slot_flat]
    grad_bottom = jnp.sum(
        picked.reshape(cells, per_cell, species) * remap_weight[:, :, None], axis=1
    ).T
    return (grad_state, grad_bottom)


def column_body(
    grad_columns,
    grad_flux,
    remap_part,
    remap_slot,
    remap_weight,
    col_count,
    neighbors,
    kappa,
    thickness,
    vertical,
    reaction,
):
    tiles = lax.axis_size("tile")
    parts = lax.axis_size("spec")
    col_max, width = grad_columns.shape
    layers = thickness.shape[1]
    shape = jax.ShapeDtypeStruct
    moved = [grad_columns, vertical, thickness, grad_flux]
    moved += [remap_part.T, remap_slot.T, remap_weight.T, neighbors.T, reaction.T]
    payload, misc, remap = call(
        prepare,
        [
            shape((tiles, 2 * (OWN + tiles + 4), col_max // 2), BF16),
            shape((16, width), F32),
            shape((16, col_max), F32),
        ],
        [SMEM] * 2 + [HBM] * 9,
        scratch=[pltpu.VMEM(a.shape, a.dtype) for a in moved] + [pltpu.SemaphoreType.DMA((9,))],
        flops=4 * 10**7,
        moved=10**6,
        limit=MOST,
    )(col_count, kappa, *moved)
    data = lax.all_to_all(payload, "tile", split_axis=0, concat_axis=0, tiled=True)
    back = call(
        functools.partial(chain, tiles, layers),
        [shape((tiles * parts, OWN + tiles, WIDE), BF16)],
        [VMEM] * 2,
        scratch=[
            pltpu.VMEM((2, tiles, OWN, col_max), F32),
            pltpu.VMEM((tiles * 4, LANES, col_max), BF16),
            pltpu.VMEM((tiles, 4, col_max), F32),
        ],
        flops=10**10,
        moved=10**6,
    )(misc, data)[0]
    home = lax.all_to_all(back, ("tile", "spec"), split_axis=0, concat_axis=0, tiled=True)
    packed = call(
        functools.partial(middle, tiles, parts, layers),
        [shape((parts, width + OWN, WIDE), BF16)],
        [VMEM] * 2,
        flops=10**9,
        moved=10**6,
    )(home, remap)[0]
    every = lax.all_to_all(packed, "spec", split_axis=0, concat_axis=0, tiled=True)
    outs = [shape((col_max, width), BF16), shape((4, col_max), F32)]
    return tuple(call(settle, outs, [VMEM], flops=10**8, moved=10**6)(every))


def body(*args):
    tiles, parts = lax.axis_size("tile"), lax.axis_size("spec")
    layers = args[8].shape[1]
    fits = tiles == 8 and layers == 2 * OWN and args[0].shape == (parts * WIDE, tiles * OWN)
    return (column_body if fits else halo_body)(*args)


def solution(mesh):
    placed = (
        P("tile", "spec"),
        P("spec", "tile"),
        P("tile", None),
        P("tile", None),
        P("tile", None),
        P("tile"),
        P("tile", None),
        P("spec"),
        P("spec", None),
        P("spec", None, None),
        P(None, "spec"),
    )
    return jax.shard_map(
        body,
        mesh=mesh,
        in_specs=placed,
        out_specs=(P("tile", "spec"), P("spec", "tile")),
        check_vma=False,
    )
```

```python
import functools

import jax
import jax.numpy as jnp
from jax import lax
from jax.experimental import pallas as pl
from jax.experimental.pallas import tpu as pltpu
from jax.sharding import PartitionSpec as P

SUB = 4
LANES = 128
WIDE = 256
OWN = 16
DEAD = 15
F32 = jnp.float32
BF16 = jnp.bfloat16
VMEM = pl.BlockSpec(memory_space=pltpu.VMEM)
HBM = pl.BlockSpec(memory_space=pltpu.HBM)
SMEM = pl.BlockSpec(memory_space=pltpu.SMEM)
LIMIT = 40 * 1024 * 1024
MOST = 60 * 1024 * 1024


def call(kernel, outs, specs, scratch=(), flops=0, moved=0, limit=LIMIT):
    return pl.pallas_call(
        kernel,
        out_shape=outs,
        in_specs=specs,
        out_specs=[VMEM] * len(outs),
        scratch_shapes=scratch,
        compiler_params=pltpu.CompilerParams(vmem_limit_bytes=limit),
        cost_estimate=pl.CostEstimate(flops=flops, bytes_accessed=moved, transcendentals=0),
    )


def nt(a, b, precision=None):
    return lax.dot_general(
        a, b, (((1,), (1,)), ((), ())), precision=precision, preferred_element_type=F32
    )


def nn(a, b, precision=None):
    return lax.dot_general(
        a, b, (((1,), (0,)), ((), ())), precision=precision, preferred_element_type=F32
    )


def row_ids(rows, cols):
    return lax.broadcasted_iota(jnp.int32, (rows, cols), 0)


def started(pairs, sems):
    copies = [pltpu.make_async_copy(a, b, sems.at[i]) for i, (a, b) in enumerate(pairs)]
    for copy in copies:
        copy.start()
    return copies


def coded(ints):
    value = (128 + (ints & 127)).astype(F32)
    for bit in range(4):
        value = value * jnp.where((ints >> (7 + bit)) & 1 == 1, float(2 ** (2**bit)), 1.0)
    return value


def decoded(value):
    high = jnp.zeros(value.shape, jnp.int32)
    for bit in (8, 4, 2, 1):
        large = value >= 128.0 * 2.0**bit
        value = jnp.where(large, value * 2.0**-bit, value)
        high = high + jnp.where(large, bit, 0)
    return value - 128.0, high


def hot(key, ids):
    return jnp.where(ids == key, jnp.ones((), BF16), jnp.zeros((), BF16))


def picked(keys, value, target):
    return jnp.where(keys == jnp.asarray(target, BF16), value, jnp.zeros((), BF16))


def narrow(ints):
    return ints.astype(F32).astype(BF16)


def folded(rows):
    middle = rows.shape[1] // 2
    return [rows[:, :middle], rows[:, middle:]]


def prepare(
    count_ref, kappa_ref, gc_any, vert_any, thick_any, flux_any, part_any, slot_any, weight_any,
    nbr_any, reaction_any, payload_ref, misc_ref, remap_ref,
    gc_ref, vert_ref, thick_ref, flux_ref, part_ref, slot_ref, weight_ref, nbr_ref, reaction_ref,
    sems,
):
    copies = started(
        [
            (vert_any, vert_ref),
            (thick_any, thick_ref),
            (reaction_any, reaction_ref),
            (slot_any, slot_ref),
            (part_any, part_ref),
            (weight_any, weight_ref),
            (flux_any, flux_ref),
            (nbr_any, nbr_ref),
            (gc_any, gc_ref),
        ],
        sems,
    )
    for copy in copies:
        copy.wait()
    tiles = payload_ref.shape[0]
    col_max = gc_ref.shape[0]
    species, layers, _ = vert_ref.shape
    width = species * layers
    subs = col_max // WIDE

    v = vert_ref[...].astype(F32).reshape(width, layers)
    v = jnp.concatenate([v] * species, axis=1)
    rows = row_ids(width, width) // layers
    cols = lax.broadcasted_iota(jnp.int32, (width, width), 1) // layers
    vt = jnp.where(rows == cols, v, 0.0).T.astype(BF16)
    hi = lax.Precision.HIGHEST
    v2 = nn(vt, vt)
    v4 = nn(v2, v2, hi)
    th = jnp.concatenate([thick_ref[s : s + 1, :] for s in range(species)], axis=1)
    misc_ref[0:8] = nt(jnp.broadcast_to(th, (8, width)), v4, hi)
    rates = [jnp.full((1, width), kappa_ref[s], F32) for s in range(species)]
    mix = reaction_ref[...].astype(F32)
    mix = jnp.concatenate([mix, jnp.zeros((4, width - mix.shape[1]), F32)], axis=1)
    misc_ref[8:16] = jnp.concatenate(rates + [mix], axis=0)
    flux, weight = flux_ref[...], weight_ref[...]
    slot = slot_ref[...]
    part, sub, low = part_ref[...], slot // WIDE, slot % WIDE
    remap_ref[...] = jnp.concatenate(
        [low.astype(F32), part.astype(F32), sub.astype(F32), weight], axis=0
    )
    low = narrow(low)
    ids = narrow(row_ids(WIDE, 1))
    place = row_ids(16, 1)
    sums = jnp.zeros((species * subs * tiles, WIDE), F32)
    for r in range(4):
        value = flux * weight[r : r + 1]
        value = [jnp.broadcast_to(value[s : s + 1], (16, col_max)).astype(BF16) for s in range(4)]
        spot = sub[r : r + 1] * tiles + part[r : r + 1]
        keys = [narrow(spot - place - 16 * k) for k in range(subs * tiles // 16)]
        blocks = [picked(key, value[s], 0) for s in range(species) for key in keys]
        sums = sums + nt(jnp.concatenate(blocks, axis=0), hot(low[r : r + 1], ids))

    live = lax.broadcasted_iota(jnp.int32, (1, col_max), 1) < count_ref[0]
    tail = folded(coded(jnp.where(live, nbr_ref[...], DEAD * LANES)))
    w = jnp.where(live, nt(v4.astype(BF16), gc_ref[...]), 0.0)
    for q in range(tiles):
        s = q * OWN // layers
        mine = sums[s * subs * tiles : (s + 1) * subs * tiles]
        mine = jnp.concatenate([mine[h * tiles : (h + 1) * tiles] for h in range(subs)], axis=1)
        pieces = folded(w[q * OWN : (q + 1) * OWN]) + folded(mine) + tail
        payload_ref[q] = jnp.concatenate(pieces, axis=0).astype(BF16)


def unfolded(block, first, rows):
    return jnp.concatenate([block[first : first + rows], block[first + rows : first + 2 * rows]], axis=1)


def chain(tiles, layers, misc_ref, data_ref, back_ref, x_ref, hot_ref, key_ref):
    col_max = x_ref.shape[3]
    blocks = col_max // LANES
    me = lax.axis_index("tile")
    ids = narrow(row_ids(LANES, 1))

    lane = lax.broadcasted_iota(jnp.int32, (OWN, misc_ref.shape[1]), 1)
    row = row_ids(OWN, 1)
    tv_own = jnp.where(lane == me * OWN + row, misc_ref[0:1], 0.0)
    tv_own = jnp.sum(tv_own, axis=1, keepdims=True)
    mine = me * OWN // layers
    rate = jnp.zeros((1, 1), F32)
    for s in range(4):
        rate = jnp.where(mine == s, misc_ref[8 + s : 9 + s, 0:1], rate)

    inj = jnp.zeros((tiles, col_max), F32)
    for q in range(tiles):
        block = data_ref[q].astype(F32)
        inj = inj + unfolded(block, 2 * OWN, tiles)

    def start(q):
        block = data_ref[q].astype(F32)
        low, high = decoded(unfolded(block, 2 * OWN + 2 * tiles, 4))
        live = high[0:1] != DEAD
        x_ref[0, q] = unfolded(block, 0, OWN) + tv_own * jnp.where(live, inj[q : q + 1], 0.0)
        high = high.astype(F32)
        for n in range(4):
            cols = slice(n * col_max, (n + 1) * col_max)
            key_ref[q, :, cols] = jnp.broadcast_to(high[n : n + 1], (OWN, col_max)).astype(BF16)
            hot_ref[q, :, cols] = hot(low[n : n + 1].astype(BF16), ids)

    def product(step, q):
        if step == 0:
            start(q)
        value = (rate * x_ref[step % 2, q]).astype(BF16)
        value = jnp.concatenate([value] * 4, axis=1)
        hits = list(range(blocks)) + [blocks] * (q > 0) + [blocks + 1] * (q < tiles - 1)
        rows = [picked(key_ref[q], value, h) for h in hits]
        total = nt(jnp.concatenate(rows, axis=0), hot_ref[q])
        pieces = [total[i * OWN : (i + 1) * OWN] for i in range(len(hits))]
        own = pieces[:blocks]
        to_prev = pieces[blocks] if q > 0 else None
        to_next = pieces[-1] if q < tiles - 1 else None
        return own, to_prev, to_next

    for step in range(SUB):
        here, there = step % 2, (step + 1) % 2
        from_prev = None
        current = product(step, 0)
        for q in range(tiles):
            following = product(step, q + 1) if q < tiles - 1 else None
            own, _, to_next = current
            if from_prev is not None:
                own[0] = own[0] + from_prev
            if following is not None:
                own[1] = own[1] + following[1]
            x_ref[there, q] = (1.0 - 4.0 * rate) * x_ref[here, q] + jnp.concatenate(own, axis=1)
            from_prev, current = to_next, following
    last = SUB % 2
    quarters = col_max // WIDE
    mix = jnp.concatenate([misc_ref[8:16], misc_ref[8:16]], axis=1)[4:8]
    mix = jnp.concatenate([mix, mix], axis=0)
    for g in range(quarters):
        top = [
            x_ref[last, tiles // quarters * g + h, 0:1, k * WIDE : (k + 1) * WIDE]
            for h in range(tiles // quarters)
            for k in range(quarters)
        ]
        top = jnp.where((me * OWN) % layers == 0, jnp.concatenate(top, axis=0), mix)
        for q in range(tiles):
            piece = x_ref[last, q, :, g * WIDE : (g + 1) * WIDE]
            back_ref[q * quarters + g] = jnp.concatenate([piece, top], axis=0).astype(BF16)


def middle(tiles, parts, layers, data_ref, remap_ref, out_ref):
    col_max = remap_ref.shape[1]
    quarters = col_max // WIDE
    halves = layers // OWN
    species = 4 * parts
    me = lax.axis_index("spec")

    def source(s, half):
        return ((s % 4) * halves + half) * parts + s // 4

    mix = [data_ref[source(4 * k, 1)].astype(F32)[OWN : OWN + 4, 0:species] for k in range(parts)]
    mix = jnp.concatenate(mix, axis=0)
    size = species * OWN
    left = row_ids(size, species) // OWN == lax.broadcasted_iota(jnp.int32, (size, species), 1)
    right = row_ids(species, size) == lax.broadcasted_iota(jnp.int32, (species, size), 1) // OWN
    left, right = (jnp.where(hit, 1.0, 0.0).astype(BF16) for hit in (left, right))
    full = nn(nn(left, mix.astype(BF16)).astype(BF16), right)
    same = row_ids(size, size) % OWN == lax.broadcasted_iota(jnp.int32, (size, size), 1) % OWN
    full = jnp.where(same, full, 0.0).astype(BF16)
    mixed = []
    for half in range(halves):
        x = [data_ref[source(s, half), 0:OWN] for s in range(species)]
        mixed.append(nn(full, jnp.concatenate(x, axis=0)))

    table = [data_ref[source(s, 0)].astype(F32)[OWN:] for s in range(species)]
    table = jnp.concatenate(table, axis=0).astype(BF16)
    low = remap_ref[0:4].astype(BF16)
    place = remap_ref[4:8].astype(jnp.int32) * quarters + remap_ref[8:12].astype(jnp.int32)
    place = place - me * tiles
    ids = narrow(row_ids(WIDE, 1))
    totals = [jnp.zeros((tiles, col_max), F32) for s in range(species)]
    for r in range(4):
        found = nn(table, hot(low[r : r + 1], ids))
        weight = jnp.where(
            place[r : r + 1] == row_ids(tiles, 1), remap_ref[12 + r : 13 + r], 0.0
        )
        for s in range(species):
            totals[s] = totals[s] + found[s * tiles : (s + 1) * tiles] * weight
    bottom = [jnp.sum(total, axis=0, keepdims=True) for total in totals]
    bottom = nn(mix, jnp.concatenate(bottom, axis=0), lax.Precision.HIGHEST)
    for k in range(parts):
        rows = []
        for t in range(4 * k, 4 * k + 4):
            rows += [mixed[half][t * OWN : (t + 1) * OWN] for half in range(halves)]
        mine = bottom[4 * k : 4 * k + 4]
        rows += [mine[:, h * WIDE : (h + 1) * WIDE] for h in range(quarters)]
        out_ref[k] = jnp.concatenate(rows, axis=0).astype(BF16)


def settle(all_ref, state_ref, bottom_ref):
    parts, rows, wide = all_ref.shape
    width = state_ref.shape[1]
    total = jnp.zeros((rows - width, wide), F32)
    for k in range(parts):
        state = all_ref[k, 0:width].astype(F32)
        state_ref[k * wide : (k + 1) * wide, :] = state.T.astype(BF16)
        total = total + all_ref[k, width:].astype(F32)
    pieces = [total[h * 4 : h * 4 + 4] for h in range(parts)]
    bottom_ref[...] = jnp.concatenate(pieces, axis=1)


def shifted(block, axis, distance):
    devices = range(lax.axis_size(axis))
    route = [(i - distance, i) for i in devices if i - distance in devices]
    return lax.ppermute(block, axis, route)


def halo_body(
    grad_columns,
    grad_flux,
    remap_part,
    remap_slot,
    remap_weight,
    col_count,
    neighbors,
    kappa,
    thickness,
    vertical,
    reaction,
):
    tiles = lax.axis_size("tile")
    col_max = grad_columns.shape[0]
    rim_width = col_max // 8
    species = kappa.shape[0]
    layers = thickness.shape[1]
    width = species * layers
    cells, per_cell = remap_part.shape
    entries = cells * per_cell
    capacity = 2 * entries // tiles
    nbr_count = neighbors.shape[1]
    dest_flat = remap_part.reshape(-1)
    slot_flat = remap_slot.reshape(-1)
    dest_table = (dest_flat[:, None] == jnp.arange(tiles, dtype=jnp.int32)[None, :]).astype(
        jnp.int32
    )
    earlier = jnp.cumsum(dest_table, axis=0) - dest_table
    rank_within = jnp.sum(earlier * dest_table, axis=1)
    bucket_pos = dest_flat * capacity + rank_within
    entry_values = (remap_weight[:, :, None] * grad_flux.T[:, None, :]).reshape(entries, species)
    send_values = (
        jnp.zeros((tiles * capacity, species), jnp.float32)
        .at[bucket_pos]
        .set(entry_values)
        .reshape(tiles, capacity, species)
    )
    send_slots = (
        jnp.full((tiles * capacity, 1), col_max, jnp.int32)
        .at[bucket_pos]
        .set(slot_flat[:, None])
        .reshape(tiles, capacity, 1)
    )
    recv_values, recv_slots = (
        lax.all_to_all(send_values, "tile", split_axis=0, concat_axis=0, tiled=True),
        lax.all_to_all(send_slots, "tile", split_axis=0, concat_axis=0, tiled=True),
    )
    slot_index = recv_slots.reshape(-1)
    injected = (
        jnp.zeros((col_max + 1, species), jnp.float32)
        .at[slot_index]
        .add(recv_values.reshape(-1, species))[:col_max]
    )
    live_mask = (jnp.arange(col_max) < col_count[0]).astype(jnp.float32)[:, None]
    adjoint = live_mask * (
        grad_columns.astype(jnp.float32)
        + (injected[:, :, None] * thickness[None, :, :]).reshape(col_max, width)
    )
    rate_row = jnp.repeat(kappa, layers)[None, :]
    eye_block = jnp.eye(species, dtype=jnp.bfloat16)
    block_operator = jnp.einsum("slm,st->sltm", vertical, eye_block).reshape(width, width)
    target_rows = jnp.arange(col_max + 2 * rim_width, dtype=jnp.int32)[:, None]
    count_matrix = jnp.zeros((col_max + 2 * rim_width, col_max), jnp.float32)
    for column in range(nbr_count):
        count_matrix = count_matrix + (neighbors[:, column][None, :] == target_rows).astype(
            jnp.float32
        )
    zero_rest = jnp.zeros((col_max - 2 * rim_width, width), jnp.float32)
    for substep in range(SUB):
        spread = rate_row * adjoint
        extended = jnp.dot(
            count_matrix,
            spread,
            precision=lax.Precision.HIGHEST,
            preferred_element_type=jnp.float32,
        )
        to_previous = extended[col_max : col_max + rim_width]
        to_following = extended[col_max + rim_width :]
        from_following = shifted(to_previous.astype(jnp.bfloat16), "tile", -1).astype(
            to_previous.dtype
        )
        from_previous = shifted(to_following.astype(jnp.bfloat16), "tile", 1).astype(
            to_following.dtype
        )
        rim_terms = jnp.concatenate([from_previous, from_following, zero_rest], axis=0)
        bedload = adjoint - nbr_count * rate_row * adjoint + extended[:col_max] + rim_terms
        adjoint = jnp.dot(
            bedload.astype(jnp.bfloat16), block_operator, preferred_element_type=jnp.float32
        )
    rounded = adjoint.astype(jnp.bfloat16)
    piece = lax.all_gather(rounded, "spec", axis=1, tiled=True)
    piece_species = piece.shape[1] // layers
    mixed = jnp.einsum(
        "jsl,st->jtl",
        piece.reshape(col_max, piece_species, layers),
        reaction,
        preferred_element_type=jnp.float32,
    )
    grad_state = mixed.reshape(col_max, width).astype(jnp.bfloat16)
    top_layer = mixed[:, :, 0]
    everything = lax.all_gather(top_layer, "tile", axis=0, tiled=True)
    picked = everything[dest_flat * col_max + slot_flat]
    grad_bottom = jnp.sum(
        picked.reshape(cells, per_cell, species) * remap_weight[:, :, None], axis=1
    ).T
    return (grad_state, grad_bottom)


def column_body(
    grad_columns,
    grad_flux,
    remap_part,
    remap_slot,
    remap_weight,
    col_count,
    neighbors,
    kappa,
    thickness,
    vertical,
    reaction,
):
    tiles = lax.axis_size("tile")
    parts = lax.axis_size("spec")
    col_max, width = grad_columns.shape
    layers = thickness.shape[1]
    shape = jax.ShapeDtypeStruct
    moved = [grad_columns, vertical, thickness, grad_flux]
    moved += [remap_part.T, remap_slot.T, remap_weight.T, neighbors.T, reaction.T]
    payload, misc, remap = call(
        prepare,
        [
            shape((tiles, 2 * (OWN + tiles + 4), col_max // 2), BF16),
            shape((16, width), F32),
            shape((16, col_max), F32),
        ],
        [SMEM] * 2 + [HBM] * 9,
        scratch=[pltpu.VMEM(a.shape, a.dtype) for a in moved] + [pltpu.SemaphoreType.DMA((9,))],
        flops=4 * 10**7,
        moved=10**6,
        limit=MOST,
    )(col_count, kappa, *moved)
    data = lax.all_to_all(payload, "tile", split_axis=0, concat_axis=0, tiled=True)
    back = call(
        functools.partial(chain, tiles, layers),
        [shape((tiles * parts, OWN + tiles, WIDE), BF16)],
        [VMEM] * 2,
        scratch=[
            pltpu.VMEM((2, tiles, OWN, col_max), F32),
            pltpu.VMEM((tiles, LANES, 4 * col_max), BF16),
            pltpu.VMEM((tiles, OWN, 4 * col_max), BF16),
        ],
        flops=10**10,
        moved=10**6,
    )(misc, data)[0]
    home = lax.all_to_all(back, ("tile", "spec"), split_axis=0, concat_axis=0, tiled=True)
    packed = call(
        functools.partial(middle, tiles, parts, layers),
        [shape((parts, width + OWN, WIDE), BF16)],
        [VMEM] * 2,
        flops=10**9,
        moved=10**6,
    )(home, remap)[0]
    every = lax.all_to_all(packed, "spec", split_axis=0, concat_axis=0, tiled=True)
    outs = [shape((col_max, width), BF16), shape((4, col_max), F32)]
    return tuple(call(settle, outs, [VMEM], flops=10**8, moved=10**6)(every))


def body(*args):
    tiles, parts = lax.axis_size("tile"), lax.axis_size("spec")
    layers = args[8].shape[1]
    fits = tiles == 8 and layers == 2 * OWN and args[0].shape == (parts * WIDE, tiles * OWN)
    return (column_body if fits else halo_body)(*args)


def solution(mesh):
    placed = (
        P("tile", "spec"),
        P("spec", "tile"),
        P("tile", None),
        P("tile", None),
        P("tile", None),
        P("tile"),
        P("tile", None),
        P("spec"),
        P("spec", None),
        P("spec", None, None),
        P(None, "spec"),
    )
    return jax.shard_map(
        body,
        mesh=mesh,
        in_specs=placed,
        out_specs=(P("tile", "spec"), P("spec", "tile")),
        check_vma=False,
    )
```

```python
import functools

import jax
import jax.numpy as jnp
from jax import lax
from jax.experimental import pallas as pl
from jax.experimental.pallas import tpu as pltpu
from jax.sharding import PartitionSpec as P

SUB = 4
LANES = 128
WIDE = 256
OWN = 16
DEAD = 15
F32 = jnp.float32
BF16 = jnp.bfloat16
VMEM = pl.BlockSpec(memory_space=pltpu.VMEM)
HBM = pl.BlockSpec(memory_space=pltpu.HBM)
SMEM = pl.BlockSpec(memory_space=pltpu.SMEM)
LIMIT = 40 * 1024 * 1024
MOST = 60 * 1024 * 1024


def call(kernel, outs, specs, scratch=(), flops=0, moved=0, limit=LIMIT):
    return pl.pallas_call(
        kernel,
        out_shape=outs,
        in_specs=specs,
        out_specs=[VMEM] * len(outs),
        scratch_shapes=scratch,
        compiler_params=pltpu.CompilerParams(vmem_limit_bytes=limit),
        cost_estimate=pl.CostEstimate(flops=flops, bytes_accessed=moved, transcendentals=0),
    )


def nt(a, b, precision=None):
    return lax.dot_general(
        a, b, (((1,), (1,)), ((), ())), precision=precision, preferred_element_type=F32
    )


def nn(a, b, precision=None):
    return lax.dot_general(
        a, b, (((1,), (0,)), ((), ())), precision=precision, preferred_element_type=F32
    )


def row_ids(rows, cols):
    return lax.broadcasted_iota(jnp.int32, (rows, cols), 0)


def started(pairs, sems):
    copies = [pltpu.make_async_copy(a, b, sems.at[i]) for i, (a, b) in enumerate(pairs)]
    for copy in copies:
        copy.start()
    return copies


def coded(ints):
    value = (128 + (ints & 127)).astype(F32)
    for bit in range(4):
        value = value * jnp.where((ints >> (7 + bit)) & 1 == 1, float(2 ** (2**bit)), 1.0)
    return value


def decoded(value):
    high = jnp.zeros(value.shape, jnp.int32)
    for bit in (8, 4, 2, 1):
        large = value >= 128.0 * 2.0**bit
        value = jnp.where(large, value * 2.0**-bit, value)
        high = high + jnp.where(large, bit, 0)
    return value - 128.0, high


def hot(key, ids):
    return jnp.where(ids == key, jnp.ones((), BF16), jnp.zeros((), BF16))


def picked(keys, value, target):
    return jnp.where(keys == jnp.asarray(target, BF16), value, jnp.zeros((), BF16))


def narrow(ints):
    return ints.astype(F32).astype(BF16)


def folded(rows):
    middle = rows.shape[1] // 2
    return [rows[:, :middle], rows[:, middle:]]


def prepare(
    count_ref, kappa_any, gc_any, vert_any, thick_any, flux_any, part_any, slot_any, weight_any,
    nbr_any, reaction_any, payload_ref, misc_ref, remap_ref,
    kappa_ref, gc_ref, vert_ref, thick_ref, flux_ref, part_ref, slot_ref, weight_ref,
    nbr_ref, reaction_ref, sems,
):
    copies = started(
        [
            (gc_any, gc_ref),
            (kappa_any, kappa_ref),
            (vert_any, vert_ref),
            (thick_any, thick_ref),
            (reaction_any, reaction_ref),
            (slot_any, slot_ref),
            (part_any, part_ref),
            (weight_any, weight_ref),
            (flux_any, flux_ref),
            (nbr_any, nbr_ref),
        ],
        sems,
    )
    for copy in copies:
        copy.wait()
    tiles = payload_ref.shape[0]
    col_max = gc_ref.shape[0]
    species, layers, _ = vert_ref.shape
    width = species * layers
    subs = col_max // WIDE

    v = vert_ref[...].astype(F32).reshape(width, layers)
    v = jnp.concatenate([v] * species, axis=1)
    rows = row_ids(width, width) // layers
    cols = lax.broadcasted_iota(jnp.int32, (width, width), 1) // layers
    vt = jnp.where(rows == cols, v, 0.0).T.astype(BF16)
    hi = lax.Precision.HIGHEST
    v2 = nn(vt, vt)
    v4 = nn(v2, v2, hi)
    th = jnp.concatenate([thick_ref[s : s + 1, :] for s in range(species)], axis=1)
    misc_ref[0:8] = nt(jnp.broadcast_to(th, (8, width)), v4, hi)
    rates = [jnp.full((1, width), kappa_ref[s], F32) for s in range(species)]
    mix = reaction_ref[...].astype(F32)
    mix = jnp.concatenate([mix, jnp.zeros((4, width - mix.shape[1]), F32)], axis=1)
    misc_ref[8:16] = jnp.concatenate(rates + [mix], axis=0)
    flux, weight = flux_ref[...], weight_ref[...]
    slot = slot_ref[...]
    part, sub, low = part_ref[...], slot // WIDE, slot % WIDE
    remap_ref[...] = jnp.concatenate(
        [low.astype(F32), part.astype(F32), sub.astype(F32), weight], axis=0
    )
    low = narrow(low)
    ids = narrow(row_ids(WIDE, 1))
    place = row_ids(16, 1)
    sums = jnp.zeros((species * subs * tiles, WIDE), F32)
    for r in range(4):
        value = flux * weight[r : r + 1]
        value = [jnp.broadcast_to(value[s : s + 1], (16, col_max)).astype(BF16) for s in range(4)]
        spot = sub[r : r + 1] * tiles + part[r : r + 1]
        keys = [narrow(spot - place - 16 * k) for k in range(subs * tiles // 16)]
        blocks = [picked(key, value[s], 0) for s in range(species) for key in keys]
        sums = sums + nt(jnp.concatenate(blocks, axis=0), hot(low[r : r + 1], ids))

    live = lax.broadcasted_iota(jnp.int32, (1, col_max), 1) < count_ref[0]
    tail = folded(coded(jnp.where(live, nbr_ref[...], DEAD * LANES)))
    w = jnp.where(live, nt(v4.astype(BF16), gc_ref[...]), 0.0)
    for q in range(tiles):
        s = q * OWN // layers
        mine = sums[s * subs * tiles : (s + 1) * subs * tiles]
        mine = jnp.concatenate([mine[h * tiles : (h + 1) * tiles] for h in range(subs)], axis=1)
        pieces = folded(w[q * OWN : (q + 1) * OWN]) + folded(mine) + tail
        payload_ref[q] = jnp.concatenate(pieces, axis=0).astype(BF16)


def unfolded(block, first, rows):
    return jnp.concatenate([block[first : first + rows], block[first + rows : first + 2 * rows]], axis=1)


def chain(tiles, layers, misc_ref, data_ref, back_ref, x_ref, hot_ref, high_ref):
    col_max = x_ref.shape[3]
    blocks = col_max // LANES
    me = lax.axis_index("tile")
    ids = narrow(row_ids(LANES, 1))

    lane = lax.broadcasted_iota(jnp.int32, (OWN, misc_ref.shape[1]), 1)
    row = row_ids(OWN, 1)
    tv_own = jnp.where(lane == me * OWN + row, misc_ref[0:1], 0.0)
    tv_own = jnp.sum(tv_own, axis=1, keepdims=True)
    mine = me * OWN // layers
    rate = jnp.zeros((1, 1), F32)
    for s in range(4):
        rate = jnp.where(mine == s, misc_ref[8 + s : 9 + s, 0:1], rate)

    inj = jnp.zeros((tiles, col_max), F32)
    for q in range(tiles):
        block = data_ref[q].astype(F32)
        inj = inj + unfolded(block, 2 * OWN, tiles)
    for q in range(tiles):
        block = data_ref[q].astype(F32)
        low, high = decoded(unfolded(block, 2 * OWN + 2 * tiles, 4))
        live = high[0:1] != DEAD
        x_ref[0, q] = unfolded(block, 0, OWN) + tv_own * jnp.where(live, inj[q : q + 1], 0.0)
        high_ref[q] = high.astype(F32)
        for n in range(4):
            hot_ref[q * 4 + n] = hot(low[n : n + 1].astype(BF16), ids)

    def product(here, q):
        high = high_ref[q]
        value = (rate * x_ref[here, q]).astype(BF16)
        hits = list(range(blocks)) + [blocks] * (q > 0) + [blocks + 1] * (q < tiles - 1)
        total = jnp.zeros((len(hits) * OWN, LANES), F32)
        for n in range(4):
            key = jnp.broadcast_to(high[n : n + 1], (OWN, col_max)).astype(BF16)
            rows = [picked(key, value, h) for h in hits]
            total = total + nt(jnp.concatenate(rows, axis=0), hot_ref[q * 4 + n])
        pieces = [total[i * OWN : (i + 1) * OWN] for i in range(len(hits))]
        own = pieces[:blocks]
        to_prev = pieces[blocks] if q > 0 else None
        to_next = pieces[-1] if q < tiles - 1 else None
        return own, to_prev, to_next

    for step in range(SUB):
        here, there = step % 2, (step + 1) % 2
        from_prev = None
        current = product(here, 0)
        for q in range(tiles):
            following = product(here, q + 1) if q < tiles - 1 else None
            own, _, to_next = current
            if from_prev is not None:
                own[0] = own[0] + from_prev
            if following is not None:
                own[1] = own[1] + following[1]
            x_ref[there, q] = (1.0 - 4.0 * rate) * x_ref[here, q] + jnp.concatenate(own, axis=1)
            from_prev, current = to_next, following
    last = SUB % 2
    quarters = col_max // WIDE
    mix = jnp.concatenate([misc_ref[8:16], misc_ref[8:16]], axis=1)[4:8]
    mix = jnp.concatenate([mix, mix], axis=0)
    for g in range(quarters):
        top = [
            x_ref[last, tiles // quarters * g + h, 0:1, k * WIDE : (k + 1) * WIDE]
            for h in range(tiles // quarters)
            for k in range(quarters)
        ]
        top = jnp.where((me * OWN) % layers == 0, jnp.concatenate(top, axis=0), mix)
        for q in range(tiles):
            piece = x_ref[last, q, :, g * WIDE : (g + 1) * WIDE]
            back_ref[q * quarters + g] = jnp.concatenate([piece, top], axis=0).astype(BF16)


def middle(tiles, parts, layers, data_ref, remap_ref, out_ref):
    col_max = remap_ref.shape[1]
    quarters = col_max // WIDE
    halves = layers // OWN
    species = 4 * parts
    me = lax.axis_index("spec")

    def source(s, half):
        return ((s % 4) * halves + half) * parts + s // 4

    mix = [data_ref[source(4 * k, 1)].astype(F32)[OWN : OWN + 4, 0:species] for k in range(parts)]
    mix = jnp.concatenate(mix, axis=0)
    size = species * OWN
    left = row_ids(size, species) // OWN == lax.broadcasted_iota(jnp.int32, (size, species), 1)
    right = row_ids(species, size) == lax.broadcasted_iota(jnp.int32, (species, size), 1) // OWN
    left, right = (jnp.where(hit, 1.0, 0.0).astype(BF16) for hit in (left, right))
    full = nn(nn(left, mix.astype(BF16)).astype(BF16), right)
    same = row_ids(size, size) % OWN == lax.broadcasted_iota(jnp.int32, (size, size), 1) % OWN
    full = jnp.where(same, full, 0.0).astype(BF16)
    mixed = []
    for half in range(halves):
        x = [data_ref[source(s, half), 0:OWN] for s in range(species)]
        mixed.append(nn(full, jnp.concatenate(x, axis=0)))

    table = [data_ref[source(s, 0)].astype(F32)[OWN:] for s in range(species)]
    table = jnp.concatenate(table, axis=0).astype(BF16)
    low = remap_ref[0:4].astype(BF16)
    place = remap_ref[4:8].astype(jnp.int32) * quarters + remap_ref[8:12].astype(jnp.int32)
    place = place - me * tiles
    ids = narrow(row_ids(WIDE, 1))
    totals = [jnp.zeros((tiles, col_max), F32) for s in range(species)]
    for r in range(4):
        found = nn(table, hot(low[r : r + 1], ids))
        weight = jnp.where(
            place[r : r + 1] == row_ids(tiles, 1), remap_ref[12 + r : 13 + r], 0.0
        )
        for s in range(species):
            totals[s] = totals[s] + found[s * tiles : (s + 1) * tiles] * weight
    bottom = [jnp.sum(total, axis=0, keepdims=True) for total in totals]
    bottom = nn(mix, jnp.concatenate(bottom, axis=0), lax.Precision.HIGHEST)
    for k in range(parts):
        rows = []
        for t in range(4 * k, 4 * k + 4):
            rows += [mixed[half][t * OWN : (t + 1) * OWN] for half in range(halves)]
        mine = bottom[4 * k : 4 * k + 4]
        rows += [mine[:, h * WIDE : (h + 1) * WIDE] for h in range(quarters)]
        out_ref[k] = jnp.concatenate(rows, axis=0).astype(BF16)


def settle(all_ref, state_ref, bottom_ref):
    parts, rows, wide = all_ref.shape
    width = state_ref.shape[1]
    total = jnp.zeros((rows - width, wide), F32)
    for k in range(parts):
        state = all_ref[k, 0:width].astype(F32)
        state_ref[k * wide : (k + 1) * wide, :] = state.T.astype(BF16)
        total = total + all_ref[k, width:].astype(F32)
    pieces = [total[h * 4 : h * 4 + 4] for h in range(parts)]
    bottom_ref[...] = jnp.concatenate(pieces, axis=1)


def shifted(block, axis, distance):
    devices = range(lax.axis_size(axis))
    route = [(i - distance, i) for i in devices if i - distance in devices]
    return lax.ppermute(block, axis, route)


def halo_body(
    grad_columns,
    grad_flux,
    remap_part,
    remap_slot,
    remap_weight,
    col_count,
    neighbors,
    kappa,
    thickness,
    vertical,
    reaction,
):
    tiles = lax.axis_size("tile")
    col_max = grad_columns.shape[0]
    rim_width = col_max // 8
    species = kappa.shape[0]
    layers = thickness.shape[1]
    width = species * layers
    cells, per_cell = remap_part.shape
    entries = cells * per_cell
    capacity = 2 * entries // tiles
    nbr_count = neighbors.shape[1]
    dest_flat = remap_part.reshape(-1)
    slot_flat = remap_slot.reshape(-1)
    dest_table = (dest_flat[:, None] == jnp.arange(tiles, dtype=jnp.int32)[None, :]).astype(
        jnp.int32
    )
    earlier = jnp.cumsum(dest_table, axis=0) - dest_table
    rank_within = jnp.sum(earlier * dest_table, axis=1)
    bucket_pos = dest_flat * capacity + rank_within
    entry_values = (remap_weight[:, :, None] * grad_flux.T[:, None, :]).reshape(entries, species)
    send_values = (
        jnp.zeros((tiles * capacity, species), jnp.float32)
        .at[bucket_pos]
        .set(entry_values)
        .reshape(tiles, capacity, species)
    )
    send_slots = (
        jnp.full((tiles * capacity, 1), col_max, jnp.int32)
        .at[bucket_pos]
        .set(slot_flat[:, None])
        .reshape(tiles, capacity, 1)
    )
    recv_values, recv_slots = (
        lax.all_to_all(send_values, "tile", split_axis=0, concat_axis=0, tiled=True),
        lax.all_to_all(send_slots, "tile", split_axis=0, concat_axis=0, tiled=True),
    )
    slot_index = recv_slots.reshape(-1)
    injected = (
        jnp.zeros((col_max + 1, species), jnp.float32)
        .at[slot_index]
        .add(recv_values.reshape(-1, species))[:col_max]
    )
    live_mask = (jnp.arange(col_max) < col_count[0]).astype(jnp.float32)[:, None]
    adjoint = live_mask * (
        grad_columns.astype(jnp.float32)
        + (injected[:, :, None] * thickness[None, :, :]).reshape(col_max, width)
    )
    rate_row = jnp.repeat(kappa, layers)[None, :]
    eye_block = jnp.eye(species, dtype=jnp.bfloat16)
    block_operator = jnp.einsum("slm,st->sltm", vertical, eye_block).reshape(width, width)
    target_rows = jnp.arange(col_max + 2 * rim_width, dtype=jnp.int32)[:, None]
    count_matrix = jnp.zeros((col_max + 2 * rim_width, col_max), jnp.float32)
    for column in range(nbr_count):
        count_matrix = count_matrix + (neighbors[:, column][None, :] == target_rows).astype(
            jnp.float32
        )
    zero_rest = jnp.zeros((col_max - 2 * rim_width, width), jnp.float32)
    for substep in range(SUB):
        spread = rate_row * adjoint
        extended = jnp.dot(
            count_matrix,
            spread,
            precision=lax.Precision.HIGHEST,
            preferred_element_type=jnp.float32,
        )
        to_previous = extended[col_max : col_max + rim_width]
        to_following = extended[col_max + rim_width :]
        from_following = shifted(to_previous.astype(jnp.bfloat16), "tile", -1).astype(
            to_previous.dtype
        )
        from_previous = shifted(to_following.astype(jnp.bfloat16), "tile", 1).astype(
            to_following.dtype
        )
        rim_terms = jnp.concatenate([from_previous, from_following, zero_rest], axis=0)
        bedload = adjoint - nbr_count * rate_row * adjoint + extended[:col_max] + rim_terms
        adjoint = jnp.dot(
            bedload.astype(jnp.bfloat16), block_operator, preferred_element_type=jnp.float32
        )
    rounded = adjoint.astype(jnp.bfloat16)
    piece = lax.all_gather(rounded, "spec", axis=1, tiled=True)
    piece_species = piece.shape[1] // layers
    mixed = jnp.einsum(
        "jsl,st->jtl",
        piece.reshape(col_max, piece_species, layers),
        reaction,
        preferred_element_type=jnp.float32,
    )
    grad_state = mixed.reshape(col_max, width).astype(jnp.bfloat16)
    top_layer = mixed[:, :, 0]
    everything = lax.all_gather(top_layer, "tile", axis=0, tiled=True)
    picked = everything[dest_flat * col_max + slot_flat]
    grad_bottom = jnp.sum(
        picked.reshape(cells, per_cell, species) * remap_weight[:, :, None], axis=1
    ).T
    return (grad_state, grad_bottom)


def column_body(
    grad_columns,
    grad_flux,
    remap_part,
    remap_slot,
    remap_weight,
    col_count,
    neighbors,
    kappa,
    thickness,
    vertical,
    reaction,
):
    tiles = lax.axis_size("tile")
    parts = lax.axis_size("spec")
    col_max, width = grad_columns.shape
    layers = thickness.shape[1]
    shape = jax.ShapeDtypeStruct
    moved = [grad_columns, vertical, thickness, grad_flux]
    moved += [remap_part.T, remap_slot.T, remap_weight.T, neighbors.T, reaction.T]
    payload, misc, remap = call(
        prepare,
        [
            shape((tiles, 2 * (OWN + tiles + 4), col_max // 2), BF16),
            shape((16, width), F32),
            shape((16, col_max), F32),
        ],
        [SMEM] + [HBM] * 10,
        scratch=[pltpu.SMEM(kappa.shape, kappa.dtype)]
        + [pltpu.VMEM(a.shape, a.dtype) for a in moved]
        + [pltpu.SemaphoreType.DMA((10,))],
        flops=4 * 10**7,
        moved=10**6,
        limit=MOST,
    )(col_count, kappa, *moved)
    data = lax.all_to_all(payload, "tile", split_axis=0, concat_axis=0, tiled=True)
    back = call(
        functools.partial(chain, tiles, layers),
        [shape((tiles * parts, OWN + tiles, WIDE), BF16)],
        [VMEM] * 2,
        scratch=[
            pltpu.VMEM((2, tiles, OWN, col_max), F32),
            pltpu.VMEM((tiles * 4, LANES, col_max), BF16),
            pltpu.VMEM((tiles, 4, col_max), F32),
        ],
        flops=10**10,
        moved=10**6,
    )(misc, data)[0]
    home = lax.all_to_all(back, ("tile", "spec"), split_axis=0, concat_axis=0, tiled=True)
    packed = call(
        functools.partial(middle, tiles, parts, layers),
        [shape((parts, width + OWN, WIDE), BF16)],
        [VMEM] * 2,
        flops=10**9,
        moved=10**6,
    )(home, remap)[0]
    every = lax.all_to_all(packed, "spec", split_axis=0, concat_axis=0, tiled=True)
    outs = [shape((col_max, width), BF16), shape((4, col_max), F32)]
    return tuple(call(settle, outs, [VMEM], flops=10**8, moved=10**6)(every))


def body(*args):
    tiles, parts = lax.axis_size("tile"), lax.axis_size("spec")
    layers = args[8].shape[1]
    fits = tiles == 8 and layers == 2 * OWN and args[0].shape == (parts * WIDE, tiles * OWN)
    return (column_body if fits else halo_body)(*args)


def solution(mesh):
    placed = (
        P("tile", "spec"),
        P("spec", "tile"),
        P("tile", None),
        P("tile", None),
        P("tile", None),
        P("tile"),
        P("tile", None),
        P("spec"),
        P("spec", None),
        P("spec", None, None),
        P(None, "spec"),
    )
    return jax.shard_map(
        body,
        mesh=mesh,
        in_specs=placed,
        out_specs=(P("tile", "spec"), P("spec", "tile")),
        check_vma=False,
    )
```

```python
import functools

import jax
import jax.numpy as jnp
from jax import lax
from jax.experimental import pallas as pl
from jax.experimental.pallas import tpu as pltpu
from jax.sharding import PartitionSpec as P

SUB = 4
LANES = 128
WIDE = 256
OWN = 16
DEAD = 15
F32 = jnp.float32
BF16 = jnp.bfloat16
VMEM = pl.BlockSpec(memory_space=pltpu.VMEM)
HBM = pl.BlockSpec(memory_space=pltpu.HBM)
SMEM = pl.BlockSpec(memory_space=pltpu.SMEM)
LIMIT = 40 * 1024 * 1024
MOST = 60 * 1024 * 1024


def call(kernel, outs, specs, scratch=(), flops=0, moved=0, limit=LIMIT):
    return pl.pallas_call(
        kernel,
        out_shape=outs,
        in_specs=specs,
        out_specs=[VMEM] * len(outs),
        scratch_shapes=scratch,
        compiler_params=pltpu.CompilerParams(vmem_limit_bytes=limit),
        cost_estimate=pl.CostEstimate(flops=flops, bytes_accessed=moved, transcendentals=0),
    )


def nt(a, b, precision=None):
    return lax.dot_general(
        a, b, (((1,), (1,)), ((), ())), precision=precision, preferred_element_type=F32
    )


def nn(a, b, precision=None):
    return lax.dot_general(
        a, b, (((1,), (0,)), ((), ())), precision=precision, preferred_element_type=F32
    )


def row_ids(rows, cols):
    return lax.broadcasted_iota(jnp.int32, (rows, cols), 0)


def started(pairs, sems):
    copies = [pltpu.make_async_copy(a, b, sems.at[i]) for i, (a, b) in enumerate(pairs)]
    for copy in copies:
        copy.start()
    return copies


def coded(ints):
    value = (128 + (ints & 127)).astype(F32)
    for bit in range(4):
        value = value * jnp.where((ints >> (7 + bit)) & 1 == 1, float(2 ** (2**bit)), 1.0)
    return value


def decoded(value):
    high = jnp.zeros(value.shape, jnp.int32)
    for bit in (8, 4, 2, 1):
        large = value >= 128.0 * 2.0**bit
        value = jnp.where(large, value * 2.0**-bit, value)
        high = high + jnp.where(large, bit, 0)
    return value - 128.0, high


def hot(key, ids):
    return jnp.where(ids == key, jnp.ones((), BF16), jnp.zeros((), BF16))


def picked(keys, value, target):
    return jnp.where(keys == jnp.asarray(target, BF16), value, jnp.zeros((), BF16))


def narrow(ints):
    return ints.astype(F32).astype(BF16)


def folded(rows):
    middle = rows.shape[1] // 2
    return [rows[:, :middle], rows[:, middle:]]


def prepare(
    count_ref, kappa_any, gc_any, vert_any, thick_any, flux_any, part_any, slot_any, weight_any,
    nbr_any, reaction_any, payload_ref, misc_ref, remap_ref,
    kappa_ref, gc_ref, vert_ref, thick_ref, flux_ref, part_ref, slot_ref, weight_ref,
    nbr_ref, reaction_ref, sems,
):
    copies = started(
        [
            (gc_any, gc_ref),
            (kappa_any, kappa_ref),
            (vert_any, vert_ref),
            (thick_any, thick_ref),
            (reaction_any, reaction_ref),
            (slot_any, slot_ref),
            (part_any, part_ref),
            (weight_any, weight_ref),
            (flux_any, flux_ref),
            (nbr_any, nbr_ref),
        ],
        sems,
    )
    for copy in copies:
        copy.wait()
    tiles = payload_ref.shape[0]
    col_max = gc_ref.shape[0]
    species, layers, _ = vert_ref.shape
    width = species * layers
    subs = col_max // WIDE

    v = vert_ref[...].astype(F32).reshape(width, layers)
    v = jnp.concatenate([v] * species, axis=1)
    rows = row_ids(width, width) // layers
    cols = lax.broadcasted_iota(jnp.int32, (width, width), 1) // layers
    vt = jnp.where(rows == cols, v, 0.0).T.astype(BF16)
    hi = lax.Precision.HIGHEST
    v2 = nn(vt, vt)
    v4 = nn(v2, v2, hi)
    th = jnp.concatenate([thick_ref[s : s + 1, :] for s in range(species)], axis=1)
    misc_ref[0:8] = nt(jnp.broadcast_to(th, (8, width)), v4, hi)
    rates = [jnp.full((1, width), kappa_ref[s], F32) for s in range(species)]
    mix = reaction_ref[...].astype(F32)
    mix = jnp.concatenate([mix, jnp.zeros((4, width - mix.shape[1]), F32)], axis=1)
    misc_ref[8:16] = jnp.concatenate(rates + [mix], axis=0)
    flux, weight = flux_ref[...], weight_ref[...]
    slot = slot_ref[...]
    part, sub, low = part_ref[...], slot // WIDE, slot % WIDE
    remap_ref[...] = jnp.concatenate(
        [low.astype(F32), part.astype(F32), sub.astype(F32), weight], axis=0
    )
    low = narrow(low)
    ids = narrow(row_ids(WIDE, 1))
    place = row_ids(16, 1)
    sums = jnp.zeros((species * subs * tiles, WIDE), F32)
    for r in range(4):
        value = flux * weight[r : r + 1]
        value = [jnp.broadcast_to(value[s : s + 1], (16, col_max)).astype(BF16) for s in range(4)]
        spot = sub[r : r + 1] * tiles + part[r : r + 1]
        keys = [narrow(spot - place - 16 * k) for k in range(subs * tiles // 16)]
        blocks = [picked(key, value[s], 0) for s in range(species) for key in keys]
        sums = sums + nt(jnp.concatenate(blocks, axis=0), hot(low[r : r + 1], ids))

    live = lax.broadcasted_iota(jnp.int32, (1, col_max), 1) < count_ref[0]
    tail = folded(coded(jnp.where(live, nbr_ref[...], DEAD * LANES)))
    w = jnp.where(live, nt(v4.astype(BF16), gc_ref[...]), 0.0)
    for q in range(tiles):
        s = q * OWN // layers
        mine = sums[s * subs * tiles : (s + 1) * subs * tiles]
        mine = jnp.concatenate([mine[h * tiles : (h + 1) * tiles] for h in range(subs)], axis=1)
        pieces = folded(w[q * OWN : (q + 1) * OWN]) + folded(mine) + tail
        payload_ref[q] = jnp.concatenate(pieces, axis=0).astype(BF16)


def unfolded(block, first, rows):
    return jnp.concatenate([block[first : first + rows], block[first + rows : first + 2 * rows]], axis=1)


def chain(tiles, layers, misc_ref, data_ref, back_ref, x_ref, hot_ref, high_ref):
    col_max = x_ref.shape[3]
    blocks = col_max // LANES
    me = lax.axis_index("tile")
    ids = narrow(row_ids(LANES, 1))

    lane = lax.broadcasted_iota(jnp.int32, (OWN, misc_ref.shape[1]), 1)
    row = row_ids(OWN, 1)
    tv_own = jnp.where(lane == me * OWN + row, misc_ref[0:1], 0.0)
    tv_own = jnp.sum(tv_own, axis=1, keepdims=True)
    mine = me * OWN // layers
    rate = jnp.zeros((1, 1), F32)
    for s in range(4):
        rate = jnp.where(mine == s, misc_ref[8 + s : 9 + s, 0:1], rate)

    inj = jnp.zeros((tiles, col_max), F32)
    for q in range(tiles):
        block = data_ref[q].astype(F32)
        inj = inj + unfolded(block, 2 * OWN, tiles)
    for q in range(tiles):
        block = data_ref[q].astype(F32)
        low, high = decoded(unfolded(block, 2 * OWN + 2 * tiles, 4))
        live = high[0:1] != DEAD
        x_ref[0, q] = unfolded(block, 0, OWN) + tv_own * jnp.where(live, inj[q : q + 1], 0.0)
        high_ref[q] = high.astype(F32)
        for n in range(4):
            hot_ref[q * 4 + n] = hot(low[n : n + 1].astype(BF16), ids)

    def product(here, q):
        high = high_ref[q]
        value = (rate * x_ref[here, q]).astype(BF16)
        hits = list(range(blocks)) + [blocks] * (q > 0) + [blocks + 1] * (q < tiles - 1)
        total = jnp.zeros((len(hits) * OWN, LANES), F32)
        for n in range(4):
            key = jnp.broadcast_to(high[n : n + 1], (OWN, col_max)).astype(BF16)
            rows = [picked(key, value, h) for h in hits]
            total = total + nt(jnp.concatenate(rows, axis=0), hot_ref[q * 4 + n])
        pieces = [total[i * OWN : (i + 1) * OWN] for i in range(len(hits))]
        own = pieces[:blocks]
        to_prev = pieces[blocks] if q > 0 else None
        to_next = pieces[-1] if q < tiles - 1 else None
        return own, to_prev, to_next

    for step in range(SUB):
        here, there = step % 2, (step + 1) % 2
        from_prev = None
        current = product(here, 0)
        for q in range(tiles):
            following = product(here, q + 1) if q < tiles - 1 else None
            own, _, to_next = current
            if from_prev is not None:
                own[0] = own[0] + from_prev
            if following is not None:
                own[1] = own[1] + following[1]
            x_ref[there, q] = (1.0 - 4.0 * rate) * x_ref[here, q] + jnp.concatenate(own, axis=1)
            from_prev, current = to_next, following
    last = SUB % 2
    quarters = col_max // WIDE
    mix = jnp.concatenate([misc_ref[8:16], misc_ref[8:16]], axis=1)[4:8]
    mix = jnp.concatenate([mix, mix], axis=0)
    for g in range(quarters):
        top = [
            x_ref[last, tiles // quarters * g + h, 0:1, k * WIDE : (k + 1) * WIDE]
            for h in range(tiles // quarters)
            for k in range(quarters)
        ]
        top = jnp.where((me * OWN) % layers == 0, jnp.concatenate(top, axis=0), mix)
        for q in range(tiles):
            piece = x_ref[last, q, :, g * WIDE : (g + 1) * WIDE]
            back_ref[g * tiles + q] = jnp.concatenate([piece, top], axis=0).astype(BF16)


def middle(tiles, parts, layers, data_ref, remap_ref, out_ref):
    col_max = remap_ref.shape[1]
    quarters = col_max // WIDE
    halves = layers // OWN
    species = 4 * parts
    me = lax.axis_index("spec")

    def source(s, half):
        return s // 4 * tiles + (s % 4) * halves + half

    mix = [data_ref[source(4 * k, 1)].astype(F32)[OWN : OWN + 4, 0:species] for k in range(parts)]
    mix = jnp.concatenate(mix, axis=0)
    size = species * OWN
    left = row_ids(size, species) // OWN == lax.broadcasted_iota(jnp.int32, (size, species), 1)
    right = row_ids(species, size) == lax.broadcasted_iota(jnp.int32, (species, size), 1) // OWN
    left, right = (jnp.where(hit, 1.0, 0.0).astype(BF16) for hit in (left, right))
    full = nn(nn(left, mix.astype(BF16)).astype(BF16), right)
    same = row_ids(size, size) % OWN == lax.broadcasted_iota(jnp.int32, (size, size), 1) % OWN
    full = jnp.where(same, full, 0.0).astype(BF16)
    mixed = []
    for half in range(halves):
        x = [data_ref[source(s, half), 0:OWN] for s in range(species)]
        mixed.append(nn(full, jnp.concatenate(x, axis=0)))

    table = [data_ref[source(s, 0)].astype(F32)[OWN:] for s in range(species)]
    table = jnp.concatenate(table, axis=0).astype(BF16)
    low = remap_ref[0:4].astype(BF16)
    place = remap_ref[4:8].astype(jnp.int32) * quarters + remap_ref[8:12].astype(jnp.int32)
    place = place - me * tiles
    ids = narrow(row_ids(WIDE, 1))
    totals = [jnp.zeros((tiles, col_max), F32) for s in range(species)]
    for r in range(4):
        found = nn(table, hot(low[r : r + 1], ids))
        weight = jnp.where(
            place[r : r + 1] == row_ids(tiles, 1), remap_ref[12 + r : 13 + r], 0.0
        )
        for s in range(species):
            totals[s] = totals[s] + found[s * tiles : (s + 1) * tiles] * weight
    bottom = [jnp.sum(total, axis=0, keepdims=True) for total in totals]
    bottom = nn(mix, jnp.concatenate(bottom, axis=0), lax.Precision.HIGHEST)
    for k in range(parts):
        rows = []
        for t in range(4 * k, 4 * k + 4):
            rows += [mixed[half][t * OWN : (t + 1) * OWN] for half in range(halves)]
        mine = bottom[4 * k : 4 * k + 4]
        rows += [mine[:, h * WIDE : (h + 1) * WIDE] for h in range(quarters)]
        out_ref[k] = jnp.concatenate(rows, axis=0).astype(BF16)


def settle(all_ref, state_ref, bottom_ref):
    parts, rows, wide = all_ref.shape
    width = state_ref.shape[1]
    total = jnp.zeros((rows - width, wide), F32)
    for k in range(parts):
        state = all_ref[k, 0:width].astype(F32)
        state_ref[k * wide : (k + 1) * wide, :] = state.T.astype(BF16)
        total = total + all_ref[k, width:].astype(F32)
    pieces = [total[h * 4 : h * 4 + 4] for h in range(parts)]
    bottom_ref[...] = jnp.concatenate(pieces, axis=1)


def shifted(block, axis, distance):
    devices = range(lax.axis_size(axis))
    route = [(i - distance, i) for i in devices if i - distance in devices]
    return lax.ppermute(block, axis, route)


def halo_body(
    grad_columns,
    grad_flux,
    remap_part,
    remap_slot,
    remap_weight,
    col_count,
    neighbors,
    kappa,
    thickness,
    vertical,
    reaction,
):
    tiles = lax.axis_size("tile")
    col_max = grad_columns.shape[0]
    rim_width = col_max // 8
    species = kappa.shape[0]
    layers = thickness.shape[1]
    width = species * layers
    cells, per_cell = remap_part.shape
    entries = cells * per_cell
    capacity = 2 * entries // tiles
    nbr_count = neighbors.shape[1]
    dest_flat = remap_part.reshape(-1)
    slot_flat = remap_slot.reshape(-1)
    dest_table = (dest_flat[:, None] == jnp.arange(tiles, dtype=jnp.int32)[None, :]).astype(
        jnp.int32
    )
    earlier = jnp.cumsum(dest_table, axis=0) - dest_table
    rank_within = jnp.sum(earlier * dest_table, axis=1)
    bucket_pos = dest_flat * capacity + rank_within
    entry_values = (remap_weight[:, :, None] * grad_flux.T[:, None, :]).reshape(entries, species)
    send_values = (
        jnp.zeros((tiles * capacity, species), jnp.float32)
        .at[bucket_pos]
        .set(entry_values)
        .reshape(tiles, capacity, species)
    )
    send_slots = (
        jnp.full((tiles * capacity, 1), col_max, jnp.int32)
        .at[bucket_pos]
        .set(slot_flat[:, None])
        .reshape(tiles, capacity, 1)
    )
    recv_values, recv_slots = (
        lax.all_to_all(send_values, "tile", split_axis=0, concat_axis=0, tiled=True),
        lax.all_to_all(send_slots, "tile", split_axis=0, concat_axis=0, tiled=True),
    )
    slot_index = recv_slots.reshape(-1)
    injected = (
        jnp.zeros((col_max + 1, species), jnp.float32)
        .at[slot_index]
        .add(recv_values.reshape(-1, species))[:col_max]
    )
    live_mask = (jnp.arange(col_max) < col_count[0]).astype(jnp.float32)[:, None]
    adjoint = live_mask * (
        grad_columns.astype(jnp.float32)
        + (injected[:, :, None] * thickness[None, :, :]).reshape(col_max, width)
    )
    rate_row = jnp.repeat(kappa, layers)[None, :]
    eye_block = jnp.eye(species, dtype=jnp.bfloat16)
    block_operator = jnp.einsum("slm,st->sltm", vertical, eye_block).reshape(width, width)
    target_rows = jnp.arange(col_max + 2 * rim_width, dtype=jnp.int32)[:, None]
    count_matrix = jnp.zeros((col_max + 2 * rim_width, col_max), jnp.float32)
    for column in range(nbr_count):
        count_matrix = count_matrix + (neighbors[:, column][None, :] == target_rows).astype(
            jnp.float32
        )
    zero_rest = jnp.zeros((col_max - 2 * rim_width, width), jnp.float32)
    for substep in range(SUB):
        spread = rate_row * adjoint
        extended = jnp.dot(
            count_matrix,
            spread,
            precision=lax.Precision.HIGHEST,
            preferred_element_type=jnp.float32,
        )
        to_previous = extended[col_max : col_max + rim_width]
        to_following = extended[col_max + rim_width :]
        from_following = shifted(to_previous.astype(jnp.bfloat16), "tile", -1).astype(
            to_previous.dtype
        )
        from_previous = shifted(to_following.astype(jnp.bfloat16), "tile", 1).astype(
            to_following.dtype
        )
        rim_terms = jnp.concatenate([from_previous, from_following, zero_rest], axis=0)
        bedload = adjoint - nbr_count * rate_row * adjoint + extended[:col_max] + rim_terms
        adjoint = jnp.dot(
            bedload.astype(jnp.bfloat16), block_operator, preferred_element_type=jnp.float32
        )
    rounded = adjoint.astype(jnp.bfloat16)
    piece = lax.all_gather(rounded, "spec", axis=1, tiled=True)
    piece_species = piece.shape[1] // layers
    mixed = jnp.einsum(
        "jsl,st->jtl",
        piece.reshape(col_max, piece_species, layers),
        reaction,
        preferred_element_type=jnp.float32,
    )
    grad_state = mixed.reshape(col_max, width).astype(jnp.bfloat16)
    top_layer = mixed[:, :, 0]
    everything = lax.all_gather(top_layer, "tile", axis=0, tiled=True)
    picked = everything[dest_flat * col_max + slot_flat]
    grad_bottom = jnp.sum(
        picked.reshape(cells, per_cell, species) * remap_weight[:, :, None], axis=1
    ).T
    return (grad_state, grad_bottom)


def column_body(
    grad_columns,
    grad_flux,
    remap_part,
    remap_slot,
    remap_weight,
    col_count,
    neighbors,
    kappa,
    thickness,
    vertical,
    reaction,
):
    tiles = lax.axis_size("tile")
    parts = lax.axis_size("spec")
    col_max, width = grad_columns.shape
    layers = thickness.shape[1]
    shape = jax.ShapeDtypeStruct
    moved = [grad_columns, vertical, thickness, grad_flux]
    moved += [remap_part.T, remap_slot.T, remap_weight.T, neighbors.T, reaction.T]
    payload, misc, remap = call(
        prepare,
        [
            shape((tiles, 2 * (OWN + tiles + 4), col_max // 2), BF16),
            shape((16, width), F32),
            shape((16, col_max), F32),
        ],
        [SMEM] + [HBM] * 10,
        scratch=[pltpu.SMEM(kappa.shape, kappa.dtype)]
        + [pltpu.VMEM(a.shape, a.dtype) for a in moved]
        + [pltpu.SemaphoreType.DMA((10,))],
        flops=4 * 10**7,
        moved=10**6,
        limit=MOST,
    )(col_count, kappa, *moved)
    data = lax.all_to_all(payload, "tile", split_axis=0, concat_axis=0, tiled=True)
    back = call(
        functools.partial(chain, tiles, layers),
        [shape((tiles * parts, OWN + tiles, WIDE), BF16)],
        [VMEM] * 2,
        scratch=[
            pltpu.VMEM((2, tiles, OWN, col_max), F32),
            pltpu.VMEM((tiles * 4, LANES, col_max), BF16),
            pltpu.VMEM((tiles, 4, col_max), F32),
        ],
        flops=10**10,
        moved=10**6,
    )(misc, data)[0]
    home = lax.all_to_all(back, ("spec", "tile"), split_axis=0, concat_axis=0, tiled=True)
    packed = call(
        functools.partial(middle, tiles, parts, layers),
        [shape((parts, width + OWN, WIDE), BF16)],
        [VMEM] * 2,
        flops=10**9,
        moved=10**6,
    )(home, remap)[0]
    every = lax.all_to_all(packed, "spec", split_axis=0, concat_axis=0, tiled=True)
    outs = [shape((col_max, width), BF16), shape((4, col_max), F32)]
    return tuple(call(settle, outs, [VMEM], flops=10**8, moved=10**6)(every))


def body(*args):
    tiles, parts = lax.axis_size("tile"), lax.axis_size("spec")
    layers = args[8].shape[1]
    fits = tiles == 8 and layers == 2 * OWN and args[0].shape == (parts * WIDE, tiles * OWN)
    return (column_body if fits else halo_body)(*args)


def solution(mesh):
    placed = (
        P("tile", "spec"),
        P("spec", "tile"),
        P("tile", None),
        P("tile", None),
        P("tile", None),
        P("tile"),
        P("tile", None),
        P("spec"),
        P("spec", None),
        P("spec", None, None),
        P(None, "spec"),
    )
    return jax.shard_map(
        body,
        mesh=mesh,
        in_specs=placed,
        out_specs=(P("tile", "spec"), P("spec", "tile")),
        check_vma=False,
    )
```

```python
import functools

import jax
import jax.numpy as jnp
from jax import lax
from jax.experimental import pallas as pl
from jax.experimental.pallas import tpu as pltpu
from jax.sharding import PartitionSpec as P

SUB = 4
LANES = 128
WIDE = 256
OWN = 16
DEAD = 15
F32 = jnp.float32
BF16 = jnp.bfloat16
VMEM = pl.BlockSpec(memory_space=pltpu.VMEM)
HBM = pl.BlockSpec(memory_space=pltpu.HBM)
SMEM = pl.BlockSpec(memory_space=pltpu.SMEM)
LIMIT = 40 * 1024 * 1024
MOST = 60 * 1024 * 1024


def call(kernel, outs, specs, scratch=(), flops=0, moved=0, limit=LIMIT, first=VMEM):
    return pl.pallas_call(
        kernel,
        out_shape=outs,
        in_specs=specs,
        out_specs=[first] + [VMEM] * (len(outs) - 1),
        scratch_shapes=scratch,
        compiler_params=pltpu.CompilerParams(vmem_limit_bytes=limit),
        cost_estimate=pl.CostEstimate(flops=flops, bytes_accessed=moved, transcendentals=0),
    )


def nt(a, b, precision=None):
    return lax.dot_general(
        a, b, (((1,), (1,)), ((), ())), precision=precision, preferred_element_type=F32
    )


def nn(a, b, precision=None):
    return lax.dot_general(
        a, b, (((1,), (0,)), ((), ())), precision=precision, preferred_element_type=F32
    )


def row_ids(rows, cols):
    return lax.broadcasted_iota(jnp.int32, (rows, cols), 0)


def started(pairs, sems):
    copies = [pltpu.make_async_copy(a, b, sems.at[i]) for i, (a, b) in enumerate(pairs)]
    for copy in copies:
        copy.start()
    return copies


def coded(ints):
    value = (128 + (ints & 127)).astype(F32)
    for bit in range(4):
        value = value * jnp.where((ints >> (7 + bit)) & 1 == 1, float(2 ** (2**bit)), 1.0)
    return value


def decoded(value):
    high = jnp.zeros(value.shape, jnp.int32)
    for bit in (8, 4, 2, 1):
        large = value >= 128.0 * 2.0**bit
        value = jnp.where(large, value * 2.0**-bit, value)
        high = high + jnp.where(large, bit, 0)
    return value - 128.0, high


def hot(key, ids):
    return jnp.where(ids == key, jnp.ones((), BF16), jnp.zeros((), BF16))


def picked(keys, value, target):
    return jnp.where(keys == jnp.asarray(target, BF16), value, jnp.zeros((), BF16))


def narrow(ints):
    return ints.astype(F32).astype(BF16)


def folded(rows):
    middle = rows.shape[1] // 2
    return [rows[:, :middle], rows[:, middle:]]


def prepare(
    count_ref, kappa_any, gc_any, vert_any, thick_any, flux_any, part_any, slot_any, weight_any,
    nbr_any, reaction_any, payload_ref, misc_ref, remap_ref,
    kappa_ref, gc_ref, vert_ref, thick_ref, flux_ref, part_ref, slot_ref, weight_ref,
    nbr_ref, reaction_ref, sems,
):
    copies = started(
        [
            (gc_any, gc_ref),
            (kappa_any, kappa_ref),
            (vert_any, vert_ref),
            (thick_any, thick_ref),
            (reaction_any, reaction_ref),
            (slot_any, slot_ref),
            (part_any, part_ref),
            (weight_any, weight_ref),
            (flux_any, flux_ref),
            (nbr_any, nbr_ref),
        ],
        sems,
    )
    for copy in copies:
        copy.wait()
    tiles = payload_ref.shape[0]
    col_max = gc_ref.shape[0]
    species, layers, _ = vert_ref.shape
    width = species * layers
    subs = col_max // WIDE

    v = vert_ref[...].astype(F32).reshape(width, layers)
    v = jnp.concatenate([v] * species, axis=1)
    rows = row_ids(width, width) // layers
    cols = lax.broadcasted_iota(jnp.int32, (width, width), 1) // layers
    vt = jnp.where(rows == cols, v, 0.0).T.astype(BF16)
    hi = lax.Precision.HIGHEST
    v2 = nn(vt, vt)
    large = v2.astype(BF16)
    small = (v2 - large.astype(F32)).astype(BF16)
    v4 = nn(large, large) + (nn(large, small) + nn(small, large))
    th = jnp.concatenate([thick_ref[s : s + 1, :] for s in range(species)], axis=1)
    misc_ref[0:8] = nt(jnp.broadcast_to(th, (8, width)), v4, hi)
    rates = [jnp.full((1, width), kappa_ref[s], F32) for s in range(species)]
    mix = reaction_ref[...].astype(F32)
    mix = jnp.concatenate([mix, jnp.zeros((4, width - mix.shape[1]), F32)], axis=1)
    misc_ref[8:16] = jnp.concatenate(rates + [mix], axis=0)
    flux, weight = flux_ref[...], weight_ref[...]
    slot = slot_ref[...]
    part, sub, low = part_ref[...], slot // WIDE, slot % WIDE
    remap_ref[...] = jnp.concatenate(
        [low.astype(F32), part.astype(F32), sub.astype(F32), weight], axis=0
    )
    low = narrow(low)
    ids = narrow(row_ids(WIDE, 1))
    place = row_ids(16, 1)
    sums = jnp.zeros((species * subs * tiles, WIDE), F32)
    for r in range(4):
        value = flux * weight[r : r + 1]
        value = [jnp.broadcast_to(value[s : s + 1], (16, col_max)).astype(BF16) for s in range(4)]
        spot = sub[r : r + 1] * tiles + part[r : r + 1]
        keys = [narrow(spot - place - 16 * k) for k in range(subs * tiles // 16)]
        blocks = [picked(key, value[s], 0) for s in range(species) for key in keys]
        sums = sums + nt(jnp.concatenate(blocks, axis=0), hot(low[r : r + 1], ids))

    live = lax.broadcasted_iota(jnp.int32, (1, col_max), 1) < count_ref[0]
    tail = folded(coded(jnp.where(live, nbr_ref[...], DEAD * LANES)))
    w = jnp.where(live, nt(v4.astype(BF16), gc_ref[...]), 0.0)
    for q in range(tiles):
        s = q * OWN // layers
        mine = sums[s * subs * tiles : (s + 1) * subs * tiles]
        mine = jnp.concatenate([mine[h * tiles : (h + 1) * tiles] for h in range(subs)], axis=1)
        pieces = folded(w[q * OWN : (q + 1) * OWN]) + folded(mine) + tail
        payload_ref[q] = jnp.concatenate(pieces, axis=0).astype(BF16)


def unfolded(block, first, rows):
    return jnp.concatenate([block[first : first + rows], block[first + rows : first + 2 * rows]], axis=1)


def chain(tiles, layers, misc_ref, data_ref, back_ref, x_ref, hot_ref, high_ref):
    col_max = x_ref.shape[3]
    blocks = col_max // LANES
    me = lax.axis_index("tile")
    ids = narrow(row_ids(LANES, 1))

    lane = lax.broadcasted_iota(jnp.int32, (OWN, misc_ref.shape[1]), 1)
    row = row_ids(OWN, 1)
    tv_own = jnp.where(lane == me * OWN + row, misc_ref[0:1], 0.0)
    tv_own = jnp.sum(tv_own, axis=1, keepdims=True)
    mine = me * OWN // layers
    rate = jnp.zeros((1, 1), F32)
    for s in range(4):
        rate = jnp.where(mine == s, misc_ref[8 + s : 9 + s, 0:1], rate)

    inj = jnp.zeros((tiles, col_max), F32)
    for q in range(tiles):
        block = data_ref[q].astype(F32)
        inj = inj + unfolded(block, 2 * OWN, tiles)
    for q in range(tiles):
        block = data_ref[q].astype(F32)
        low, high = decoded(unfolded(block, 2 * OWN + 2 * tiles, 4))
        live = high[0:1] != DEAD
        x_ref[0, q] = unfolded(block, 0, OWN) + tv_own * jnp.where(live, inj[q : q + 1], 0.0)
        high_ref[q] = high.astype(F32)
        for n in range(4):
            hot_ref[q * 4 + n] = hot(low[n : n + 1].astype(BF16), ids)

    def product(here, q):
        high = high_ref[q]
        value = (rate * x_ref[here, q]).astype(BF16)
        hits = list(range(blocks)) + [blocks] * (q > 0) + [blocks + 1] * (q < tiles - 1)
        total = jnp.zeros((len(hits) * OWN, LANES), F32)
        for n in range(4):
            key = jnp.broadcast_to(high[n : n + 1], (OWN, col_max)).astype(BF16)
            rows = [picked(key, value, h) for h in hits]
            total = total + nt(jnp.concatenate(rows, axis=0), hot_ref[q * 4 + n])
        pieces = [total[i * OWN : (i + 1) * OWN] for i in range(len(hits))]
        own = pieces[:blocks]
        to_prev = pieces[blocks] if q > 0 else None
        to_next = pieces[-1] if q < tiles - 1 else None
        return own, to_prev, to_next

    for step in range(SUB):
        here, there = step % 2, (step + 1) % 2
        from_prev = None
        current = product(here, 0)
        for q in range(tiles):
            following = product(here, q + 1) if q < tiles - 1 else None
            own, _, to_next = current
            if from_prev is not None:
                own[0] = own[0] + from_prev
            if following is not None:
                own[1] = own[1] + following[1]
            x_ref[there, q] = (1.0 - 4.0 * rate) * x_ref[here, q] + jnp.concatenate(own, axis=1)
            from_prev, current = to_next, following
    last = SUB % 2
    quarters = col_max // WIDE
    mix = jnp.concatenate([misc_ref[8:16], misc_ref[8:16]], axis=1)[4:8]
    mix = jnp.concatenate([mix, mix], axis=0)
    for g in range(quarters):
        top = [
            x_ref[last, tiles // quarters * g + h, 0:1, k * WIDE : (k + 1) * WIDE]
            for h in range(tiles // quarters)
            for k in range(quarters)
        ]
        top = jnp.where((me * OWN) % layers == 0, jnp.concatenate(top, axis=0), mix)
        for q in range(tiles):
            piece = x_ref[last, q, :, g * WIDE : (g + 1) * WIDE]
            back_ref[q * quarters + g] = jnp.concatenate([piece, top], axis=0).astype(BF16)


def middle(tiles, parts, layers, data_ref, remap_ref, out_ref):
    col_max = remap_ref.shape[1]
    quarters = col_max // WIDE
    halves = layers // OWN
    species = 4 * parts
    me = lax.axis_index("spec")

    def source(s, half):
        return ((s % 4) * halves + half) * parts + s // 4

    mix = [data_ref[source(4 * k, 1)].astype(F32)[OWN : OWN + 4, 0:species] for k in range(parts)]
    mix = jnp.concatenate(mix, axis=0)
    size = species * OWN
    left = row_ids(size, species) // OWN == lax.broadcasted_iota(jnp.int32, (size, species), 1)
    right = row_ids(species, size) == lax.broadcasted_iota(jnp.int32, (species, size), 1) // OWN
    left, right = (jnp.where(hit, 1.0, 0.0).astype(BF16) for hit in (left, right))
    full = nn(nn(left, mix.astype(BF16)).astype(BF16), right)
    same = row_ids(size, size) % OWN == lax.broadcasted_iota(jnp.int32, (size, size), 1) % OWN
    full = jnp.where(same, full, 0.0).astype(BF16)
    mixed = []
    for half in range(halves):
        x = [data_ref[source(s, half), 0:OWN] for s in range(species)]
        mixed.append(nn(full, jnp.concatenate(x, axis=0)))

    table = [data_ref[source(s, 0)].astype(F32)[OWN:] for s in range(species)]
    table = jnp.concatenate(table, axis=0).astype(BF16)
    low = remap_ref[0:4].astype(BF16)
    place = remap_ref[4:8].astype(jnp.int32) * quarters + remap_ref[8:12].astype(jnp.int32)
    place = place - me * tiles
    ids = narrow(row_ids(WIDE, 1))
    totals = [jnp.zeros((tiles, col_max), F32) for s in range(species)]
    for r in range(4):
        found = nn(table, hot(low[r : r + 1], ids))
        weight = jnp.where(
            place[r : r + 1] == row_ids(tiles, 1), remap_ref[12 + r : 13 + r], 0.0
        )
        for s in range(species):
            totals[s] = totals[s] + found[s * tiles : (s + 1) * tiles] * weight
    bottom = [jnp.sum(total, axis=0, keepdims=True) for total in totals]
    bottom = nn(mix, jnp.concatenate(bottom, axis=0), lax.Precision.HIGHEST)
    for k in range(parts):
        rows = []
        for t in range(4 * k, 4 * k + 4):
            rows += [mixed[half][t * OWN : (t + 1) * OWN] for half in range(halves)]
        mine = bottom[4 * k : 4 * k + 4]
        rows += [mine[:, h * WIDE : (h + 1) * WIDE] for h in range(quarters)]
        out_ref[k] = jnp.concatenate(rows, axis=0).astype(BF16)


def settle(all_ref, state_any, bottom_ref, state_ref, sems):
    parts, rows, wide = all_ref.shape
    width = state_ref.shape[1]
    total = jnp.zeros((rows - width, wide), F32)
    copies = []
    for k in range(parts):
        here = pl.ds(k * wide, wide)
        state_ref[here, :] = all_ref[k, 0:width].astype(F32).T.astype(BF16)
        copies.append(pltpu.make_async_copy(state_ref.at[here], state_any.at[here], sems.at[k]))
        copies[-1].start()
        total = total + all_ref[k, width:].astype(F32)
    pieces = [total[h * 4 : h * 4 + 4] for h in range(parts)]
    bottom_ref[...] = jnp.concatenate(pieces, axis=1)
    for copy in copies:
        copy.wait()


def shifted(block, axis, distance):
    devices = range(lax.axis_size(axis))
    route = [(i - distance, i) for i in devices if i - distance in devices]
    return lax.ppermute(block, axis, route)


def halo_body(
    grad_columns,
    grad_flux,
    remap_part,
    remap_slot,
    remap_weight,
    col_count,
    neighbors,
    kappa,
    thickness,
    vertical,
    reaction,
):
    tiles = lax.axis_size("tile")
    col_max = grad_columns.shape[0]
    rim_width = col_max // 8
    species = kappa.shape[0]
    layers = thickness.shape[1]
    width = species * layers
    cells, per_cell = remap_part.shape
    entries = cells * per_cell
    capacity = 2 * entries // tiles
    nbr_count = neighbors.shape[1]
    dest_flat = remap_part.reshape(-1)
    slot_flat = remap_slot.reshape(-1)
    dest_table = (dest_flat[:, None] == jnp.arange(tiles, dtype=jnp.int32)[None, :]).astype(
        jnp.int32
    )
    earlier = jnp.cumsum(dest_table, axis=0) - dest_table
    rank_within = jnp.sum(earlier * dest_table, axis=1)
    bucket_pos = dest_flat * capacity + rank_within
    entry_values = (remap_weight[:, :, None] * grad_flux.T[:, None, :]).reshape(entries, species)
    send_values = (
        jnp.zeros((tiles * capacity, species), jnp.float32)
        .at[bucket_pos]
        .set(entry_values)
        .reshape(tiles, capacity, species)
    )
    send_slots = (
        jnp.full((tiles * capacity, 1), col_max, jnp.int32)
        .at[bucket_pos]
        .set(slot_flat[:, None])
        .reshape(tiles, capacity, 1)
    )
    recv_values, recv_slots = (
        lax.all_to_all(send_values, "tile", split_axis=0, concat_axis=0, tiled=True),
        lax.all_to_all(send_slots, "tile", split_axis=0, concat_axis=0, tiled=True),
    )
    slot_index = recv_slots.reshape(-1)
    injected = (
        jnp.zeros((col_max + 1, species), jnp.float32)
        .at[slot_index]
        .add(recv_values.reshape(-1, species))[:col_max]
    )
    live_mask = (jnp.arange(col_max) < col_count[0]).astype(jnp.float32)[:, None]
    adjoint = live_mask * (
        grad_columns.astype(jnp.float32)
        + (injected[:, :, None] * thickness[None, :, :]).reshape(col_max, width)
    )
    rate_row = jnp.repeat(kappa, layers)[None, :]
    eye_block = jnp.eye(species, dtype=jnp.bfloat16)
    block_operator = jnp.einsum("slm,st->sltm", vertical, eye_block).reshape(width, width)
    target_rows = jnp.arange(col_max + 2 * rim_width, dtype=jnp.int32)[:, None]
    count_matrix = jnp.zeros((col_max + 2 * rim_width, col_max), jnp.float32)
    for column in range(nbr_count):
        count_matrix = count_matrix + (neighbors[:, column][None, :] == target_rows).astype(
            jnp.float32
        )
    zero_rest = jnp.zeros((col_max - 2 * rim_width, width), jnp.float32)
    for substep in range(SUB):
        spread = rate_row * adjoint
        extended = jnp.dot(
            count_matrix,
            spread,
            precision=lax.Precision.HIGHEST,
            preferred_element_type=jnp.float32,
        )
        to_previous = extended[col_max : col_max + rim_width]
        to_following = extended[col_max + rim_width :]
        from_following = shifted(to_previous.astype(jnp.bfloat16), "tile", -1).astype(
            to_previous.dtype
        )
        from_previous = shifted(to_following.astype(jnp.bfloat16), "tile", 1).astype(
            to_following.dtype
        )
        rim_terms = jnp.concatenate([from_previous, from_following, zero_rest], axis=0)
        bedload = adjoint - nbr_count * rate_row * adjoint + extended[:col_max] + rim_terms
        adjoint = jnp.dot(
            bedload.astype(jnp.bfloat16), block_operator, preferred_element_type=jnp.float32
        )
    rounded = adjoint.astype(jnp.bfloat16)
    piece = lax.all_gather(rounded, "spec", axis=1, tiled=True)
    piece_species = piece.shape[1] // layers
    mixed = jnp.einsum(
        "jsl,st->jtl",
        piece.reshape(col_max, piece_species, layers),
        reaction,
        preferred_element_type=jnp.float32,
    )
    grad_state = mixed.reshape(col_max, width).astype(jnp.bfloat16)
    top_layer = mixed[:, :, 0]
    everything = lax.all_gather(top_layer, "tile", axis=0, tiled=True)
    picked = everything[dest_flat * col_max + slot_flat]
    grad_bottom = jnp.sum(
        picked.reshape(cells, per_cell, species) * remap_weight[:, :, None], axis=1
    ).T
    return (grad_state, grad_bottom)


def column_body(
    grad_columns,
    grad_flux,
    remap_part,
    remap_slot,
    remap_weight,
    col_count,
    neighbors,
    kappa,
    thickness,
    vertical,
    reaction,
):
    tiles = lax.axis_size("tile")
    parts = lax.axis_size("spec")
    col_max, width = grad_columns.shape
    layers = thickness.shape[1]
    shape = jax.ShapeDtypeStruct
    moved = [grad_columns, vertical, thickness, grad_flux]
    moved += [remap_part.T, remap_slot.T, remap_weight.T, neighbors.T, reaction.T]
    payload, misc, remap = call(
        prepare,
        [
            shape((tiles, 2 * (OWN + tiles + 4), col_max // 2), BF16),
            shape((16, width), F32),
            shape((16, col_max), F32),
        ],
        [SMEM] + [HBM] * 10,
        scratch=[pltpu.SMEM(kappa.shape, kappa.dtype)]
        + [pltpu.VMEM(a.shape, a.dtype) for a in moved]
        + [pltpu.SemaphoreType.DMA((10,))],
        flops=4 * 10**7,
        moved=10**6,
        limit=MOST,
    )(col_count, kappa, *moved)
    data = lax.all_to_all(payload, "tile", split_axis=0, concat_axis=0, tiled=True)
    back = call(
        functools.partial(chain, tiles, layers),
        [shape((tiles * parts, OWN + tiles, WIDE), BF16)],
        [VMEM] * 2,
        scratch=[
            pltpu.VMEM((2, tiles, OWN, col_max), F32),
            pltpu.VMEM((tiles * 4, LANES, col_max), BF16),
            pltpu.VMEM((tiles, 4, col_max), F32),
        ],
        flops=10**10,
        moved=10**6,
    )(misc, data)[0]
    home = lax.all_to_all(back, ("tile", "spec"), split_axis=0, concat_axis=0, tiled=True)
    packed = call(
        functools.partial(middle, tiles, parts, layers),
        [shape((parts, width + OWN, WIDE), BF16)],
        [VMEM] * 2,
        flops=10**9,
        moved=10**6,
    )(home, remap)[0]
    every = lax.all_to_all(packed, "spec", split_axis=0, concat_axis=0, tiled=True)
    outs = [shape((col_max, width), BF16), shape((4, col_max), F32)]
    scratch = [pltpu.VMEM((col_max, width), BF16), pltpu.SemaphoreType.DMA((parts,))]
    return tuple(call(settle, outs, [VMEM], scratch, 10**8, 10**6, first=HBM)(every))


def body(*args):
    tiles, parts = lax.axis_size("tile"), lax.axis_size("spec")
    layers = args[8].shape[1]
    fits = tiles == 8 and layers == 2 * OWN and args[0].shape == (parts * WIDE, tiles * OWN)
    return (column_body if fits else halo_body)(*args)


def solution(mesh):
    placed = (
        P("tile", "spec"),
        P("spec", "tile"),
        P("tile", None),
        P("tile", None),
        P("tile", None),
        P("tile"),
        P("tile", None),
        P("spec"),
        P("spec", None),
        P("spec", None, None),
        P(None, "spec"),
    )
    return jax.shard_map(
        body,
        mesh=mesh,
        in_specs=placed,
        out_specs=(P("tile", "spec"), P("spec", "tile")),
        check_vma=False,
    )
```

```python
import functools

import jax
import jax.numpy as jnp
from jax import lax
from jax.experimental import pallas as pl
from jax.experimental.pallas import tpu as pltpu
from jax.sharding import PartitionSpec as P

SUB = 4
LANES = 128
WIDE = 256
OWN = 16
DEAD = 15
F32 = jnp.float32
BF16 = jnp.bfloat16
VMEM = pl.BlockSpec(memory_space=pltpu.VMEM)
HBM = pl.BlockSpec(memory_space=pltpu.HBM)
SMEM = pl.BlockSpec(memory_space=pltpu.SMEM)
LIMIT = 40 * 1024 * 1024
MOST = 60 * 1024 * 1024


def call(kernel, outs, specs, scratch=(), flops=0, moved=0, limit=LIMIT):
    return pl.pallas_call(
        kernel,
        out_shape=outs,
        in_specs=specs,
        out_specs=[VMEM] * len(outs),
        scratch_shapes=scratch,
        compiler_params=pltpu.CompilerParams(vmem_limit_bytes=limit),
        cost_estimate=pl.CostEstimate(flops=flops, bytes_accessed=moved, transcendentals=0),
    )


def nt(a, b, precision=None):
    return lax.dot_general(
        a, b, (((1,), (1,)), ((), ())), precision=precision, preferred_element_type=F32
    )


def nn(a, b, precision=None):
    return lax.dot_general(
        a, b, (((1,), (0,)), ((), ())), precision=precision, preferred_element_type=F32
    )


def row_ids(rows, cols):
    return lax.broadcasted_iota(jnp.int32, (rows, cols), 0)


def started(pairs, sems):
    copies = [pltpu.make_async_copy(a, b, sems.at[i]) for i, (a, b) in enumerate(pairs)]
    for copy in copies:
        copy.start()
    return copies


def coded(ints):
    value = (128 + (ints & 127)).astype(F32)
    for bit in range(4):
        value = value * jnp.where((ints >> (7 + bit)) & 1 == 1, float(2 ** (2**bit)), 1.0)
    return value


def decoded(value):
    high = jnp.zeros(value.shape, jnp.int32)
    for bit in (8, 4, 2, 1):
        large = value >= 128.0 * 2.0**bit
        value = jnp.where(large, value * 2.0**-bit, value)
        high = high + jnp.where(large, bit, 0)
    return value - 128.0, high


def hot(key, ids):
    return jnp.where(ids == key, jnp.ones((), BF16), jnp.zeros((), BF16))


def picked(keys, value, target):
    return jnp.where(keys == jnp.asarray(target, BF16), value, jnp.zeros((), BF16))


def narrow(ints):
    return ints.astype(F32).astype(BF16)


def folded(rows):
    middle = rows.shape[1] // 2
    return [rows[:, :middle], rows[:, middle:]]


def prepare(
    count_ref, kappa_any, gc_any, vert_any, thick_any, flux_any, part_any, slot_any, weight_any,
    nbr_any, reaction_any, payload_ref, misc_ref, remap_ref,
    kappa_ref, gc_ref, vert_ref, thick_ref, flux_ref, part_ref, slot_ref, weight_ref,
    nbr_ref, reaction_ref, sems,
):
    copies = started(
        [
            (gc_any, gc_ref),
            (kappa_any, kappa_ref),
            (vert_any, vert_ref),
            (thick_any, thick_ref),
            (reaction_any, reaction_ref),
            (slot_any, slot_ref),
            (part_any, part_ref),
            (weight_any, weight_ref),
            (flux_any, flux_ref),
            (nbr_any, nbr_ref),
        ],
        sems,
    )
    for copy in copies:
        copy.wait()
    tiles = payload_ref.shape[0]
    col_max = gc_ref.shape[0]
    species, layers, _ = vert_ref.shape
    width = species * layers
    subs = col_max // WIDE

    v = vert_ref[...].astype(F32).reshape(width, layers)
    v = jnp.concatenate([v] * species, axis=1)
    rows = row_ids(width, width) // layers
    cols = lax.broadcasted_iota(jnp.int32, (width, width), 1) // layers
    vt = jnp.where(rows == cols, v, 0.0).T.astype(BF16)
    hi = lax.Precision.HIGHEST
    v2 = nn(vt, vt)
    v4 = nn(v2, v2, hi)
    th = jnp.concatenate([thick_ref[s : s + 1, :] for s in range(species)], axis=1)
    misc_ref[0:8] = nt(jnp.broadcast_to(th, (8, width)), v4, hi)
    rates = [jnp.full((1, width), kappa_ref[s], F32) for s in range(species)]
    mix = reaction_ref[...].astype(F32)
    mix = jnp.concatenate([mix, jnp.zeros((4, width - mix.shape[1]), F32)], axis=1)
    misc_ref[8:16] = jnp.concatenate(rates + [mix], axis=0)
    flux, weight = flux_ref[...], weight_ref[...]
    slot = slot_ref[...]
    part, sub, low = part_ref[...], slot // WIDE, slot % WIDE
    remap_ref[...] = jnp.concatenate(
        [low.astype(F32), part.astype(F32), sub.astype(F32), weight], axis=0
    )
    low = narrow(low)
    ids = narrow(row_ids(WIDE, 1))
    place = row_ids(16, 1)
    sums = jnp.zeros((species * subs * tiles, WIDE), F32)
    for r in range(4):
        value = flux * weight[r : r + 1]
        value = [jnp.broadcast_to(value[s : s + 1], (16, col_max)).astype(BF16) for s in range(4)]
        spot = sub[r : r + 1] * tiles + part[r : r + 1]
        keys = [narrow(spot - place - 16 * k) for k in range(subs * tiles // 16)]
        blocks = [picked(key, value[s], 0) for s in range(species) for key in keys]
        sums = sums + nt(jnp.concatenate(blocks, axis=0), hot(low[r : r + 1], ids))

    live = lax.broadcasted_iota(jnp.int32, (1, col_max), 1) < count_ref[0]
    tail = folded(coded(jnp.where(live, nbr_ref[...], DEAD * LANES)))
    w = jnp.where(live, nt(v4.astype(BF16), gc_ref[...]), 0.0)
    for q in range(tiles):
        s = q * OWN // layers
        mine = sums[s * subs * tiles : (s + 1) * subs * tiles]
        mine = jnp.concatenate([mine[h * tiles : (h + 1) * tiles] for h in range(subs)], axis=1)
        pieces = folded(w[q * OWN : (q + 1) * OWN]) + folded(mine) + tail
        payload_ref[q] = jnp.concatenate(pieces, axis=0).astype(BF16)


def unfolded(block, first, rows):
    return jnp.concatenate([block[first : first + rows], block[first + rows : first + 2 * rows]], axis=1)


def chain(tiles, layers, misc_ref, data_ref, back_ref, x_ref, hot_ref, high_ref):
    col_max = x_ref.shape[3]
    blocks = col_max // LANES
    me = lax.axis_index("tile")
    ids = narrow(row_ids(LANES, 1))

    lane = lax.broadcasted_iota(jnp.int32, (OWN, misc_ref.shape[1]), 1)
    row = row_ids(OWN, 1)
    tv_own = jnp.where(lane == me * OWN + row, misc_ref[0:1], 0.0)
    tv_own = jnp.sum(tv_own, axis=1, keepdims=True)
    mine = me * OWN // layers
    rate = jnp.zeros((1, 1), F32)
    for s in range(4):
        rate = jnp.where(mine == s, misc_ref[8 + s : 9 + s, 0:1], rate)

    inj = jnp.zeros((tiles, col_max), F32)
    for q in range(tiles):
        block = data_ref[q].astype(F32)
        inj = inj + unfolded(block, 2 * OWN, tiles)
    for q in range(tiles):
        block = data_ref[q].astype(F32)
        low, high = decoded(unfolded(block, 2 * OWN + 2 * tiles, 4))
        live = high[0:1] != DEAD
        x_ref[0, q] = unfolded(block, 0, OWN) + tv_own * jnp.where(live, inj[q : q + 1], 0.0)
        high_ref[q] = high.astype(F32)
        for n in range(4):
            hot_ref[q * 4 + n] = hot(low[n : n + 1].astype(BF16), ids)

    def product(here, q):
        high = high_ref[q]
        value = (rate * x_ref[here, q]).astype(BF16)
        hits = list(range(blocks)) + [blocks] * (q > 0) + [blocks + 1] * (q < tiles - 1)
        total = jnp.zeros((len(hits) * OWN, LANES), F32)
        for n in range(4):
            key = jnp.broadcast_to(high[n : n + 1], (OWN, col_max)).astype(BF16)
            rows = [picked(key, value, h) for h in hits]
            total = total + nt(jnp.concatenate(rows, axis=0), hot_ref[q * 4 + n])
        pieces = [total[i * OWN : (i + 1) * OWN] for i in range(len(hits))]
        own = pieces[:blocks]
        to_prev = pieces[blocks] if q > 0 else None
        to_next = pieces[-1] if q < tiles - 1 else None
        return own, to_prev, to_next

    for step in range(SUB):
        here, there = step % 2, (step + 1) % 2
        from_prev = None
        current = product(here, 0)
        for q in range(tiles):
            following = product(here, q + 1) if q < tiles - 1 else None
            own, _, to_next = current
            if from_prev is not None:
                own[0] = own[0] + from_prev
            if following is not None:
                own[1] = own[1] + following[1]
            x_ref[there, q] = (1.0 - 4.0 * rate) * x_ref[here, q] + jnp.concatenate(own, axis=1)
            from_prev, current = to_next, following
    last = SUB % 2
    quarters = col_max // WIDE
    mix = jnp.concatenate([misc_ref[8:16], misc_ref[8:16]], axis=1)[4:8]
    mix = jnp.concatenate([mix, mix], axis=0)
    for g in range(quarters):
        top = [
            x_ref[last, tiles // quarters * g + h, 0:1, k * WIDE : (k + 1) * WIDE]
            for h in range(tiles // quarters)
            for k in range(quarters)
        ]
        top = jnp.where((me * OWN) % layers == 0, jnp.concatenate(top, axis=0), mix)
        for q in range(tiles):
            piece = x_ref[last, q, :, g * WIDE : (g + 1) * WIDE]
            back_ref[q * quarters + g] = jnp.concatenate([piece, top], axis=0).astype(BF16)


def middle(tiles, parts, layers, data_ref, remap_ref, out_ref):
    col_max = remap_ref.shape[1]
    quarters = col_max // WIDE
    halves = layers // OWN
    species = 4 * parts
    me = lax.axis_index("spec")

    def source(s, half):
        return ((s % 4) * halves + half) * parts + s // 4

    mix = [data_ref[source(4 * k, 1)].astype(F32)[OWN : OWN + 4, 0:species] for k in range(parts)]
    mix = jnp.concatenate(mix, axis=0)
    size = species * OWN
    left = row_ids(size, species) // OWN == lax.broadcasted_iota(jnp.int32, (size, species), 1)
    right = row_ids(species, size) == lax.broadcasted_iota(jnp.int32, (species, size), 1) // OWN
    left, right = (jnp.where(hit, 1.0, 0.0).astype(BF16) for hit in (left, right))
    full = nn(nn(left, mix.astype(BF16)).astype(BF16), right)
    same = row_ids(size, size) % OWN == lax.broadcasted_iota(jnp.int32, (size, size), 1) % OWN
    full = jnp.where(same, full, 0.0).astype(BF16)
    mixed = []
    for half in range(halves):
        x = [data_ref[source(s, half), 0:OWN] for s in range(species)]
        mixed.append(nn(full, jnp.concatenate(x, axis=0)))

    table = [data_ref[source(s, 0)].astype(F32)[OWN:] for s in range(species)]
    table = jnp.concatenate(table, axis=0).astype(BF16)
    low = remap_ref[0:4].astype(BF16)
    place = remap_ref[4:8].astype(jnp.int32) * quarters + remap_ref[8:12].astype(jnp.int32)
    place = place - me * tiles
    ids = narrow(row_ids(WIDE, 1))
    totals = [jnp.zeros((tiles, col_max), F32) for s in range(species)]
    for r in range(4):
        found = nn(table, hot(low[r : r + 1], ids))
        weight = jnp.where(
            place[r : r + 1] == row_ids(tiles, 1), remap_ref[12 + r : 13 + r], 0.0
        )
        for s in range(species):
            totals[s] = totals[s] + found[s * tiles : (s + 1) * tiles] * weight
    bottom = [jnp.sum(total, axis=0, keepdims=True) for total in totals]
    bottom = nn(mix, jnp.concatenate(bottom, axis=0), lax.Precision.HIGHEST)
    for k in range(parts):
        rows = []
        for t in range(4 * k, 4 * k + 4):
            rows += [mixed[half][t * OWN : (t + 1) * OWN] for half in range(halves)]
        mine = bottom[4 * k : 4 * k + 4]
        rows += [mine[:, h * WIDE : (h + 1) * WIDE] for h in range(quarters)]
        out_ref[k] = jnp.concatenate(rows, axis=0).astype(BF16)


def settle(all_ref, state_ref, bottom_ref):
    parts, rows, wide = all_ref.shape
    width = state_ref.shape[1]
    total = jnp.zeros((rows - width, wide), F32)
    for k in range(parts):
        state_ref[k * wide : (k + 1) * wide, :] = all_ref[k, 0:width].T
        total = total + all_ref[k, width:].astype(F32)
    pieces = [total[h * 4 : h * 4 + 4] for h in range(parts)]
    bottom_ref[...] = jnp.concatenate(pieces, axis=1)


def shifted(block, axis, distance):
    devices = range(lax.axis_size(axis))
    route = [(i - distance, i) for i in devices if i - distance in devices]
    return lax.ppermute(block, axis, route)


def halo_body(
    grad_columns,
    grad_flux,
    remap_part,
    remap_slot,
    remap_weight,
    col_count,
    neighbors,
    kappa,
    thickness,
    vertical,
    reaction,
):
    tiles = lax.axis_size("tile")
    col_max = grad_columns.shape[0]
    rim_width = col_max // 8
    species = kappa.shape[0]
    layers = thickness.shape[1]
    width = species * layers
    cells, per_cell = remap_part.shape
    entries = cells * per_cell
    capacity = 2 * entries // tiles
    nbr_count = neighbors.shape[1]
    dest_flat = remap_part.reshape(-1)
    slot_flat = remap_slot.reshape(-1)
    dest_table = (dest_flat[:, None] == jnp.arange(tiles, dtype=jnp.int32)[None, :]).astype(
        jnp.int32
    )
    earlier = jnp.cumsum(dest_table, axis=0) - dest_table
    rank_within = jnp.sum(earlier * dest_table, axis=1)
    bucket_pos = dest_flat * capacity + rank_within
    entry_values = (remap_weight[:, :, None] * grad_flux.T[:, None, :]).reshape(entries, species)
    send_values = (
        jnp.zeros((tiles * capacity, species), jnp.float32)
        .at[bucket_pos]
        .set(entry_values)
        .reshape(tiles, capacity, species)
    )
    send_slots = (
        jnp.full((tiles * capacity, 1), col_max, jnp.int32)
        .at[bucket_pos]
        .set(slot_flat[:, None])
        .reshape(tiles, capacity, 1)
    )
    recv_values, recv_slots = (
        lax.all_to_all(send_values, "tile", split_axis=0, concat_axis=0, tiled=True),
        lax.all_to_all(send_slots, "tile", split_axis=0, concat_axis=0, tiled=True),
    )
    slot_index = recv_slots.reshape(-1)
    injected = (
        jnp.zeros((col_max + 1, species), jnp.float32)
        .at[slot_index]
        .add(recv_values.reshape(-1, species))[:col_max]
    )
    live_mask = (jnp.arange(col_max) < col_count[0]).astype(jnp.float32)[:, None]
    adjoint = live_mask * (
        grad_columns.astype(jnp.float32)
        + (injected[:, :, None] * thickness[None, :, :]).reshape(col_max, width)
    )
    rate_row = jnp.repeat(kappa, layers)[None, :]
    eye_block = jnp.eye(species, dtype=jnp.bfloat16)
    block_operator = jnp.einsum("slm,st->sltm", vertical, eye_block).reshape(width, width)
    target_rows = jnp.arange(col_max + 2 * rim_width, dtype=jnp.int32)[:, None]
    count_matrix = jnp.zeros((col_max + 2 * rim_width, col_max), jnp.float32)
    for column in range(nbr_count):
        count_matrix = count_matrix + (neighbors[:, column][None, :] == target_rows).astype(
            jnp.float32
        )
    zero_rest = jnp.zeros((col_max - 2 * rim_width, width), jnp.float32)
    for substep in range(SUB):
        spread = rate_row * adjoint
        extended = jnp.dot(
            count_matrix,
            spread,
            precision=lax.Precision.HIGHEST,
            preferred_element_type=jnp.float32,
        )
        to_previous = extended[col_max : col_max + rim_width]
        to_following = extended[col_max + rim_width :]
        from_following = shifted(to_previous.astype(jnp.bfloat16), "tile", -1).astype(
            to_previous.dtype
        )
        from_previous = shifted(to_following.astype(jnp.bfloat16), "tile", 1).astype(
            to_following.dtype
        )
        rim_terms = jnp.concatenate([from_previous, from_following, zero_rest], axis=0)
        bedload = adjoint - nbr_count * rate_row * adjoint + extended[:col_max] + rim_terms
        adjoint = jnp.dot(
            bedload.astype(jnp.bfloat16), block_operator, preferred_element_type=jnp.float32
        )
    rounded = adjoint.astype(jnp.bfloat16)
    piece = lax.all_gather(rounded, "spec", axis=1, tiled=True)
    piece_species = piece.shape[1] // layers
    mixed = jnp.einsum(
        "jsl,st->jtl",
        piece.reshape(col_max, piece_species, layers),
        reaction,
        preferred_element_type=jnp.float32,
    )
    grad_state = mixed.reshape(col_max, width).astype(jnp.bfloat16)
    top_layer = mixed[:, :, 0]
    everything = lax.all_gather(top_layer, "tile", axis=0, tiled=True)
    picked = everything[dest_flat * col_max + slot_flat]
    grad_bottom = jnp.sum(
        picked.reshape(cells, per_cell, species) * remap_weight[:, :, None], axis=1
    ).T
    return (grad_state, grad_bottom)


def column_body(
    grad_columns,
    grad_flux,
    remap_part,
    remap_slot,
    remap_weight,
    col_count,
    neighbors,
    kappa,
    thickness,
    vertical,
    reaction,
):
    tiles = lax.axis_size("tile")
    parts = lax.axis_size("spec")
    col_max, width = grad_columns.shape
    layers = thickness.shape[1]
    shape = jax.ShapeDtypeStruct
    moved = [grad_columns, vertical, thickness, grad_flux]
    moved += [remap_part.T, remap_slot.T, remap_weight.T, neighbors.T, reaction.T]
    payload, misc, remap = call(
        prepare,
        [
            shape((tiles, 2 * (OWN + tiles + 4), col_max // 2), BF16),
            shape((16, width), F32),
            shape((16, col_max), F32),
        ],
        [SMEM] + [HBM] * 10,
        scratch=[pltpu.SMEM(kappa.shape, kappa.dtype)]
        + [pltpu.VMEM(a.shape, a.dtype) for a in moved]
        + [pltpu.SemaphoreType.DMA((10,))],
        flops=4 * 10**7,
        moved=10**6,
        limit=MOST,
    )(col_count, kappa, *moved)
    data = lax.all_to_all(payload, "tile", split_axis=0, concat_axis=0, tiled=True)
    back = call(
        functools.partial(chain, tiles, layers),
        [shape((tiles * parts, OWN + tiles, WIDE), BF16)],
        [VMEM] * 2,
        scratch=[
            pltpu.VMEM((2, tiles, OWN, col_max), F32),
            pltpu.VMEM((tiles * 4, LANES, col_max), BF16),
            pltpu.VMEM((tiles, 4, col_max), F32),
        ],
        flops=10**10,
        moved=10**6,
    )(misc, data)[0]
    home = lax.all_to_all(back, ("tile", "spec"), split_axis=0, concat_axis=0, tiled=True)
    packed = call(
        functools.partial(middle, tiles, parts, layers),
        [shape((parts, width + OWN, WIDE), BF16)],
        [VMEM] * 2,
        flops=10**9,
        moved=10**6,
    )(home, remap)[0]
    every = lax.all_to_all(packed, "spec", split_axis=0, concat_axis=0, tiled=True)
    outs = [shape((col_max, width), BF16), shape((4, col_max), F32)]
    return tuple(call(settle, outs, [VMEM], flops=10**8, moved=10**6)(every))


def body(*args):
    tiles, parts = lax.axis_size("tile"), lax.axis_size("spec")
    layers = args[8].shape[1]
    fits = tiles == 8 and layers == 2 * OWN and args[0].shape == (parts * WIDE, tiles * OWN)
    return (column_body if fits else halo_body)(*args)


def solution(mesh):
    placed = (
        P("tile", "spec"),
        P("spec", "tile"),
        P("tile", None),
        P("tile", None),
        P("tile", None),
        P("tile"),
        P("tile", None),
        P("spec"),
        P("spec", None),
        P("spec", None, None),
        P(None, "spec"),
    )
    return jax.shard_map(
        body,
        mesh=mesh,
        in_specs=placed,
        out_specs=(P("tile", "spec"), P("spec", "tile")),
        check_vma=False,
    )
```
